32 devices in a mesh: section: 2 (over core), tensor: 4 (over y, x), dp: 4 (over z).
Axes of the slice: x: 2, y: 2, z: 4, core: 2. Of those that a mesh axis runs over, the one named last changes fastest.
Arguments:
- enc_in: bfloat16 [2, 4, 512, 768], P(None, 'dp', 'tensor'), may hold values from -40 to 40
- dec_in: bfloat16 [2, 4, 448, 768], P(None, 'dp', 'tensor'), may hold values from -40 to 40
- lengths: int32 [2, 4], P(None, 'dp'), may hold values from 5 to 448, as said below
- enc_cot: bfloat16 [2, 4, 512, 768], P(None, 'dp', 'tensor'), may hold values from -6 to 6
- dec_cot: bfloat16 [2, 4, 448, 768], P(None, 'dp', 'tensor'), may hold values from -6 to 6
- norm_params: float32 [2, 3, 2, 768], P('section'), may hold values from -1 to 2
- attn_in: bfloat16 [2, 768, 3, 768], P('section', None, None, 'tensor'), may hold values from -0.21875 to 0.21875
- attn_out: bfloat16 [2, 768, 768], P('section', 'tensor'), may hold values from -2.5 to 2.5
- cross_proj: bfloat16 [2, 768, 2, 768], P('section', None, None, 'tensor'), may hold values from -3 to 3
- w_up: bfloat16 [2, 768, 3072], P('section', None, 'tensor'), may hold values from -0.21875 to 0.21875
- b_up: float32 [2, 3072], P('section', 'tensor'), may hold values from -3 to 3
- w_down: bfloat16 [2, 3072, 768], P('section', 'tensor'), may hold values from -0.109375 to 0.109375
- b_down: float32 [2, 768], P('section'), may hold values from -3 to 3
Outputs:
- enc_out: bfloat16 [2, 4, 512, 768], P('section', 'dp', 'tensor')
- dec_out: bfloat16 [2, 4, 448, 768], P('section', 'dp', 'tensor')
- enc_in_grad: float32 [2, 4, 512, 768], P('section', 'dp', 'tensor')
- dec_in_grad: float32 [2, 4, 448, 768], P('section', 'dp', 'tensor')
- norm_params_grad: float32 [2, 3, 2, 768], P('section')
- attn_in_grad: float32 [2, 768, 3, 768], P('section', None, None, 'tensor')
- attn_out_grad: float32 [2, 768, 768], P('section', 'tensor')
- cross_proj_grad: float32 [2, 768, 2, 768], P('section', None, None, 'tensor')
- w_up_grad: float32 [2, 768, 3072], P('section', None, 'tensor')
- b_up_grad: float32 [2, 3072], P('section', 'tensor')
- w_down_grad: float32 [2, 3072, 768], P('section', 'tensor')
- b_down_grad: float32 [2, 768], P('section')
The draws below stay inside these ranges and needn't reach their ends.
Inputs may be any that keep to these rules, and one draw needn't show every extreme that they name: lengths[m, g] is the number of real decoder positions of clip (m, g); in every draw some clip has exactly 448 and another exactly 5.
All inputs are finite; a program needn't handle non-finite values.
Results may differ from the reference program's by a relative error of at most 0.019.
Values may be sent and summed in bfloat16 or wider, within the bound.
No kernel may reach another device: no remote copies, remote signals or barrier semaphores. Data moves between devices by JAX's collectives and lax.ppermute only.
A program may use at most 192 MiB of HBM per device.

```python
import math
import jax
import jax.numpy as jnp
from jax import lax

D = 768
HEADS = 12
HEAD_DIM = 64
FF = 3072
FR = 512
LEN = 448
MICRO = 2
N_DP = 4


def row_scales(key, shape):
    row_key, col_key = jax.random.split(key)
    row_part = jnp.exp(jax.random.uniform(row_key, shape[:-1] + (1,), jnp.float32, math.log(0.5), math.log(5.0)))
    col_part = jnp.exp(jax.random.uniform(col_key, (shape[-1],), jnp.float32, -0.5, 0.5))
    return row_part * col_part


def draw_enc_in(key, part):
    key = jax.random.fold_in(key, 11)
    scale_key, base_key = jax.random.split(key, 2)
    shape = (MICRO, N_DP, FR, D)
    base = jnp.clip(jax.random.normal(base_key, shape, jnp.float32), -4.0, 4.0)
    return (base * row_scales(scale_key, shape)).astype(jnp.bfloat16)


def draw_dec_in(key, part):
    key = jax.random.fold_in(key, 13)
    scale_key, base_key = jax.random.split(key, 2)
    shape = (MICRO, N_DP, LEN, D)
    base = jnp.clip(jax.random.normal(base_key, shape, jnp.float32), -4.0, 4.0)
    return (base * row_scales(scale_key, shape)).astype(jnp.bfloat16)


def draw_lengths(key, part):
    key = jax.random.fold_in(key, 3)
    pick_key, value_key = jax.random.split(key)
    clip_count = MICRO * N_DP
    values = jax.random.randint(value_key, (clip_count,), 5, LEN + 1)
    order = jax.random.permutation(pick_key, clip_count)
    values = values.at[order[0]].set(LEN).at[order[1]].set(5)
    return values.reshape(MICRO, N_DP).astype(jnp.int32)


def draw_norm_params(key, part):
    key = jax.random.fold_in(key, 5)
    gain_key, shift_key = jax.random.split(key)
    gains = jnp.exp(jax.random.uniform(gain_key, (2, 3, D), jnp.float32, math.log(0.5), math.log(2.0)))
    shifts = 0.3 * jnp.clip(jax.random.normal(shift_key, (2, 3, D), jnp.float32), -3.0, 3.0)
    return jnp.stack([gains, shifts], axis=2)


def draw_cross_proj(key, part):
    key = jax.random.fold_in(key, 7)
    base = jnp.clip(jax.random.normal(key, (2, D, 2, D), jnp.float32), -4.0, 4.0) * D ** (-0.5)
    factor = jnp.ones((2, 1, 2, 1), jnp.float32).at[1, 0, 1, 0].set(16.0)
    return jnp.clip(base * factor, -3.0, 3.0).astype(jnp.bfloat16)


def level_of(key, extent, shards, low, top_value):
    level = 1.0
    for axis_at, parts in shards:
        draws = jax.random.uniform(jax.random.fold_in(jax.random.fold_in(key, 6), axis_at), (parts,), jnp.float32, low / len(shards), top_value / len(shards))
        level = level * jnp.repeat(jnp.exp(draws), extent[axis_at] // parts).reshape((-1,) + (1,) * (len(extent) - 1 - axis_at))
    return level


def scatter_about(rng, shape, deviation, limit, cuts=(), kind=jnp.bfloat16):
    values = jax.random.normal(rng, shape, jnp.float32) * deviation
    if len(cuts) > 0:
        values = level_of(rng, shape, cuts, -0.22, 0.18) * values
    return jnp.clip(values, min=-limit, max=limit).astype(kind)


def setup_inputs(seed: int = 0) -> dict:
    arg_keys = jax.random.split(jax.random.key(seed), 14)
    return {
        "enc_in": draw_enc_in(jax.random.fold_in(arg_keys[13], 71), 0),
        "dec_in": draw_dec_in(jax.random.fold_in(arg_keys[13], 71), 0),
        "lengths": draw_lengths(jax.random.fold_in(arg_keys[13], 71), 0),
        "enc_cot": scatter_about(arg_keys[3], (MICRO, N_DP, FR, D), 1.0, 6.0, ((1, 4), (2, 4))),
        "dec_cot": scatter_about(arg_keys[4], (MICRO, N_DP, LEN, D), 1.0, 6.0, ((1, 4), (2, 4))),
        "norm_params": draw_norm_params(jax.random.fold_in(arg_keys[13], 71), 0),
        "attn_in": scatter_about(arg_keys[6], (2, D, 3, D), D ** -0.5, 0.21875, ((0, 2), (3, 4))),
        "attn_out": scatter_about(arg_keys[7], (2, D, D), (max(D // 128, 1)) ** -0.5, 2.5, ((0, 2), (1, 4))),
        "cross_proj": draw_cross_proj(jax.random.fold_in(arg_keys[13], 71), 0),
        "w_up": scatter_about(arg_keys[9], (2, D, FF), D ** -0.5, 0.21875, ((0, 2), (2, 4))),
        "b_up": scatter_about(arg_keys[10], (2, FF), 0.5, 3.0, ((0, 2), (1, 4)), jnp.float32),
        "w_down": scatter_about(arg_keys[11], (2, FF, D), FF ** -0.5, 0.109375, ((0, 2), (1, 4))),
        "b_down": scatter_about(arg_keys[12], (2, D), 0.5, 3.0, ((0, 2),), jnp.float32),
    }


HIGHEST = lax.Precision.HIGHEST

@jax.custom_vjp
def low(v):
    return lax.optimization_barrier(v.astype(jnp.bfloat16)).astype(jnp.float32)

@jax.custom_vjp
def low_back(v):
    return v

def low_keep(v):
    return (low(v), None)

def low_pass(kept, grad):
    return (grad,)

def back_keep(v):
    return (v, None)

def back_low(kept, grad):
    return (low(grad),)
low.defvjp(low_keep, low_pass)
low_back.defvjp(back_keep, back_low)

def norm_rows(values, gain, shift):
    center = values - lax.optimization_barrier(jnp.mean(values, axis=-1, keepdims=True))
    spread = lax.optimization_barrier(jnp.mean(center * center, axis=-1, keepdims=True))
    return center * lax.rsqrt(spread + 1e-05) * gain + shift

def attend(queries, keyset, valueset, allowed):
    scores = low_back(jnp.einsum('qhd,khd->hqk', queries, keyset, precision=HIGHEST) * HEAD_DIM ** (-0.5))
    if allowed is not None:
        scores = jnp.where(allowed[None], scores, -1e+30)
    row_top = lax.optimization_barrier(jnp.max(scores, axis=-1, keepdims=True))
    powers = jnp.exp(scores - row_top)
    weights = low(powers / lax.optimization_barrier(jnp.sum(powers, axis=-1, keepdims=True)))
    return jnp.einsum('hqk,khd->qhd', weights, valueset, precision=HIGHEST)

def self_block(residual, norm_pair, w_in, w_out, allowed):
    row_count = residual.shape[0]
    normed = low(norm_rows(residual, norm_pair[0], norm_pair[1]))
    packed = low(low_back(jnp.einsum('rd,dtc->rtc', normed, w_in, precision=HIGHEST)))
    heads = packed.reshape(row_count, 3, HEADS, HEAD_DIM)
    blended = low(low_back(attend(heads[:, 0], heads[:, 1], heads[:, 2], allowed)))
    return residual + low_back(jnp.dot(blended.reshape(row_count, D), w_out, precision=HIGHEST))

def ffn_block(residual, norm_pair, w_up, b_up, w_down, b_down):
    normed = low(norm_rows(residual, norm_pair[0], norm_pair[1]))
    hidden = low_back(jnp.dot(normed, w_up, precision=HIGHEST) + b_up)
    active = low(jax.nn.gelu(hidden, approximate=False))
    return residual + low_back(jnp.dot(active, w_down, precision=HIGHEST)) + b_down

def clip_forward(params, frames, tokens, length):
    norm_params, attn_in, attn_out, cross_proj, w_up, b_up, w_down, b_down = params
    after_self = self_block(frames, norm_params[0, 0], attn_in[0], attn_out[0], None)
    enc_final = ffn_block(after_self, norm_params[0, 2], w_up[0], b_up[0], w_down[0], b_down[0])
    post = low(norm_rows(enc_final, norm_params[0, 1, 0], norm_params[0, 1, 1]))
    memory = low(low_back(jnp.einsum('rd,dtc->rtc', post, cross_proj[0], precision=HIGHEST)))
    keyset = memory[:, 0].reshape(FR, HEADS, HEAD_DIM)
    valueset = memory[:, 1].reshape(FR, HEADS, HEAD_DIM)
    positions = jnp.arange(LEN, dtype=jnp.int32)
    allowed = (positions[None, :] <= positions[:, None]) & (positions[None, :] < length)
    dec_self = self_block(tokens, norm_params[1, 0], attn_in[1], attn_out[1], allowed)
    normed = low(norm_rows(dec_self, norm_params[1, 1, 0], norm_params[1, 1, 1]))
    queries = low(low_back(jnp.dot(normed, cross_proj[1][:, 0], precision=HIGHEST))).reshape(LEN, HEADS, HEAD_DIM)
    blended = low(low_back(attend(queries, keyset, valueset, None))).reshape(LEN, D)
    after_cross = dec_self + low_back(jnp.dot(blended, cross_proj[1][:, 1].T, precision=HIGHEST))
    dec_final = ffn_block(after_cross, norm_params[1, 2], w_up[1], b_up[1], w_down[1], b_down[1])
    keep_rows = positions < length
    return (enc_final, jnp.where(keep_rows[:, None], dec_final, 0.0))

def reference(enc_in, dec_in, lengths, enc_cot, dec_cot, norm_params, attn_in, attn_out, cross_proj, w_up, b_up, w_down, b_down):
    params = tuple((member.astype(jnp.float32) for member in (norm_params, attn_in, attn_out, cross_proj, w_up, b_up, w_down, b_down)))
    clip_count = MICRO * N_DP

    def clip_step(totals, bundle):
        frames, tokens, length, cot_enc, cot_dec = bundle

        def forward(weight_set, frames_in, tokens_in):
            return clip_forward(weight_set, frames_in, tokens_in, length)
        results, pull_back = jax.vjp(forward, params, frames.astype(jnp.float32), tokens.astype(jnp.float32))
        grad_params, grad_frames, grad_tokens = pull_back((cot_enc.astype(jnp.float32), cot_dec.astype(jnp.float32)))
        totals = jax.tree.map(jnp.add, totals, grad_params)
        return (totals, (results[0].astype(jnp.bfloat16), results[1].astype(jnp.bfloat16), grad_frames, grad_tokens))
    initial = jax.tree.map(jnp.zeros_like, params)
    inputs_all = (enc_in.reshape(clip_count, FR, D), dec_in.reshape(clip_count, LEN, D), lengths.reshape(clip_count).astype(jnp.int32), enc_cot.reshape(clip_count, FR, D), dec_cot.reshape(clip_count, LEN, D))
    totals, (enc_out, dec_out, enc_grad, dec_grad) = lax.scan(clip_step, initial, inputs_all)
    return (enc_out.reshape(MICRO, N_DP, FR, D), dec_out.reshape(MICRO, N_DP, LEN, D), enc_grad.reshape(MICRO, N_DP, FR, D), dec_grad.reshape(MICRO, N_DP, LEN, D), totals[0], totals[1], totals[2], totals[3], totals[4], totals[5], totals[6], totals[7])
```

```python
import jax
import jax.numpy as jnp
from jax import lax
from jax.sharding import PartitionSpec as P

HEAD_DIM = 64
EPSILON = 1e-05
NEG_FILL = -1e30
LOW = jnp.bfloat16
WIDE = jnp.float32


def dot_nn(left, right):
    return jnp.dot(left, right, preferred_element_type=WIDE)


def dot_tn(left, right):
    return lax.dot_general(left, right, (((0,), (0,)), ((), ())), preferred_element_type=WIDE)


def dot_nt(left, right):
    return lax.dot_general(left, right, (((1,), (1,)), ((), ())), preferred_element_type=WIDE)


def peers(step):
    count = lax.axis_size("tensor")
    return [(source, source ^ step) for source in range(count)]


def gather_rows(rows):
    count = lax.axis_size("tensor")
    return jnp.concatenate(
        [rows] + [lax.ppermute(rows, "tensor", peers(step)) for step in range(1, count)], axis=0
    )


def scatter_rows(partial):
    count = lax.axis_size("tensor")
    size = partial.shape[0] // count
    low = partial.astype(LOW)
    total = partial[:size].astype(WIDE)
    for step in range(1, count):
        block = low[step * size : (step + 1) * size]
        total = total + lax.ppermute(block, "tensor", peers(step)).astype(WIDE)
    return total


def norm(values, pair):
    center = values - jnp.mean(values, axis=-1, keepdims=True)
    rate = lax.rsqrt(jnp.mean(center * center, axis=-1, keepdims=True) + EPSILON)
    unit = center * rate
    return (unit * pair[0] + pair[1]).astype(LOW), (unit, rate)


def norm_back(kept, pair, grad):
    unit, rate = kept
    scaled = grad * pair[0]
    along = jnp.mean(scaled * unit, axis=-1, keepdims=True)
    grad_in = rate * (scaled - jnp.mean(scaled, axis=-1, keepdims=True) - unit * along)
    return grad_in, jnp.stack([jnp.sum(grad * unit, axis=0), jnp.sum(grad, axis=0)])


def gelu_both(hidden):
    share = 0.5 * (1.0 + lax.erf(hidden * 0.7071067811865476))
    slope = share + hidden * (0.3989422804014327 * jnp.exp(-0.5 * hidden * hidden))
    return (hidden * share).astype(LOW), slope


def scores_of(queries, keyset, allowed):
    scores = jnp.einsum("qhd,khd->hqk", queries, keyset, preferred_element_type=WIDE)
    scores = scores * HEAD_DIM ** (-0.5)
    return scores if allowed is None else jnp.where(allowed[None], scores, NEG_FILL)


def attend(queries, keyset, valueset, allowed):
    scores = scores_of(queries, keyset, allowed)
    row_top = jnp.max(scores, axis=-1, keepdims=True)
    powers = jnp.exp(scores - row_top)
    row_total = jnp.sum(powers, axis=-1, keepdims=True)
    weights = (powers / row_total).astype(LOW)
    blended = jnp.einsum("hqk,khd->qhd", weights, valueset, preferred_element_type=WIDE)
    return blended.astype(LOW), row_top + jnp.log(row_total)


def attend_back(queries, keyset, valueset, allowed, log_total, grad_blend):
    scores = scores_of(queries, keyset, allowed)
    shares = jnp.exp(scores - log_total)
    weights = shares.astype(LOW)
    grad_value = jnp.einsum("hqk,qhd->khd", weights, grad_blend, preferred_element_type=WIDE)
    grad_weights = jnp.einsum("qhd,khd->hqk", grad_blend, valueset, preferred_element_type=WIDE)
    grad_scores = shares * (grad_weights - jnp.sum(grad_weights * shares, axis=-1, keepdims=True))
    grad_low = grad_scores.astype(LOW)
    scaling = HEAD_DIM ** (-0.5)
    grad_query = jnp.einsum("hqk,khd->qhd", grad_low, keyset, preferred_element_type=WIDE) * scaling
    grad_key = jnp.einsum("hqk,qhd->khd", grad_low, queries, preferred_element_type=WIDE) * scaling
    return grad_query, grad_key, grad_value


def heads_of(flat):
    return flat.reshape(flat.shape[0], -1, HEAD_DIM)


def self_forward(rows, pair, w_in, w_out, allowed):
    normed, kept = norm(rows, pair)
    gathered = gather_rows(normed)
    packed = dot_nn(gathered, w_in).astype(LOW)
    packed = packed.reshape(packed.shape[0], 3, -1, HEAD_DIM)
    blended, log_total = attend(packed[:, 0], packed[:, 1], packed[:, 2], allowed)
    flat = blended.reshape(blended.shape[0], -1)
    after = rows + scatter_rows(dot_nn(flat, w_out))
    return after, (kept, gathered, packed, log_total, flat)


def self_backward(pair, w_in, w_out, allowed, state, grad_rows):
    kept, gathered, packed, log_total, flat = state
    grad_full = gather_rows(grad_rows.astype(LOW))
    grad_w_out = dot_tn(flat, grad_full)
    grad_flat = dot_nt(grad_full, w_out).astype(LOW)
    parts = attend_back(
        packed[:, 0], packed[:, 1], packed[:, 2], allowed, log_total, heads_of(grad_flat)
    )
    grad_packed = jnp.stack(parts, axis=1).reshape(flat.shape[0], -1).astype(LOW)
    grad_normed = scatter_rows(dot_nt(grad_packed, w_in))
    grad_w_in = dot_tn(gathered, grad_packed)
    grad_in, grad_pair = norm_back(kept, pair, grad_normed)
    return grad_rows + grad_in, grad_pair, grad_w_in, grad_w_out


def swapped(value):
    return lax.ppermute(value, "section", [(0, 1), (1, 0)])


def body(
    enc_in, dec_in, lengths, enc_cot, dec_cot, norm_params, attn_in, attn_out, cross_proj, w_up, b_up, w_down, b_down
):
    own = lax.axis_index("section")
    part = lax.axis_index("tensor")
    dp_count = lax.axis_size("dp")
    dp_at = lax.axis_index("dp")
    tensor_count = lax.axis_size("tensor")
    first = own == 0
    width = enc_in.shape[3]

    def both_sections(value):
        other = swapped(value)
        return jnp.where(first, value, other), jnp.where(first, other, value)

    def own_clip(value):
        return lax.dynamic_index_in_dim(value, own, 0, keepdims=False)[0]

    w_in = both_sections(attn_in[0].reshape(width, -1))
    norms = both_sections(norm_params[0])
    w_out = both_sections(attn_out[0])
    up = both_sections(w_up[0])
    up_bias = both_sections(b_up)
    down = both_sections(w_down[0])
    down_bias = both_sections(b_down)
    cross = both_sections(cross_proj[0].reshape(width, -1))
    w_memory = cross[0]
    w_query, w_back = jnp.split(cross[1], 2, axis=1)

    frames = own_clip(enc_in).astype(WIDE)
    tokens = own_clip(dec_in).astype(WIDE)
    length = own_clip(lengths)
    top_enc = own_clip(enc_cot).astype(WIDE)
    dec_rows_count = tokens.shape[0]
    own_at = part * dec_rows_count + jnp.arange(dec_rows_count, dtype=jnp.int32)
    keep = (own_at < length)[:, None]
    places = jnp.concatenate(
        [
            (part ^ step) * dec_rows_count + jnp.arange(dec_rows_count, dtype=jnp.int32)
            for step in range(tensor_count)
        ]
    )
    allowed = (places[None, :] <= places[:, None]) & (places[None, :] < length)
    top_dec = jnp.where(keep, own_clip(dec_cot), jnp.zeros((), LOW))

    enc_self, enc_self_state = self_forward(frames, norms[0][0], w_in[0], w_out[0], None)
    normed, enc_ffn_kept = norm(enc_self, norms[0][2])
    enc_ffn_in = gather_rows(normed)
    enc_active, enc_slope = gelu_both(dot_nn(enc_ffn_in, up[0]) + up_bias[0])
    enc_final = enc_self + scatter_rows(dot_nn(enc_active, down[0])) + down_bias[0]
    normed, post_kept = norm(enc_final, norms[0][1])
    post = gather_rows(normed)
    memory = dot_nn(post, w_memory).astype(LOW)
    memory_heads = memory.reshape(memory.shape[0], 2, -1, HEAD_DIM)

    dec_self, dec_self_state = self_forward(tokens, norms[1][0], w_in[1], w_out[1], allowed)
    normed, cross_kept = norm(dec_self, norms[1][1])
    cross_in = gather_rows(normed)
    queries = heads_of(dot_nn(cross_in, w_query).astype(LOW))
    blended, cross_log = attend(queries, memory_heads[:, 0], memory_heads[:, 1], None)
    cross_flat = blended.reshape(blended.shape[0], -1)
    dec_cross = dec_self + scatter_rows(dot_nt(cross_flat, w_back))
    normed, dec_ffn_kept = norm(dec_cross, norms[1][2])
    dec_ffn_in = gather_rows(normed)
    dec_active, dec_slope = gelu_both(dot_nn(dec_ffn_in, up[1]) + up_bias[1])
    dec_final = dec_cross + scatter_rows(dot_nn(dec_active, down[1])) + down_bias[1]
    dec_out = jnp.where(keep, dec_final, 0.0).astype(LOW)

    def ffn_backward(rows_in, active, slope, kept, pair, w_up_one, w_down_one, grad_rows, grad_full):
        grad_active = dot_nt(grad_full, w_down_one)
        grad_hidden_wide = grad_active * slope
        grad_hidden = grad_hidden_wide.astype(LOW)
        grad_normed = scatter_rows(dot_nt(grad_hidden, w_up_one))
        grad_w_down = dot_tn(active, grad_full)
        grad_w_up = dot_tn(rows_in, grad_hidden)
        grad_b_up = jnp.sum(grad_hidden.astype(WIDE), axis=0)
        grad_in, grad_pair = norm_back(kept, pair, grad_normed)
        grad_b_down = jnp.sum(grad_rows, axis=0)
        return grad_rows + grad_in, grad_pair, grad_w_up, grad_b_up, grad_w_down, grad_b_down

    def summed(value, section):
        low = value.astype(LOW)
        total = low.astype(WIDE) + lax.ppermute(low, "section", [(1 - section, section)]).astype(WIDE)
        total = total.astype(LOW)
        if dp_count != 4:
            return lax.psum(total, "dp")

        def along(value, pairs):
            at = section * dp_count
            return lax.ppermute(value, ("section", "dp"), [(at + s, at + d) for s, d in pairs]).astype(WIDE)

        total = (total.astype(WIDE) + along(total, [(0, 1), (3, 2)])).astype(LOW)
        total = (total.astype(WIDE) + along(total, [(1, 2), (2, 1)])).astype(LOW)
        back = along(total, [(1, 0), (2, 3)])
        ends = (dp_at == 0) | (dp_at == dp_count - 1)
        return jnp.where(ends, back.astype(LOW), total)

    grad, pair_ffn, g_up, g_bup, g_down, g_bdown = ffn_backward(
        dec_ffn_in, dec_active, dec_slope, dec_ffn_kept, norms[1][2], up[1], down[1],
        top_dec.astype(WIDE), gather_rows(top_dec),
    )
    dec_down = summed(g_down, 1)
    dec_up = summed(g_up, 1)
    grad_full = gather_rows(grad.astype(LOW))
    g_back = dot_tn(grad_full, cross_flat)
    grad_flat = dot_nn(grad_full, w_back).astype(LOW)
    grad_query, grad_key, grad_value = attend_back(
        queries, memory_heads[:, 0], memory_heads[:, 1], None, cross_log, heads_of(grad_flat)
    )
    grad_memory = jnp.stack([grad_key, grad_value], axis=1).reshape(memory.shape[0], -1).astype(LOW)
    grad_query = grad_query.reshape(cross_flat.shape[0], -1).astype(LOW)
    grad_post, pair_post = norm_back(post_kept, norms[0][1], scatter_rows(dot_nt(grad_memory, w_memory)))
    g_memory = dot_tn(post, grad_memory)
    grad_in, pair_cross = norm_back(cross_kept, norms[1][1], scatter_rows(dot_nt(grad_query, w_query)))
    g_query = dot_tn(cross_in, grad_query)
    dec_cross_sum = summed(jnp.concatenate([g_query, g_back], axis=1), 1)
    dec_in_grad, pair_self, g_in, g_out = self_backward(
        norms[1][0], w_in[1], w_out[1], allowed, dec_self_state, grad + grad_in
    )
    dec_w_out = summed(g_out, 1)
    dec_w_in = summed(g_in, 1)
    dec_small = jnp.concatenate([pair_self, pair_cross, pair_ffn, g_bdown[None], g_bup.reshape(-1, width)])

    enc_memory = summed(g_memory, 0)
    enc_grad = top_enc + grad_post
    grad, pair_ffn, g_up, g_bup, g_down, g_bdown = ffn_backward(
        enc_ffn_in, enc_active, enc_slope, enc_ffn_kept, norms[0][2], up[0], down[0],
        enc_grad, gather_rows(enc_grad.astype(LOW)),
    )
    enc_down = summed(g_down, 0)
    enc_up = summed(g_up, 0)
    enc_in_grad, pair_self, g_in, g_out = self_backward(
        norms[0][0], w_in[0], w_out[0], None, enc_self_state, grad
    )
    enc_w_out = summed(g_out, 0)
    enc_w_in = summed(g_in, 0)
    enc_small = jnp.concatenate([pair_self, pair_post, pair_ffn, g_bdown[None], g_bup.reshape(-1, width)])

    def total_small(enc_value, dec_value):
        pack = jnp.concatenate([enc_value[:7], dec_value[:7]])
        whole = pack
        for step in range(1, tensor_count):
            whole = whole + lax.ppermute(pack, "tensor", peers(step))
        enc_all = jnp.concatenate([whole[:7], enc_value[7:]])
        dec_all = jnp.concatenate([whole[7:], dec_value[7:]])
        mine = jnp.where(first, enc_all, dec_all) + swapped(jnp.where(first, dec_all, enc_all))
        if dp_count != 4:
            return lax.psum(mine, "dp")
        total = mine
        for step in range(1, dp_count):
            ring = [(at, (at + step) % dp_count) for at in range(dp_count)]
            total = total + lax.ppermute(mine, "dp", ring)
        return total

    small = total_small(enc_small, dec_small)

    def chosen(enc_value, dec_value):
        return jnp.where(first, enc_value, dec_value).astype(WIDE)[None]

    return (
        enc_final.astype(LOW)[None, None],
        dec_out[None, None],
        enc_in_grad[None, None],
        dec_in_grad[None, None],
        small[:6].reshape(1, 3, 2, width),
        chosen(enc_w_in, dec_w_in).reshape(1, width, 3, -1),
        chosen(enc_w_out, dec_w_out),
        chosen(enc_memory, dec_cross_sum).reshape(1, width, 2, -1),
        chosen(enc_up, dec_up),
        small[7:].reshape(1, -1),
        chosen(enc_down, dec_down),
        small[6:7],
    )


def solution(mesh):
    placed = (
        P(None, "dp", "tensor", None),
        P(None, "dp", "tensor", None),
        P(None, "dp"),
        P(None, "dp", "tensor", None),
        P(None, "dp", "tensor", None),
        P("section", None, None, None),
        P("section", None, None, "tensor"),
        P("section", "tensor", None),
        P("section", None, None, "tensor"),
        P("section", None, "tensor"),
        P("section", "tensor"),
        P("section", "tensor", None),
        P("section", None),
    )
    return jax.shard_map(
        body,
        mesh=mesh,
        in_specs=placed,
        out_specs=(
            P("section", "dp", "tensor", None),
            P("section", "dp", "tensor", None),
            P("section", "dp", "tensor", None),
            P("section", "dp", "tensor", None),
            P("section", None, None, None),
            P("section", None, None, "tensor"),
            P("section", "tensor", None),
            P("section", None, None, "tensor"),
            P("section", None, "tensor"),
            P("section", "tensor"),
            P("section", "tensor", None),
            P("section", None),
        ),
        check_vma=False,
    )
```

```python
import functools

import jax
import jax.numpy as jnp
from jax import lax
from jax.experimental import pallas as pl
from jax.experimental.pallas import tpu as pltpu
from jax.sharding import PartitionSpec as P

HEAD_DIM = 64
SCALING = HEAD_DIM ** (-0.5)
EPSILON = 1e-05
NEG_FILL = -1e30
LOW = jnp.bfloat16
WIDE = jnp.float32
BESIDE = 20 * 10**9


def dot_nn(left, right):
    return jnp.dot(left, right, preferred_element_type=WIDE)


def dot_tn(left, right):
    return lax.dot_general(left, right, (((0,), (0,)), ((), ())), preferred_element_type=WIDE)


def dot_nt(left, right):
    return lax.dot_general(left, right, (((1,), (1,)), ((), ())), preferred_element_type=WIDE)


def low(*shape):
    return jax.ShapeDtypeStruct(shape, LOW)


def wide(*shape):
    return jax.ShapeDtypeStruct(shape, WIDE)


class Pair:
    def __init__(self, section, own, other, which, rows=None):
        self.section, self.own, self.other, self.which = section, own, other, which
        self.rows = rows or (0, own.shape[0])
        self.shape = (self.rows[1] - self.rows[0], own.shape[1])

    def part(self, start, stop):
        return Pair(self.section, self.own, self.other, self.which, (start, stop))


class Chosen:
    def __init__(self, pair, section, own, other):
        self.mine, self.start, self.stop = section[0] == pair.which, *pair.rows
        self.own, self.other = own, other

    def __getitem__(self, index):
        if index is Ellipsis:
            index = (slice(self.start, self.stop), slice(None))
        return jnp.where(self.mine, self.own[index], self.other[index])


def run_kernel(kernel, outs, args, flops, scalars=0, beside=False, scratch=(), last=False):
    pairs = [item for item in args if isinstance(item, Pair)]
    flat = [pairs[0].section] if pairs else []
    for item in args:
        if isinstance(item, Pair):
            flat += [pltpu.with_memory_space_constraint(one, pltpu.VMEM) for one in (item.own, item.other)]
        else:
            flat.append(item)

    def body(*refs):
        given, refs = [], list(refs)
        section = refs.pop(0) if pairs else None
        for item in args:
            ref = refs.pop(0)
            given.append(Chosen(item, section, ref, refs.pop(0)) if isinstance(item, Pair) else ref)
        kernel(*given, *refs)

    whole = pl.BlockSpec(memory_space=pltpu.VMEM)
    scalars += bool(pairs)
    moved_bytes = sum(item.size * item.dtype.itemsize for item in (*flat, *outs))
    return pl.pallas_call(
        body,
        out_shape=outs if last else [pltpu.VMEM(item.shape, item.dtype) for item in outs],
        in_specs=[pl.BlockSpec(memory_space=pltpu.SMEM)] * scalars + [whole] * (len(flat) - scalars),
        out_specs=[whole] * len(outs),
        scratch_shapes=[pltpu.VMEM(shape, LOW) for shape in scratch],
        cost_estimate=pl.CostEstimate(
            flops=BESIDE if beside else flops, bytes_accessed=moved_bytes, transcendentals=0
        ),
        compiler_params=pltpu.CompilerParams(vmem_limit_bytes=24 << 20),
    )(*flat)


def put_rows(parts, rows):
    at = 0
    for part in parts:
        rows[at : at + part.shape[0], :] = part[...]
        at += part.shape[0]


def put_partial(value, outs):
    at = 0
    for out in outs:
        out[...] = value[at : at + out.shape[0]].astype(out.dtype)
        at += out.shape[0]


def partial_outs(size, width, halves=False):
    return [wide(size, width), low(size, width)] + ([low(2 * size, width)] if halves else [low(size, width)] * 2)


def normalized(values):
    center = values - jnp.mean(values, axis=-1, keepdims=True)
    rate = lax.rsqrt(jnp.mean(center * center, axis=-1, keepdims=True) + EPSILON)
    return center * rate, rate


def parts_sum(parts):
    total = parts[0][...]
    for part in parts[1:]:
        total = total + part[: total.shape[0], :].astype(WIDE)
    return total


def gelu_both(value):
    size = jnp.abs(value) * 0.7071067811865476
    bell = jnp.exp(-size * size)
    inner = 1.0 / (1.0 + 0.3275911 * size)
    series = 1.061405429 * inner - 1.453152027
    series = series * inner + 1.421413741
    series = series * inner - 0.284496736
    series = series * inner + 0.254829592
    tail = 0.5 * series * inner * bell
    share = jnp.where(value >= 0, 1.0 - tail, tail)
    return value * share, share + value * (0.3989422804014327 * bell)


def allowed_pairs(places, size, rows):
    keys = spots_of(places, size, rows, 1)
    return (keys <= spots_of(places, size, rows, 0)) & (keys < places[3])


def scores_of(queries, keyset, allowed):
    scores = dot_nt(queries, keyset) * SCALING
    return scores if allowed is None else jnp.where(allowed, scores, NEG_FILL)


def attend(queries, keyset, valueset, allowed):
    scores = scores_of(queries, keyset, allowed)
    top = jnp.max(scores, axis=-1, keepdims=True)
    powers = jnp.exp(scores - top)
    total = jnp.sum(powers, axis=-1, keepdims=True)
    weights = (powers * (1.0 / total)).astype(LOW)
    return dot_nn(weights, valueset).astype(LOW), top + jnp.log(total)


def attend_back(queries, keyset, valueset, allowed, log_total, grad):
    shares = jnp.exp(scores_of(queries, keyset, allowed) - log_total)
    grad_weights = dot_nt(grad, valueset)
    along = jnp.sum(grad_weights * shares, axis=-1, keepdims=True)
    grad_scores = (shares * (grad_weights - along)).astype(LOW)
    grad_value = dot_tn(shares.astype(LOW), grad).astype(LOW)
    grad_query = (dot_nn(grad_scores, keyset) * SCALING).astype(LOW)
    grad_key = (dot_tn(grad_scores, queries) * SCALING).astype(LOW)
    return grad_query, grad_key, grad_value


def columns(block, head, width):
    start = block * width + head * HEAD_DIM
    return slice(start, start + HEAD_DIM)


def put_normed(parts, vec, rows):
    at = 0
    for part in parts:
        unit, _ = normalized(part[...].astype(WIDE))
        rows[at : at + part.shape[0], :] = (unit * vec[0:1, :] + vec[1:2, :]).astype(LOW)
        at += part.shape[0]


def spots_of(places, size, rows, axis):
    index = lax.broadcasted_iota(jnp.int32, (rows, 1) if axis == 0 else (1, rows), axis)
    slot = index // size
    mask = jnp.where(slot == 1, places[1], jnp.where(slot == 2, places[2], slot))
    return (places[0] ^ mask) * size + index - slot * size


def after_kernel(line, count, biased, residual, vec, *refs):
    value = residual[...].astype(WIDE) + parts_sum(refs[:count])
    after, normed = refs[count : count + 2]
    if biased:
        value = value + vec[6:7, :]
        refs[-1][...] = value.astype(LOW)
    after[...] = value
    unit, _ = normalized(value)
    normed[...] = (unit * vec[line : line + 1, :] + vec[line + 1 : line + 2, :]).astype(LOW)


def after_step(residual, vec, parts, line, biased=False):
    size, width = residual.shape
    outs = [wide(size, width), low(size, width)] + [low(size, width)] * biased
    kernel = functools.partial(after_kernel, line, len(parts), biased)
    return run_kernel(kernel, outs, [residual, vec, *parts], 20 * size * width)


def back_kernel(line, upper_kind, *refs):
    if upper_kind:
        places, refs = refs[0], refs[1:]
    (after, vec, upper), parts, (grad, grad_low, sums) = refs[:3], refs[3:-3], refs[-3:]
    above = (upper[places[4]] if upper_kind == "picked" else upper[...]).astype(WIDE)
    if upper_kind == "masked":
        size = above.shape[0]
        above = jnp.where(spots_of(places, size, size, 0) < places[3], above, 0.0)
    unit, rate = normalized(after[...].astype(WIDE))
    below = parts_sum(parts)
    scaled = below * vec[line : line + 1, :]
    along = jnp.mean(scaled * unit, axis=-1, keepdims=True)
    value = above + rate * (scaled - jnp.mean(scaled, axis=-1, keepdims=True) - unit * along)
    grad[...] = value
    grad_low[...] = value.astype(LOW)
    sums[0:1, :] = jnp.sum(below * unit, axis=0, keepdims=True)
    sums[1:2, :] = jnp.sum(below, axis=0, keepdims=True)
    sums[2:3, :] = jnp.sum(above, axis=0, keepdims=True)


def back_step(after, vec, upper, parts, line, upper_kind="", places=None):
    size, width = after.shape
    outs = [wide(size, width), low(size, width), wide(3, width)]
    args = [places] * bool(upper_kind) + [after, vec, upper, *parts]
    kernel = functools.partial(back_kernel, line, upper_kind)
    return run_kernel(kernel, outs, args, 30 * size * width, int(bool(upper_kind)), last=line == 0)


def joint_back_kernel(*refs):
    places, enc_after, enc_vec, top, dec_after, dec_vec, upper = refs[:7]
    parts, (enc_grad, dec_grad, both, enc_sums, dec_sums) = refs[7:11], refs[11:]
    size = enc_after.shape[0]
    below = parts_sum(parts)
    for after, vec, above, grad, sums, place in (
        (enc_after, enc_vec, top[places[4]].astype(WIDE), enc_grad, enc_sums, slice(None, size)),
        (dec_after, dec_vec, upper[...], dec_grad, dec_sums, slice(size, None)),
    ):
        unit, rate = normalized(after[...])
        lower = below[place]
        scaled = lower * vec[2:3, :]
        along = jnp.mean(scaled * unit, axis=-1, keepdims=True)
        value = above + rate * (scaled - jnp.mean(scaled, axis=-1, keepdims=True) - unit * along)
        grad[...] = value
        both[place, :] = value.astype(LOW)
        sums[0:1, :] = jnp.sum(lower * unit, axis=0, keepdims=True)
        sums[1:2, :] = jnp.sum(lower, axis=0, keepdims=True)


def joint_back_step(places, enc_after, enc_vec, top, dec_after, dec_vec, upper, parts):
    size, width = enc_after.shape
    other = dec_after.shape[0]
    outs = [wide(size, width), wide(other, width), low(size + other, width), wide(2, width), wide(2, width)]
    args = [places, enc_after, enc_vec, top, dec_after, dec_vec, upper, *parts]
    return run_kernel(joint_back_kernel, outs, args, 60 * size * width, 1)


def self_kernel(count, masked, *refs):
    if masked:
        places, refs = refs[0], refs[1:]
    parts, refs = refs[:count], refs[count:]
    (vec, w_in, w_out, rows, packed, flat, logs), outs = refs[:7], refs[7:]
    put_normed(parts, vec, rows)
    packed[...] = dot_nt(rows[...], w_in[...]).astype(LOW)
    allowed = allowed_pairs(places, rows.shape[0] // 4, rows.shape[0]) if masked else None
    width = flat.shape[1]
    for head in range(width // HEAD_DIM):
        q, k, v = (packed[:, columns(block, head, width)] for block in range(3))
        flat[:, columns(0, head, width)], logs[:, head : head + 1] = attend(q, k, v, allowed)
    put_partial(dot_nn(flat[...], w_out[...]), outs)


def self_step(parts, vec, w_in, w_out, places=None):
    size, depth = parts[0].shape
    rows, width = 4 * size, w_out.shape[0]
    outs = [low(rows, depth), low(rows, 3 * width), low(rows, width), wide(rows, width // HEAD_DIM)]
    masked = places is not None
    outs += partial_outs(size, depth, masked)
    flops = 8 * rows * depth * width + 4 * rows * rows * width
    args = [places] * masked + [*parts, vec, w_in, w_out]
    kernel = functools.partial(self_kernel, len(parts), masked)
    return run_kernel(kernel, outs, args, flops, int(masked), masked)


def self_back_kernel(count, masked, *refs):
    if masked:
        places, refs = refs[0], refs[1:]
    parts, refs = refs[:count], refs[count:]
    (w_in, w_out, packed, logs, rows, grad_packed), outs, grad_flat = refs[:6], refs[6:-1], refs[-1]
    put_rows(parts, rows)
    grad_flat[...] = dot_nt(rows[...], w_out[...]).astype(LOW)
    allowed = allowed_pairs(places, rows.shape[0] // 4, rows.shape[0]) if masked else None
    width = grad_flat.shape[1]
    for head in range(width // HEAD_DIM):
        q, k, v = (packed[:, columns(block, head, width)] for block in range(3))
        grads = attend_back(
            q, k, v, allowed, logs[:, head : head + 1], grad_flat[:, columns(0, head, width)]
        )
        for block in range(3):
            grad_packed[:, columns(block, head, width)] = grads[block]
    put_partial(dot_nn(grad_packed[...], w_in[...]), outs)


def self_back_step(parts, w_in, w_out, packed, logs, places=None):
    rows, (width, depth) = packed.shape[0], w_out.shape
    size = rows // 4
    masked = places is not None
    outs = [low(rows, depth), low(rows, 3 * width), *partial_outs(size, depth, masked)]
    flops = 8 * rows * depth * width + 10 * rows * rows * width
    args = [places] * masked + [*parts, w_in, w_out, packed, logs]
    kernel = functools.partial(self_back_kernel, len(parts), masked)
    return run_kernel(kernel, outs, args, flops, int(masked), masked, [(rows, width)])


def ffn_kernel(part0, part1, part2, part3, up, down, vec, rows, active, slope, *outs):
    put_rows((part0, part1, part2, part3), rows)
    value, slant = gelu_both(dot_nn(rows[...], up[...]) + vec[7:8, :])
    active[...] = value.astype(LOW)
    slope[...] = slant.astype(LOW)
    put_partial(dot_nn(active[...], down[...]), outs)


def ffn_step(parts, up, down, vec):
    size, depth = parts[0].shape
    rows, units = 4 * size, up.shape[1]
    outs = [low(rows, depth), low(rows, units), low(rows, units), *partial_outs(size, depth)]
    return run_kernel(ffn_kernel, outs, [*parts, up, down, vec], 4 * rows * depth * units)


def ffn_back_kernel(part0, part1, part2, part3, up, down, slope, rows, other_rows, grad_hidden, sums, *outs):
    put_joint((part0, part1, part2, part3), rows, other_rows)
    grad = (dot_nt(rows[...], down[...]) * slope[...].astype(WIDE)).astype(LOW)
    grad_hidden[...] = grad
    sums[...] = jnp.sum(grad.astype(WIDE), axis=0, keepdims=True)
    put_partial(dot_nt(grad_hidden[...], up[...]), outs)


def ffn_back_step(parts, up, down, slope):
    both, depth = parts[0].shape
    rows, units = slope.shape
    size = rows // 4
    outs = [low(rows, depth), low(4 * (both - size), depth), low(rows, units), wide(1, units)]
    outs += partial_outs(size, depth)
    return run_kernel(ffn_back_kernel, outs, [*parts, up, down, slope], 4 * rows * depth * units)


def ffn_both_kernel(count, *refs):
    places, parts, refs = refs[0], refs[1:5], refs[5:]
    grads, refs = refs[:count], refs[count:]
    (up, down, vec), (rows, grad_rows, active, grad_hidden, sums), outs = refs[:3], refs[3:8], refs[8:]
    put_rows(parts, rows)
    put_rows(grads, grad_rows)
    keep = spots_of(places, parts[0].shape[0], rows.shape[0], 0) < places[3]
    grad_rows[...] = jnp.where(keep, grad_rows[...].astype(WIDE), 0.0).astype(LOW)
    value, slant = gelu_both(dot_nn(rows[...], up[...]) + vec[7:8, :])
    active[...] = value.astype(LOW)
    grad = (dot_nt(grad_rows[...], down[...]) * slant).astype(LOW)
    grad_hidden[...] = grad
    sums[...] = jnp.sum(grad.astype(WIDE), axis=0, keepdims=True)
    put_partial(dot_nt(grad_hidden[...], up[...]), outs)


def ffn_both_step(parts, grads, up, down, vec, places):
    size, depth = parts[0].shape
    rows, units = 4 * size, up.shape[1]
    outs = [low(rows, depth)] * 2 + [low(rows, units)] * 2 + [wide(1, units)]
    args = [places, *parts, *grads, up, down, vec]
    kernel = functools.partial(ffn_both_kernel, len(grads))
    return run_kernel(kernel, outs + partial_outs(size, depth), args, 6 * rows * depth * units, 1)


def down_kernel(active, down, *outs):
    put_partial(dot_nn(active[...], down[...]), outs)


def down_step(active, down):
    rows, units = active.shape
    depth = down.shape[1]
    return run_kernel(
        down_kernel, partial_outs(rows // 4, depth, True), [active, down], 2 * rows * units * depth, beside=True
    )


def put_joint(parts, rows, other_rows):
    size = rows.shape[0] // 4
    other = other_rows.shape[0] // 4
    for slot, part in enumerate(parts):
        rows[slot * size : (slot + 1) * size, :] = part[:size, :]
        other_rows[slot * other : (slot + 1) * other, :] = part[size:, :]


def cross_kernel(*refs):
    parts, (w_memory, w_query, w_back) = refs[:4], refs[4:7]
    rows, query_rows, memory, queries, flat, logs = refs[7:13]
    put_joint(parts, rows, query_rows)
    queries[...] = dot_nt(query_rows[...], w_query[...]).astype(LOW)
    memory[...] = dot_nt(rows[...], w_memory[...]).astype(LOW)
    width = flat.shape[1]
    for head in range(width // HEAD_DIM):
        k, v = (memory[:, columns(block, head, width)] for block in range(2))
        own = columns(0, head, width)
        flat[:, own], logs[:, head : head + 1] = attend(queries[:, own], k, v, None)
    put_partial(dot_nn(flat[...], w_back[...]), refs[13:])


def cross_step(parts, size, w_memory, w_query, w_back):
    both, depth = parts[0].shape
    frames, rows, width = 4 * size, 4 * (both - size), w_query.shape[0]
    outs = [low(frames, depth), low(rows, depth), low(frames, 2 * width), low(rows, width), low(rows, width)]
    outs += [wide(rows, width // HEAD_DIM), *partial_outs(rows // 4, depth)]
    flops = 4 * frames * depth * width + 4 * frames * rows * width + 4 * rows * depth * width
    args = [*parts, w_memory, w_query, w_back]
    return run_kernel(cross_kernel, outs, args, flops)


def cross_back_kernel(*refs):
    parts, (w_memory, w_query, w_back, queries, memory, logs) = refs[:4], refs[4:10]
    (rows, grad_query, grad_memory), grad_flat = refs[10:13], refs[-1]
    put_rows(parts, rows)
    grad_flat[...] = dot_nt(rows[...], w_back[...]).astype(LOW)
    width = queries.shape[1]
    for head in range(width // HEAD_DIM):
        own = columns(0, head, width)
        k, v = (memory[:, columns(block, head, width)] for block in range(2))
        grads = attend_back(queries[:, own], k, v, None, logs[:, head : head + 1], grad_flat[:, own])
        grad_query[:, own] = grads[0]
        grad_memory[:, own] = grads[1]
        grad_memory[:, columns(1, head, width)] = grads[2]
    outs = refs[13:-1]
    size, other = memory.shape[0] // 4, queries.shape[0] // 4
    to_memory = dot_nn(grad_memory[...], w_memory[...])
    to_query = dot_nn(grad_query[...], w_query[...])
    for slot, out in enumerate(outs):
        out[:size, :] = to_memory[slot * size : (slot + 1) * size].astype(out.dtype)
        out[size:, :] = to_query[slot * other : (slot + 1) * other].astype(out.dtype)


def cross_back_step(parts, w_memory, w_query, w_back, queries, memory, logs):
    depth = parts[0].shape[1]
    rows, width = queries.shape
    frames = memory.shape[0]
    outs = [low(rows, depth), low(rows, width), low(frames, 2 * width)]
    outs += partial_outs((frames + rows) // 4, depth)
    flops = 4 * rows * depth * width + 10 * frames * rows * width + 4 * frames * depth * width
    args = [*parts, w_memory, w_query, w_back, queries, memory, logs]
    return run_kernel(cross_back_kernel, outs, args, flops, scratch=[(rows, width)])


def grads_kernel(pairs, *refs):
    out = refs[-1]
    at = 0
    if len(refs) > 2 * pairs + 1:
        at = refs[-2].shape[0]
        out[:at, :] = refs[-2][...]
    for pair in range(pairs):
        left, right = refs[2 * pair], refs[2 * pair + 1]
        size = left.shape[1]
        out[at : at + size, :] = dot_tn(left[...], right[...]).astype(LOW)
        at += size


def weight_grads(*args, under=None):
    depth = args[1].shape[1]
    total = sum(left.shape[1] for left in args[::2])
    flops = sum(2 * left.size * depth for left in args[::2])
    kernel = functools.partial(grads_kernel, len(args) // 2)
    if under is not None:
        total, args = total + under.shape[0], (*args, under)
    return run_kernel(kernel, [low(total, depth)], args, flops, beside=True)[0]


def add_kernel(left, right, out):
    size = out.shape[0]
    out[...] = (left[...].astype(WIDE) + right[-size:, :].astype(WIDE)).astype(out.dtype)


def add_step(left, right):
    return run_kernel(add_kernel, [low(*left.shape)], [left, right], left.size)[0]


def pick_kernel(flag, left, right, out):
    out[...] = jnp.where(flag[0] == 1, left[...], right[...])


def pick_step(flag, left, right):
    return run_kernel(pick_kernel, [low(*left.shape)], [flag, left, right], left.size, 1)[0]


def own_kernel(flag, first_value, second_value, other, *outs):
    at = 0
    for out in outs:
        place = slice(at, at + out.shape[0])
        mine = jnp.where(flag[0] == 1, first_value[place, :], second_value[place, :])
        out[...] = (mine.astype(WIDE) + other[place, :].astype(WIDE)).astype(LOW)
        at += out.shape[0]


def own_sum(flag, first_value, second_value, other, pieces):
    rows, width = other.shape
    outs = [low(rows // pieces, width)] * pieces
    return run_kernel(own_kernel, outs, [flag, first_value, second_value, other], other.size, 1)


def stack_kernel(*refs):
    put_rows(refs[:-1], refs[-1])


def stack_step(*parts):
    rows = sum(part.shape[0] for part in parts)
    return run_kernel(stack_kernel, [low(rows, parts[0].shape[1])], parts, rows)[0]


def last_kernel(flag, *refs):
    out, at = refs[-1], 0
    for value, other in zip(refs[:-1:2], refs[1:-1:2]):
        size = value.shape[0]
        out[at : at + size, :] = jnp.where(flag[0] == 1, other[...], value[...]).astype(out.dtype)
        at += size


def last_step(flag, *args, kind=LOW):
    rows, width = sum(value.shape[0] for value in args[::2]), args[0].shape[1]
    outs = [jax.ShapeDtypeStruct((rows, width), kind)]
    return run_kernel(last_kernel, outs, [flag, *args], rows * width, 1, last=kind == WIDE)[0]


def pack_kernel(*refs):
    out = refs[-1]
    for at, sums in enumerate(refs[:3]):
        out[2 * at : 2 * at + 2, :] = sums[:2, :]
    out[6:7, :] = refs[2][2:3, :]
    for at, sums in enumerate(refs[3:6]):
        out[7 + 2 * at : 9 + 2 * at, :] = sums[:2, :]
    out[13:14, :] = refs[5][2:3, :]


def pack_step(*sums):
    return run_kernel(pack_kernel, [wide(14, sums[0].shape[1])], sums, 1)[0]


def total_kernel(flag, enc_bias, dec_bias, part0, part1, part2, part3, mine, other):
    total = part0[...] + part1[...] + part2[...] + part3[...]
    here = flag[0] == 1
    mine[:7, :] = jnp.where(here, total[:7], total[7:])
    other[:7, :] = jnp.where(here, total[7:], total[:7])
    mine[7:, :] = jnp.where(here, enc_bias[...], dec_bias[...])
    other[7:, :] = jnp.where(here, dec_bias[...], enc_bias[...])


def total_step(flag, enc_bias, dec_bias, parts):
    rows, width = 7 + enc_bias.shape[0], enc_bias.shape[1]
    args = [flag, enc_bias, dec_bias, *parts]
    return run_kernel(total_kernel, [wide(rows, width)] * 2, args, 1, 1)


def self_final_kernel(first_flag, end_flag, value, other, lower, upper, w_in, w_out):
    half, split = lower.shape[0], w_in.shape[0]
    enc = jnp.where(end_flag[0] == 1, other[...], value[...])
    here = first_flag[0] == 1
    low_half = jnp.where(here, enc[:half], lower[...]).astype(WIDE)
    high_half = jnp.where(here, enc[half:], upper[...]).astype(WIDE)
    w_in[:half, :] = low_half
    w_in[half:, :] = high_half[: split - half]
    w_out[...] = high_half[split - half :]


def self_final_step(first_flag, end_flag, value, other, lower, upper, split):
    rows, width = value.shape
    args = [first_flag, end_flag, value, other, lower, upper]
    return run_kernel(self_final_kernel, [wide(split, width), wide(rows - split, width)], args, 1, 2, last=True)


def scatter_kernel(flag, rows_in, keep, send):
    half = keep.shape[0]
    here = flag[0] == 1
    keep[...] = jnp.where(here, rows_in[:half, :], rows_in[half:, :])
    send[...] = jnp.where(here, rows_in[half:, :], rows_in[:half, :])


def scatter_step(flag, value):
    rows, width = value.shape
    return run_kernel(scatter_kernel, [low(rows // 2, width)] * 2, [flag, value], 1, 1)


def final_kernel(flag, first_value, second_value, out):
    out[...] = jnp.where(flag[0] == 1, first_value[...].astype(WIDE), second_value[...].astype(WIDE))


def final_step(flag, first_value, second_value):
    args = [flag, first_value, second_value]
    return run_kernel(final_kernel, [wide(*first_value.shape)], args, first_value.size, 1, last=True)[0]


def peers(slot):
    count = lax.axis_size("tensor")
    pairs = []
    for section in range(lax.axis_size("section")):
        mask = (0, 1 << section, 2 >> section, 3)[slot]
        pairs += [(section * count + at, section * count + (at ^ mask)) for at in range(count)]
    return pairs


def moved(value, slot):
    return lax.ppermute(value, ("section", "tensor"), peers(slot))


def tie(*values):
    return lax.optimization_barrier(values)


def send_rows(rows):
    far, near, side = (moved(rows, slot) for slot in (3, 1, 2))
    return [rows, near, side, far]


def send_sums(blocks):
    far, near, side = (moved(blocks[slot], slot) for slot in (3, 1, 2))
    return [blocks[0], near, side, far]


def near_rows(rows):
    return moved(rows, 1)


def far_rows(rows, near):
    return [rows, near, moved(stack_step(rows, near), 2)]


def far_sums(blocks):
    there = moved(blocks[2], 2)
    return add_step(blocks[1], there), [blocks[0], there]


def near_sums(onward, kept):
    return [*kept, moved(onward, 1)]


def swapped(value):
    return lax.ppermute(value, "section", [(0, 1), (1, 0)])


def body(
    enc_in, dec_in, lengths, enc_cot, dec_cot, norm_params, attn_in, attn_out, cross_proj, w_up, b_up, w_down, b_down
):
    own = lax.axis_index("section")
    part = lax.axis_index("tensor")
    dp_count = lax.axis_size("dp")
    dp_at = lax.axis_index("dp")
    first = own == 0
    width = enc_in.shape[3]
    enc_size = enc_in.shape[2]
    dec_size = dec_in.shape[2]
    heads_width = attn_out.shape[1]

    def own_clip(value):
        return lax.dynamic_index_in_dim(value[:, 0], own, 0, keepdims=False)

    def by_rows(value):
        return jnp.transpose(value[0], (1, 2, 0)).reshape(-1, width)

    frames, tokens, top_dec = own_clip(enc_in), own_clip(dec_in), own_clip(dec_cot)
    enc_parts = send_rows(frames)
    section = jnp.full((1,), own, jnp.int32)
    own_vec = jnp.concatenate([norm_params[0].reshape(6, width), b_down, b_up.reshape(-1, width)])

    def both(value, *after):
        value, *after = tie(value, *after)
        other = swapped(value)
        return [Pair(section, value, other, which) for which in (0, 1)], after

    (enc_vec, dec_vec), _ = both(own_vec)
    (enc_in_w, dec_in_w), _ = both(by_rows(attn_in))

    first_flag = first.astype(jnp.int32).reshape(1)

    at_end = (dp_at == 0) | (dp_at == 3)
    end_flag = at_end.astype(jnp.int32).reshape(1)

    def over_cores(first_value, second_value, pieces=1):
        other = swapped(pick_step(first_flag, second_value, first_value))
        return own_sum(first_flag, first_value, second_value, other, pieces)

    def hop(value, pairs, cores=(0, 1)):
        pairs = [(core * dp_count + a, core * dp_count + b) for core in cores for a, b in pairs]
        return lax.ppermute(value, ("section", "dp"), pairs)

    def outer_hop(inward=None, outward=None, cores=(0, 1)):
        if dp_count != 4:
            if outward is not None:
                outward[0] = lax.psum(outward[0], "dp")
                outward.append(outward[0])
            return
        pairs = [(0, 1), (3, 2)] * (inward is not None) + [(1, 0), (2, 3)] * (outward is not None)
        if inward is None or outward is None:
            value = (inward or outward)[0]
        else:
            value = pick_step(end_flag, inward[0], outward[0])
        other = hop(value, pairs, cores)
        if inward is not None:
            inward[0] = add_step(inward[0], other)
        if outward is not None:
            outward.append(other)

    def inner_hop(piece, cores=(0, 1)):
        if dp_count == 4:
            piece[0] = add_step(piece[0], hop(piece[0], [(1, 2), (2, 1)], cores))

    def pin(value, *pieces):
        value, found = tie(value, list(pieces))
        for piece, kept in zip(pieces, found):
            piece[:] = kept
        return value

    enc_parts[2], tokens = tie(enc_parts[2], tokens)
    near = near_rows(tokens)
    (enc_out_w, dec_out_w), _ = both(attn_out[0], tokens)
    enc_parts, near, lengths = tie(enc_parts, near, lengths)
    dec_parts = far_rows(tokens, near)
    length = lax.dynamic_index_in_dim(lengths, own, 0, keepdims=False)[0]
    places = jnp.stack([part, jnp.left_shift(1, own), jnp.right_shift(2, own), length, own]).astype(jnp.int32)
    enc_rows, enc_packed, enc_flat, enc_logs, *partial = self_step(enc_parts, enc_vec, enc_in_w, enc_out_w)
    partial, dec_parts, places = tie(partial, dec_parts, places)
    parts = send_sums(partial)
    (enc_up_w, dec_up_w), _ = both(w_up[0], partial[0])
    (enc_down_w, dec_down_w), _ = both(w_down[0], partial[0])
    dec_rows, dec_packed, dec_flat, dec_logs, *dec_partial = self_step(
        dec_parts, dec_vec, dec_in_w, dec_out_w, places
    )
    parts, dec_partial = tie(parts, dec_partial)
    enc_self, normed = after_step(frames, enc_vec, parts, 4)
    normed, dec_partial = tie(normed, dec_partial)
    parts = send_rows(normed)
    onward, kept = far_sums(dec_partial)
    (w_memory, w_cross), _ = both(by_rows(cross_proj), normed)
    w_query, w_back = w_cross.part(0, heads_width), w_cross.part(heads_width, 2 * heads_width)
    parts = tie(*parts)
    enc_ffn_rows, enc_active, enc_slope, *partial = ffn_step(parts, enc_up_w, enc_down_w, enc_vec)
    partial, onward, kept, top_dec = tie(partial, onward, kept, top_dec)
    parts = send_sums(partial)
    dec_parts = near_sums(onward, kept)
    near = near_rows(top_dec)
    parts, dec_parts, near = tie(parts, dec_parts, near)
    dec_self, dec_normed = after_step(tokens, dec_vec, dec_parts, 2)
    enc_final, normed, enc_low = after_step(enc_self, enc_vec, parts, 2, True)
    parts = send_rows(stack_step(normed, dec_normed))
    top_parts = far_rows(top_dec, near)
    parts = tie(*parts)
    post_rows, cross_rows, memory, queries, cross_flat, cross_logs, *partial = cross_step(
        parts, enc_size, w_memory, w_query, w_back
    )
    partial, top_parts = tie(partial, top_parts)
    parts = send_sums(partial)
    dec_cross, normed = after_step(dec_self, dec_vec, parts, 4)
    parts = send_rows(normed)
    dec_ffn_rows, top_rows, dec_active, dec_hidden, dec_bup, *partial = ffn_both_step(
        parts, top_parts, dec_up_w, dec_down_w, dec_vec, places
    )
    partial, dec_active, dec_hidden = tie(partial, dec_active, dec_hidden)
    parts = send_sums(partial)
    g_down = weight_grads(dec_active, top_rows)
    g_up = weight_grads(dec_ffn_rows, dec_hidden)
    parts, g_down, g_up = tie(parts, g_down, g_up)
    dec_grad, grad_low, dec_sums_ffn = back_step(dec_cross, dec_vec, top_dec, parts, 4, "masked", places)
    grad_low, dec_active, g_down, g_up = tie(grad_low, dec_active, g_down, g_up)
    parts = send_rows(grad_low)
    dec_near, dec_far = ([item] for item in over_cores(g_down, g_up, 2))
    out_partial = down_step(dec_active, dec_down_w)
    parts, out_partial = pin((parts, out_partial), dec_near, dec_far)
    grad_rows, grad_query, grad_memory, *partial = cross_back_step(
        parts, w_memory, w_query, w_back, queries, memory, cross_logs
    )
    partial, grad_memory, grad_query, *dec_near = tie(partial, grad_memory, grad_query, *dec_near)
    parts = send_sums(partial)
    outer_hop(dec_near)
    g_cross = weight_grads(grad_query, cross_rows, cross_flat, grad_rows)
    parts, g_cross = pin((parts, g_cross), dec_near)
    enc_grad, dec_grad, grad_low, enc_sums_post, dec_sums_cross = joint_back_step(
        places, enc_final, enc_vec, enc_cot[:, 0], dec_self, dec_vec, dec_grad, parts
    )
    grad_low, grad_memory = tie(grad_low, grad_memory)
    grad_low = pin(grad_low, dec_near, dec_far)
    parts = send_rows(grad_low)
    outer_hop(dec_far)
    inner_hop(dec_near)
    g_memory = weight_grads(grad_memory, post_rows)
    parts, g_memory = pin((parts, g_memory), dec_near, dec_far)
    cross = list(over_cores(g_memory, g_cross))
    grad_rows, dec_grad_rows, enc_hidden, enc_bup, *partial = ffn_back_step(
        parts, enc_up_w, enc_down_w, enc_slope
    )
    partial, enc_hidden, grad_rows, dec_grad_rows = tie(partial, enc_hidden, grad_rows, dec_grad_rows)
    partial = pin(partial, dec_near, dec_far, cross)
    parts = send_sums(partial)
    outer_hop(cross, dec_near)
    inner_hop(dec_far)
    g_down = weight_grads(enc_active, grad_rows)
    g_up = weight_grads(enc_ffn_rows, enc_hidden)
    dec_grad_rows, dec_grad_packed, *dec_partial = self_back_step(
        [dec_grad_rows], dec_in_w, dec_out_w, dec_packed, dec_logs, places
    )
    parts, dec_partial, dec_grad_packed, g_down, g_up = pin(
        (parts, dec_partial, dec_grad_packed, g_down, g_up), cross, dec_near, dec_far
    )
    near_ffn, far_ffn = ([item] for item in over_cores(g_down, g_up, 2))
    enc_grad, grad_low, enc_sums_ffn = back_step(enc_self, enc_vec, enc_grad, parts, 4)
    grad_low, dec_partial, dec_grad_packed = tie(grad_low, dec_partial, dec_grad_packed)
    grad_low = pin(grad_low, near_ffn, far_ffn, cross, dec_far)
    parts = send_rows(grad_low)
    outer_hop(near_ffn, dec_far)
    inner_hop(cross)
    g_dec = weight_grads(dec_grad_packed, dec_rows, dec_flat, dec_grad_rows)
    parts, g_dec = pin((parts, g_dec), near_ffn, cross, dec_far)
    outer_hop(far_ffn, cross)
    inner_hop(near_ffn)
    dec_self_sum, dec_send = scatter_step(first_flag, g_dec)
    dec_self_sum = [add_step(dec_self_sum, swapped(dec_send))]
    enc_grad_rows, enc_grad_packed, *partial = self_back_step(parts, enc_in_w, enc_out_w, enc_packed, enc_logs)
    partial, enc_grad_packed, dec_partial = tie(partial, enc_grad_packed, dec_partial)
    partial = pin(partial, near_ffn, far_ffn, cross, dec_self_sum)
    parts = send_sums(partial)
    outer_hop(dec_self_sum, near_ffn)
    inner_hop(far_ffn)
    g_enc = weight_grads(enc_grad_packed, enc_rows, enc_flat, enc_grad_rows)
    parts, g_enc, dec_partial = pin((parts, g_enc, dec_partial), dec_self_sum, far_ffn, near_ffn)
    enc_self_sum = [add_step(g_enc, lax.ppermute(g_enc, "section", [(1, 0)]))]
    outer_hop(None, far_ffn)
    inner_hop(dec_self_sum)
    onward, kept = far_sums(dec_partial)
    enc_in_grad, _, enc_sums_self = back_step(frames, enc_vec, enc_grad, parts, 0)
    enc_in_grad = pin(enc_in_grad, enc_self_sum)
    outer_hop(enc_self_sum, cores=(0,))
    dec_parts = near_sums(onward, kept)
    dec_in_grad, _, dec_sums_self = back_step(tokens, dec_vec, dec_grad, dec_parts, 0)
    pack = pack_step(enc_sums_self, enc_sums_post, enc_sums_ffn, dec_sums_self, dec_sums_cross, dec_sums_ffn)
    pack = pin(pack, enc_self_sum, far_ffn, dec_self_sum)
    outer_hop(None, dec_self_sum)
    inner_hop(enc_self_sum, cores=(0,))
    pieces = [pack, moved(pack, 1), moved(pack, 2), moved(pack, 3)]
    pieces, out_partial = tie(pieces, out_partial)
    mine, theirs = total_step(first_flag, enc_bup.reshape(-1, width), dec_bup.reshape(-1, width), pieces)
    mine = mine + swapped(theirs)
    onward, kept = far_sums(out_partial)
    enc_ffn = last_step(end_flag, *near_ffn, *far_ffn)
    dec_ffn = last_step(end_flag, *dec_near, *dec_far)
    other_ffn = swapped(pick_step(first_flag, dec_ffn, enc_ffn))
    mine, onward, kept = pin((mine, onward, kept), enc_self_sum, dec_self_sum)
    outer_hop(None, enc_self_sum, cores=(0,))
    dec_half = last_step(end_flag, *dec_self_sum)
    dec_lower = lax.ppermute(dec_half, "section", [(0, 1)])
    if dp_count != 4:
        small = lax.psum(mine, "dp")
    else:
        small = mine
        for step in range(1, dp_count):
            small = small + lax.ppermute(mine, "dp", [(at, at ^ step) for at in range(dp_count)])
    out_parts = near_sums(onward, kept)
    down_bias = jnp.where(first, dec_vec.other[6], dec_vec.own[6])
    dec_final = dec_cross + out_parts[0] + down_bias
    for item in out_parts[1:]:
        dec_final = dec_final + item[:dec_size].astype(WIDE)
    keep = part * dec_size + jnp.arange(dec_size, dtype=jnp.int32) < length
    dec_out = jnp.where(keep[:, None], dec_final, 0.0).astype(LOW)
    down_grad = final_step(first_flag, enc_ffn, other_ffn)
    up_grad = final_step(first_flag, other_ffn, dec_ffn)
    cross_grad = last_step(end_flag, *cross, kind=WIDE)
    small, dec_out, down_grad, up_grad, cross_grad, dec_lower = pin(
        (small, dec_out, down_grad, up_grad, cross_grad, dec_lower), enc_self_sum
    )
    in_grad, out_grad = self_final_step(
        first_flag, end_flag, *enc_self_sum, dec_lower, dec_half, 3 * heads_width
    )

    def by_columns(value, groups):
        return jnp.transpose(value.reshape(groups, -1, width), (2, 0, 1))[None]

    return (
        enc_low[None, None],
        dec_out[None, None],
        enc_in_grad[None, None],
        dec_in_grad[None, None],
        small[:6].reshape(1, 3, 2, width),
        by_columns(in_grad, 3),
        out_grad[None],
        by_columns(cross_grad, 2),
        up_grad[None],
        small[7:].reshape(1, -1),
        down_grad[None],
        small[6:7],
    )


def solution(mesh):
    placed = (
        P(None, "dp", "tensor", None),
        P(None, "dp", "tensor", None),
        P(None, "dp"),
        P(None, "dp", "tensor", None),
        P(None, "dp", "tensor", None),
        P("section", None, None, None),
        P("section", None, None, "tensor"),
        P("section", "tensor", None),
        P("section", None, None, "tensor"),
        P("section", None, "tensor"),
        P("section", "tensor"),
        P("section", "tensor", None),
        P("section", None),
    )
    return jax.shard_map(
        body,
        mesh=mesh,
        in_specs=placed,
        out_specs=(
            P("section", "dp", "tensor", None),
            P("section", "dp", "tensor", None),
            P("section", "dp", "tensor", None),
            P("section", "dp", "tensor", None),
            P("section", None, None, None),
            P("section", None, None, "tensor"),
            P("section", "tensor", None),
            P("section", None, None, "tensor"),
            P("section", None, "tensor"),
            P("section", "tensor"),
            P("section", "tensor", None),
            P("section", None),
        ),
        check_vma=False,
    )
```

```python
import functools

import jax
import jax.numpy as jnp
from jax import lax
from jax.experimental import pallas as pl
from jax.experimental.pallas import tpu as pltpu
from jax.sharding import PartitionSpec as P

HEAD_DIM = 64
SCALING = HEAD_DIM ** (-0.5)
EPSILON = 1e-05
NEG_FILL = -1e30
LOW = jnp.bfloat16
WIDE = jnp.float32
BESIDE = 20 * 10**9


def dot_nn(left, right):
    return jnp.dot(left, right, preferred_element_type=WIDE)


def dot_tn(left, right):
    return lax.dot_general(left, right, (((0,), (0,)), ((), ())), preferred_element_type=WIDE)


def dot_nt(left, right):
    return lax.dot_general(left, right, (((1,), (1,)), ((), ())), preferred_element_type=WIDE)


def low(*shape):
    return jax.ShapeDtypeStruct(shape, LOW)


def wide(*shape):
    return jax.ShapeDtypeStruct(shape, WIDE)


class Pair:
    def __init__(self, section, own, other, which, rows=None):
        self.section, self.own, self.other, self.which = section, own, other, which
        self.rows = rows or (0, own.shape[0])
        self.shape = (self.rows[1] - self.rows[0], own.shape[1])

    def part(self, start, stop):
        return Pair(self.section, self.own, self.other, self.which, (start, stop))


class Far:
    def __init__(self, item):
        self.item = item
        self.shape = item.shape

    def sources(self):
        return [self.item.own, self.item.other] if isinstance(self.item, Pair) else [self.item]

    def start(self, section, refs, scratch, sem):
        if not isinstance(self.item, Pair):
            copy = pltpu.make_async_copy(refs[0], scratch, sem)
            copy.start()
            return copy
        rows = pl.ds(self.item.rows[0], self.shape[0])
        copies = [pltpu.make_async_copy(ref.at[rows, :], scratch, sem) for ref in refs]
        pl.when(section[0] == self.item.which)(copies[0].start)
        pl.when(section[0] != self.item.which)(copies[1].start)
        return copies[0]


class Held:
    def __init__(self, ref, copy):
        self.ref, self.copy, self.shape, self.dtype = ref, copy, ref.shape, ref.dtype

    def __getitem__(self, index):
        if self.copy is not None:
            self.copy.wait()
            self.copy = None
        return self.ref[index]


class Chosen:
    def __init__(self, pair, section, own, other):
        self.mine, self.start, self.stop = section[0] == pair.which, *pair.rows
        self.own, self.other = own, other

    def __getitem__(self, index):
        if index is Ellipsis:
            index = (slice(self.start, self.stop), slice(None))
        return jnp.where(self.mine, self.own[index], self.other[index])


def run_kernel(kernel, outs, args, flops, scalars=0, beside=False, scratch=(), last=False):
    away, near = pl.BlockSpec(memory_space=pltpu.HBM), pl.BlockSpec(memory_space=pltpu.VMEM)
    smem = pl.BlockSpec(memory_space=pltpu.SMEM)
    coming = [item for item in args if isinstance(item, Far)]
    pairs = [item.item if isinstance(item, Far) else item for item in args]
    pairs = [item for item in pairs if isinstance(item, Pair)]
    flat, specs = [item.section for item in pairs[:1]], [smem] * len(pairs[:1])
    for at, item in enumerate(args):
        kind, place = (away, pltpu.HBM) if isinstance(item, Far) else (near, pltpu.VMEM)
        sources = item.sources() if isinstance(item, Far) else [item]
        if isinstance(item, Pair):
            sources = [item.own, item.other]
        if isinstance(item, (Far, Pair)):
            sources = [pltpu.with_memory_space_constraint(one, place) for one in sources]
        flat += sources
        specs += [smem if at < scalars else kind] * len(sources)

    def body(*refs):
        given, refs = [], list(refs)
        section = refs.pop(0) if pairs else None
        sources = []
        for item in args:
            double = isinstance(item.item if isinstance(item, Far) else item, Pair)
            sources.append([refs.pop(0) for _ in range(1 + double)])
        results, refs = refs[: len(outs)], refs[len(outs) :]
        buffers, refs = refs[: len(coming)], refs[len(coming) :]
        sems = refs.pop(0) if coming else None
        at = 0
        for item, found in zip(args, sources):
            if isinstance(item, Far):
                given.append(Held(buffers[at], item.start(section, found, buffers[at], sems.at[at])))
                at += 1
            else:
                given.append(Chosen(item, section, *found) if isinstance(item, Pair) else found[0])
        kernel(*given, *results, *refs)
        for item in given:
            if isinstance(item, Held) and item.copy is not None:
                item.copy.wait()

    moved_bytes = sum(item.size * item.dtype.itemsize for item in (*flat, *outs))
    return pl.pallas_call(
        body,
        out_shape=outs if last else [pltpu.VMEM(item.shape, item.dtype) for item in outs],
        in_specs=specs,
        out_specs=[near] * len(outs),
        scratch_shapes=[
            *[pltpu.VMEM(item.shape, item.sources()[0].dtype) for item in coming],
            *[pltpu.SemaphoreType.DMA((len(coming),))] * bool(coming),
            *[pltpu.VMEM(shape, LOW) for shape in scratch],
        ],
        cost_estimate=pl.CostEstimate(
            flops=BESIDE if beside else flops, bytes_accessed=moved_bytes, transcendentals=0
        ),
        compiler_params=pltpu.CompilerParams(vmem_limit_bytes=24 << 20),
    )(*flat)


def put_rows(parts, rows):
    at = 0
    for part in parts:
        rows[at : at + part.shape[0], :] = part[...]
        at += part.shape[0]


def put_partial(value, outs):
    at = 0
    for out in outs:
        out[...] = value[at : at + out.shape[0]].astype(out.dtype)
        at += out.shape[0]


def partial_outs(size, width, halves=False):
    return [wide(size, width), low(size, width)] + ([low(2 * size, width)] if halves else [low(size, width)] * 2)


def normalized(values):
    center = values - jnp.mean(values, axis=-1, keepdims=True)
    rate = lax.rsqrt(jnp.mean(center * center, axis=-1, keepdims=True) + EPSILON)
    return center * rate, rate


def parts_sum(parts):
    total = parts[0][...]
    for part in parts[1:]:
        total = total + part[: total.shape[0], :].astype(WIDE)
    return total


def gelu_both(value):
    size = jnp.abs(value) * 0.7071067811865476
    bell = jnp.exp(-size * size)
    inner = 1.0 / (1.0 + 0.3275911 * size)
    series = 1.061405429 * inner - 1.453152027
    series = series * inner + 1.421413741
    series = series * inner - 0.284496736
    series = series * inner + 0.254829592
    tail = 0.5 * series * inner * bell
    share = jnp.where(value >= 0, 1.0 - tail, tail)
    return value * share, share + value * (0.3989422804014327 * bell)


def allowed_pairs(places, size, rows):
    keys = spots_of(places, size, rows, 1)
    return (keys <= spots_of(places, size, rows, 0)) & (keys < places[3])


def scores_of(queries, keyset, allowed):
    scores = dot_nt(queries, keyset) * SCALING
    return scores if allowed is None else jnp.where(allowed, scores, NEG_FILL)


def attend(queries, keyset, valueset, allowed):
    scores = scores_of(queries, keyset, allowed)
    top = jnp.max(scores, axis=-1, keepdims=True)
    powers = jnp.exp(scores - top)
    total = jnp.sum(powers, axis=-1, keepdims=True)
    weights = (powers * (1.0 / total)).astype(LOW)
    return dot_nn(weights, valueset).astype(LOW), top + jnp.log(total)


def attend_back(queries, keyset, valueset, allowed, log_total, grad):
    shares = jnp.exp(scores_of(queries, keyset, allowed) - log_total)
    grad_weights = dot_nt(grad, valueset)
    along = jnp.sum(grad_weights * shares, axis=-1, keepdims=True)
    grad_scores = (shares * (grad_weights - along)).astype(LOW)
    grad_value = dot_tn(shares.astype(LOW), grad).astype(LOW)
    grad_query = (dot_nn(grad_scores, keyset) * SCALING).astype(LOW)
    grad_key = (dot_tn(grad_scores, queries) * SCALING).astype(LOW)
    return grad_query, grad_key, grad_value


def columns(block, head, width):
    start = block * width + head * HEAD_DIM
    return slice(start, start + HEAD_DIM)


def put_normed(parts, vec, rows):
    at = 0
    for part in parts:
        unit, _ = normalized(part[...].astype(WIDE))
        rows[at : at + part.shape[0], :] = (unit * vec[0:1, :] + vec[1:2, :]).astype(LOW)
        at += part.shape[0]


def spots_of(places, size, rows, axis):
    index = lax.broadcasted_iota(jnp.int32, (rows, 1) if axis == 0 else (1, rows), axis)
    slot = index // size
    mask = jnp.where(slot == 1, places[1], jnp.where(slot == 2, places[2], slot))
    return (places[0] ^ mask) * size + index - slot * size


def after_kernel(line, count, biased, residual, vec, *refs):
    value = residual[...].astype(WIDE) + parts_sum(refs[:count])
    after, normed = refs[count : count + 2]
    if biased:
        value = value + vec[6:7, :]
        refs[-1][...] = value.astype(LOW)
    after[...] = value
    unit, _ = normalized(value)
    normed[...] = (unit * vec[line : line + 1, :] + vec[line + 1 : line + 2, :]).astype(LOW)


def after_step(residual, vec, parts, line, biased=False):
    size, width = residual.shape
    outs = [wide(size, width), low(size, width)] + [low(size, width)] * biased
    kernel = functools.partial(after_kernel, line, len(parts), biased)
    return run_kernel(kernel, outs, [residual, vec, *parts], 20 * size * width)


def back_kernel(line, upper_kind, *refs):
    if upper_kind:
        places, refs = refs[0], refs[1:]
    (after, vec, upper), parts, (grad, grad_low, sums) = refs[:3], refs[3:-3], refs[-3:]
    above = (upper[places[4]] if upper_kind == "picked" else upper[...]).astype(WIDE)
    if upper_kind == "masked":
        size = above.shape[0]
        above = jnp.where(spots_of(places, size, size, 0) < places[3], above, 0.0)
    unit, rate = normalized(after[...].astype(WIDE))
    below = parts_sum(parts)
    scaled = below * vec[line : line + 1, :]
    along = jnp.mean(scaled * unit, axis=-1, keepdims=True)
    value = above + rate * (scaled - jnp.mean(scaled, axis=-1, keepdims=True) - unit * along)
    grad[...] = value
    grad_low[...] = value.astype(LOW)
    sums[0:1, :] = jnp.sum(below * unit, axis=0, keepdims=True)
    sums[1:2, :] = jnp.sum(below, axis=0, keepdims=True)
    sums[2:3, :] = jnp.sum(above, axis=0, keepdims=True)


def back_step(after, vec, upper, parts, line, upper_kind="", places=None):
    size, width = after.shape
    outs = [wide(size, width), low(size, width), wide(3, width)]
    args = [places] * bool(upper_kind) + [after, vec, upper, *parts]
    kernel = functools.partial(back_kernel, line, upper_kind)
    return run_kernel(kernel, outs, args, 30 * size * width, int(bool(upper_kind)), last=line == 0)


def joint_back_kernel(*refs):
    places, enc_after, enc_vec, top, dec_after, dec_vec, upper = refs[:7]
    parts, (enc_grad, dec_grad, both, enc_sums, dec_sums) = refs[7:11], refs[11:]
    size = enc_after.shape[0]
    below = parts_sum(parts)
    for after, vec, above, grad, sums, place in (
        (enc_after, enc_vec, top[places[4]].astype(WIDE), enc_grad, enc_sums, slice(None, size)),
        (dec_after, dec_vec, upper[...], dec_grad, dec_sums, slice(size, None)),
    ):
        unit, rate = normalized(after[...])
        lower = below[place]
        scaled = lower * vec[2:3, :]
        along = jnp.mean(scaled * unit, axis=-1, keepdims=True)
        value = above + rate * (scaled - jnp.mean(scaled, axis=-1, keepdims=True) - unit * along)
        grad[...] = value
        both[place, :] = value.astype(LOW)
        sums[0:1, :] = jnp.sum(lower * unit, axis=0, keepdims=True)
        sums[1:2, :] = jnp.sum(lower, axis=0, keepdims=True)


def joint_back_step(places, enc_after, enc_vec, top, dec_after, dec_vec, upper, parts):
    size, width = enc_after.shape
    other = dec_after.shape[0]
    outs = [wide(size, width), wide(other, width), low(size + other, width), wide(2, width), wide(2, width)]
    args = [places, enc_after, enc_vec, top, dec_after, dec_vec, upper, *parts]
    return run_kernel(joint_back_kernel, outs, args, 60 * size * width, 1)


def self_kernel(count, masked, *refs):
    if masked:
        places, refs = refs[0], refs[1:]
    parts, refs = refs[:count], refs[count:]
    (vec, w_in, w_out, rows, packed, flat, logs), outs = refs[:7], refs[7:]
    put_normed(parts, vec, rows)
    packed[...] = dot_nt(rows[...], w_in[...]).astype(LOW)
    allowed = allowed_pairs(places, rows.shape[0] // 4, rows.shape[0]) if masked else None
    width = flat.shape[1]
    for head in range(width // HEAD_DIM):
        q, k, v = (packed[:, columns(block, head, width)] for block in range(3))
        flat[:, columns(0, head, width)], logs[:, head : head + 1] = attend(q, k, v, allowed)
    put_partial(dot_nn(flat[...], w_out[...]), outs)


def self_step(parts, vec, w_in, w_out, places=None):
    size, depth = parts[0].shape
    rows, width = 4 * size, w_out.shape[0]
    outs = [low(rows, depth), low(rows, 3 * width), low(rows, width), wide(rows, width // HEAD_DIM)]
    masked = places is not None
    outs += partial_outs(size, depth, masked)
    flops = 8 * rows * depth * width + 4 * rows * rows * width
    args = [places] * masked + [*parts, vec, w_in, w_out]
    kernel = functools.partial(self_kernel, len(parts), masked)
    return run_kernel(kernel, outs, args, flops, int(masked), masked)


def self_back_kernel(count, masked, *refs):
    if masked:
        places, refs = refs[0], refs[1:]
    parts, refs = refs[:count], refs[count:]
    (w_in, w_out, packed, logs, rows, grad_packed), outs, grad_flat = refs[:6], refs[6:-1], refs[-1]
    put_rows(parts, rows)
    grad_flat[...] = dot_nt(rows[...], w_out[...]).astype(LOW)
    allowed = allowed_pairs(places, rows.shape[0] // 4, rows.shape[0]) if masked else None
    width = grad_flat.shape[1]
    for head in range(width // HEAD_DIM):
        q, k, v = (packed[:, columns(block, head, width)] for block in range(3))
        grads = attend_back(
            q, k, v, allowed, logs[:, head : head + 1], grad_flat[:, columns(0, head, width)]
        )
        for block in range(3):
            grad_packed[:, columns(block, head, width)] = grads[block]
    put_partial(dot_nn(grad_packed[...], w_in[...]), outs)


def self_back_step(parts, w_in, w_out, packed, logs, places=None):
    rows, (width, depth) = packed.shape[0], w_out.shape
    size = rows // 4
    masked = places is not None
    outs = [low(rows, depth), low(rows, 3 * width), *partial_outs(size, depth, masked)]
    flops = 8 * rows * depth * width + 10 * rows * rows * width
    args = [places] * masked + [*parts, w_in, w_out, packed, logs]
    kernel = functools.partial(self_back_kernel, len(parts), masked)
    return run_kernel(kernel, outs, args, flops, int(masked), masked, [(rows, width)])


def ffn_kernel(part0, part1, part2, part3, up, down, vec, rows, active, slope, *outs):
    put_rows((part0, part1, part2, part3), rows)
    value, slant = gelu_both(dot_nn(rows[...], up[...]) + vec[7:8, :])
    active[...] = value.astype(LOW)
    slope[...] = slant.astype(LOW)
    put_partial(dot_nn(active[...], down[...]), outs)


def ffn_step(parts, up, down, vec):
    size, depth = parts[0].shape
    rows, units = 4 * size, up.shape[1]
    outs = [low(rows, depth), low(rows, units), low(rows, units), *partial_outs(size, depth)]
    return run_kernel(ffn_kernel, outs, [*parts, up, down, vec], 4 * rows * depth * units)


def ffn_back_kernel(part0, part1, part2, part3, up, down, slope, rows, other_rows, grad_hidden, sums, *outs):
    put_joint((part0, part1, part2, part3), rows, other_rows)
    grad = (dot_nt(rows[...], down[...]) * slope[...].astype(WIDE)).astype(LOW)
    grad_hidden[...] = grad
    sums[...] = jnp.sum(grad.astype(WIDE), axis=0, keepdims=True)
    put_partial(dot_nt(grad_hidden[...], up[...]), outs)


def ffn_back_step(parts, up, down, slope):
    both, depth = parts[0].shape
    rows, units = slope.shape
    size = rows // 4
    outs = [low(rows, depth), low(4 * (both - size), depth), low(rows, units), wide(1, units)]
    outs += partial_outs(size, depth)
    return run_kernel(ffn_back_kernel, outs, [*parts, up, down, slope], 4 * rows * depth * units)


def ffn_both_kernel(count, *refs):
    places, parts, refs = refs[0], refs[1:5], refs[5:]
    grads, refs = refs[:count], refs[count:]
    (up, down, vec), (rows, grad_rows, active, grad_hidden, sums), outs = refs[:3], refs[3:8], refs[8:]
    put_rows(parts, rows)
    put_rows(grads, grad_rows)
    keep = spots_of(places, parts[0].shape[0], rows.shape[0], 0) < places[3]
    grad_rows[...] = jnp.where(keep, grad_rows[...].astype(WIDE), 0.0).astype(LOW)
    value, slant = gelu_both(dot_nn(rows[...], up[...]) + vec[7:8, :])
    active[...] = value.astype(LOW)
    grad = (dot_nt(grad_rows[...], down[...]) * slant).astype(LOW)
    grad_hidden[...] = grad
    sums[...] = jnp.sum(grad.astype(WIDE), axis=0, keepdims=True)
    put_partial(dot_nt(grad_hidden[...], up[...]), outs)


def ffn_both_step(parts, grads, up, down, vec, places):
    size, depth = parts[0].shape
    rows, units = 4 * size, up.shape[1]
    outs = [low(rows, depth)] * 2 + [low(rows, units)] * 2 + [wide(1, units)]
    args = [places, *parts, *grads, up, down, vec]
    kernel = functools.partial(ffn_both_kernel, len(grads))
    return run_kernel(kernel, outs + partial_outs(size, depth), args, 6 * rows * depth * units, 1)


def down_kernel(active, down, *outs):
    put_partial(dot_nn(active[...], down[...]), outs)


def down_step(active, down):
    rows, units = active.shape
    depth = down.shape[1]
    return run_kernel(
        down_kernel, partial_outs(rows // 4, depth, True), [active, down], 2 * rows * units * depth, beside=True
    )


def put_joint(parts, rows, other_rows):
    size = rows.shape[0] // 4
    other = other_rows.shape[0] // 4
    for slot, part in enumerate(parts):
        rows[slot * size : (slot + 1) * size, :] = part[:size, :]
        other_rows[slot * other : (slot + 1) * other, :] = part[size:, :]


def cross_kernel(*refs):
    parts, (w_memory, w_query, w_back) = refs[:4], refs[4:7]
    rows, query_rows, memory, queries, flat, logs = refs[7:13]
    put_joint(parts, rows, query_rows)
    queries[...] = dot_nt(query_rows[...], w_query[...]).astype(LOW)
    memory[...] = dot_nt(rows[...], w_memory[...]).astype(LOW)
    width = flat.shape[1]
    for head in range(width // HEAD_DIM):
        k, v = (memory[:, columns(block, head, width)] for block in range(2))
        own = columns(0, head, width)
        flat[:, own], logs[:, head : head + 1] = attend(queries[:, own], k, v, None)
    put_partial(dot_nn(flat[...], w_back[...]), refs[13:])


def cross_step(parts, size, w_memory, w_query, w_back):
    both, depth = parts[0].shape
    frames, rows, width = 4 * size, 4 * (both - size), w_query.shape[0]
    outs = [low(frames, depth), low(rows, depth), low(frames, 2 * width), low(rows, width), low(rows, width)]
    outs += [wide(rows, width // HEAD_DIM), *partial_outs(rows // 4, depth)]
    flops = 4 * frames * depth * width + 4 * frames * rows * width + 4 * rows * depth * width
    args = [*parts, w_memory, w_query, w_back]
    return run_kernel(cross_kernel, outs, args, flops)


def cross_back_kernel(*refs):
    parts, (w_memory, w_query, w_back, queries, memory, logs) = refs[:4], refs[4:10]
    (rows, grad_query, grad_memory), grad_flat = refs[10:13], refs[-1]
    put_rows(parts, rows)
    grad_flat[...] = dot_nt(rows[...], w_back[...]).astype(LOW)
    width = queries.shape[1]
    for head in range(width // HEAD_DIM):
        own = columns(0, head, width)
        k, v = (memory[:, columns(block, head, width)] for block in range(2))
        grads = attend_back(queries[:, own], k, v, None, logs[:, head : head + 1], grad_flat[:, own])
        grad_query[:, own] = grads[0]
        grad_memory[:, own] = grads[1]
        grad_memory[:, columns(1, head, width)] = grads[2]
    outs = refs[13:-1]
    size, other = memory.shape[0] // 4, queries.shape[0] // 4
    to_memory = dot_nn(grad_memory[...], w_memory[...])
    to_query = dot_nn(grad_query[...], w_query[...])
    for slot, out in enumerate(outs):
        out[:size, :] = to_memory[slot * size : (slot + 1) * size].astype(out.dtype)
        out[size:, :] = to_query[slot * other : (slot + 1) * other].astype(out.dtype)


def cross_back_step(parts, w_memory, w_query, w_back, queries, memory, logs):
    depth = parts[0].shape[1]
    rows, width = queries.shape
    frames = memory.shape[0]
    outs = [low(rows, depth), low(rows, width), low(frames, 2 * width)]
    outs += partial_outs((frames + rows) // 4, depth)
    flops = 4 * rows * depth * width + 10 * frames * rows * width + 4 * frames * depth * width
    args = [*parts, w_memory, w_query, w_back, queries, memory, logs]
    return run_kernel(cross_back_kernel, outs, args, flops, scratch=[(rows, width)])


def grads_kernel(pairs, *refs):
    out = refs[-1]
    at = 0
    if len(refs) > 2 * pairs + 1:
        at = refs[-2].shape[0]
        out[:at, :] = refs[-2][...]
    for pair in range(pairs):
        left, right = refs[2 * pair], refs[2 * pair + 1]
        size = left.shape[1]
        out[at : at + size, :] = dot_tn(left[...], right[...]).astype(LOW)
        at += size


def weight_grads(*args, under=None):
    depth = args[1].shape[1]
    total = sum(left.shape[1] for left in args[::2])
    flops = sum(2 * left.size * depth for left in args[::2])
    kernel = functools.partial(grads_kernel, len(args) // 2)
    if under is not None:
        total, args = total + under.shape[0], (*args, under)
    return run_kernel(kernel, [low(total, depth)], args, flops, beside=True)[0]


def add_kernel(left, right, out):
    size = out.shape[0]
    out[...] = (left[...].astype(WIDE) + right[-size:, :].astype(WIDE)).astype(out.dtype)


def add_step(left, right):
    return run_kernel(add_kernel, [low(*left.shape)], [left, right], left.size)[0]


def pick_kernel(flag, left, right, out):
    out[...] = jnp.where(flag[0] == 1, left[...], right[...])


def pick_step(flag, left, right):
    return run_kernel(pick_kernel, [low(*left.shape)], [flag, left, right], left.size, 1)[0]


def own_kernel(flag, first_value, second_value, other, *outs):
    at = 0
    for out in outs:
        place = slice(at, at + out.shape[0])
        mine = jnp.where(flag[0] == 1, first_value[place, :], second_value[place, :])
        out[...] = (mine.astype(WIDE) + other[place, :].astype(WIDE)).astype(LOW)
        at += out.shape[0]


def own_sum(flag, first_value, second_value, other, pieces):
    rows, width = other.shape
    outs = [low(rows // pieces, width)] * pieces
    return run_kernel(own_kernel, outs, [flag, first_value, second_value, other], other.size, 1)


def stack_kernel(*refs):
    put_rows(refs[:-1], refs[-1])


def stack_step(*parts):
    rows = sum(part.shape[0] for part in parts)
    return run_kernel(stack_kernel, [low(rows, parts[0].shape[1])], parts, rows)[0]


def last_kernel(flag, *refs):
    out, at = refs[-1], 0
    for value, other in zip(refs[:-1:2], refs[1:-1:2]):
        size = value.shape[0]
        out[at : at + size, :] = jnp.where(flag[0] == 1, other[...], value[...]).astype(out.dtype)
        at += size


def last_step(flag, *args, kind=LOW):
    rows, width = sum(value.shape[0] for value in args[::2]), args[0].shape[1]
    outs = [jax.ShapeDtypeStruct((rows, width), kind)]
    return run_kernel(last_kernel, outs, [flag, *args], rows * width, 1, last=kind == WIDE)[0]


def pack_kernel(*refs):
    out = refs[-1]
    for at, sums in enumerate(refs[:3]):
        out[2 * at : 2 * at + 2, :] = sums[:2, :]
    out[6:7, :] = refs[2][2:3, :]
    for at, sums in enumerate(refs[3:6]):
        out[7 + 2 * at : 9 + 2 * at, :] = sums[:2, :]
    out[13:14, :] = refs[5][2:3, :]


def pack_step(*sums):
    return run_kernel(pack_kernel, [wide(14, sums[0].shape[1])], sums, 1)[0]


def plus_kernel(left, right, out):
    out[...] = left[...] + right[...]


def plus_step(left, right):
    return run_kernel(plus_kernel, [wide(*left.shape)], [left, right], 1)[0]


def total_kernel(flag, enc_bias, dec_bias, part0, part1, mine, other):
    total = part0[...] + part1[...]
    here = flag[0] == 1
    mine[:7, :] = jnp.where(here, total[:7], total[7:])
    other[:7, :] = jnp.where(here, total[7:], total[:7])
    mine[7:, :] = jnp.where(here, enc_bias[...], dec_bias[...])
    other[7:, :] = jnp.where(here, dec_bias[...], enc_bias[...])


def total_step(flag, enc_bias, dec_bias, parts):
    rows, width = 7 + enc_bias.shape[0], enc_bias.shape[1]
    args = [flag, enc_bias, dec_bias, *parts]
    return run_kernel(total_kernel, [wide(rows, width)] * 2, args, 1, 1)


def self_final_kernel(first_flag, end_flag, value, other, lower, upper, w_in, w_out):
    half, split = lower.shape[0], w_in.shape[0]
    enc = jnp.where(end_flag[0] == 1, other[...], value[...])
    here = first_flag[0] == 1
    low_half = jnp.where(here, enc[:half], lower[...]).astype(WIDE)
    high_half = jnp.where(here, enc[half:], upper[...]).astype(WIDE)
    w_in[:half, :] = low_half
    w_in[half:, :] = high_half[: split - half]
    w_out[...] = high_half[split - half :]


def self_final_step(first_flag, end_flag, value, other, lower, upper, split):
    rows, width = value.shape
    args = [first_flag, end_flag, value, Far(other), lower, upper]
    return run_kernel(self_final_kernel, [wide(split, width), wide(rows - split, width)], args, 1, 2, last=True)


def scatter_kernel(flag, rows_in, keep, send):
    half = keep.shape[0]
    here = flag[0] == 1
    keep[...] = jnp.where(here, rows_in[:half, :], rows_in[half:, :])
    send[...] = jnp.where(here, rows_in[half:, :], rows_in[:half, :])


def scatter_step(flag, value):
    rows, width = value.shape
    return run_kernel(scatter_kernel, [low(rows // 2, width)] * 2, [flag, value], 1, 1)


def small_kernel(count, *refs):
    total = refs[0][...]
    for part in refs[1:count]:
        total = total + part[...]
    norm, up, down = refs[count:]
    for at in range(3):
        norm[at] = total[2 * at : 2 * at + 2, :]
    down[...] = total[6:7, :]
    up[...] = total[7:, :]


def small_step(parts):
    rows, width = parts[0].shape
    outs = [wide(3, 2, width), wide(rows - 7, width), wide(1, width)]
    return run_kernel(functools.partial(small_kernel, len(parts)), outs, parts, 1, last=True)


def out_kernel(places, cross, vec, *refs):
    parts, out = refs[:-1], refs[-1]
    size = out.shape[0]
    value = cross[...] + parts_sum(parts) + vec[6:7, :]
    keep = spots_of(places, size, size, 0) < places[3]
    out[...] = jnp.where(keep, value, 0.0).astype(LOW)


def out_step(places, cross, vec, parts):
    outs = [low(*cross.shape)]
    return run_kernel(out_kernel, outs, [places, cross, vec, *parts], 1, 1, last=True)[0]


def final_kernel(flag, first_value, second_value, out):
    out[...] = jnp.where(flag[0] == 1, first_value[...].astype(WIDE), second_value[...].astype(WIDE))


def final_step(flag, first_value, second_value):
    args = [flag, first_value, second_value]
    return run_kernel(final_kernel, [wide(*first_value.shape)], args, first_value.size, 1, last=True)[0]


def peers(slot):
    count = lax.axis_size("tensor")
    pairs = []
    for section in range(lax.axis_size("section")):
        mask = (0, 1 << section, 2 >> section, 3)[slot]
        pairs += [(section * count + at, section * count + (at ^ mask)) for at in range(count)]
    return pairs


def moved(value, slot):
    return lax.ppermute(value, ("section", "tensor"), peers(slot))


def tie(*values):
    return lax.optimization_barrier(values)


def send_rows(rows):
    far, near, side = (moved(rows, slot) for slot in (3, 1, 2))
    return [rows, near, side, far]


def send_sums(blocks):
    far, near, side = (moved(blocks[slot], slot) for slot in (3, 1, 2))
    return [blocks[0], near, side, far]


def near_rows(rows):
    return moved(rows, 1)


def far_rows(rows, near):
    return [rows, near, moved(stack_step(rows, near), 2)]


def far_sums(blocks):
    there = moved(blocks[2], 2)
    return add_step(blocks[1], there), [blocks[0], there]


def near_sums(onward, kept):
    return [*kept, moved(onward, 1)]


def swapped(value):
    return lax.ppermute(value, "section", [(0, 1), (1, 0)])


def body(
    enc_in, dec_in, lengths, enc_cot, dec_cot, norm_params, attn_in, attn_out, cross_proj, w_up, b_up, w_down, b_down
):
    own = lax.axis_index("section")
    part = lax.axis_index("tensor")
    dp_count = lax.axis_size("dp")
    dp_at = lax.axis_index("dp")
    first = own == 0
    width = enc_in.shape[3]
    enc_size = enc_in.shape[2]
    dec_size = dec_in.shape[2]
    heads_width = attn_out.shape[1]

    def own_clip(value):
        return lax.dynamic_index_in_dim(value[:, 0], own, 0, keepdims=False)

    def by_rows(value):
        return jnp.transpose(value[0], (1, 2, 0)).reshape(-1, width)

    frames, tokens, top_dec = own_clip(enc_in), own_clip(dec_in), own_clip(dec_cot)
    enc_parts = send_rows(frames)
    section = jnp.full((1,), own, jnp.int32)
    own_vec = jnp.concatenate([norm_params[0].reshape(6, width), b_down, b_up.reshape(-1, width)])

    def both(value, *after):
        value, *after = tie(value, *after)
        other = swapped(value)
        return [Pair(section, value, other, which) for which in (0, 1)], after

    (enc_vec, dec_vec), _ = both(own_vec)
    (enc_in_w, dec_in_w), _ = both(by_rows(attn_in))

    first_flag = first.astype(jnp.int32).reshape(1)

    at_end = (dp_at == 0) | (dp_at == 3)
    end_flag = at_end.astype(jnp.int32).reshape(1)

    def over_cores(first_value, second_value, pieces=1):
        other = swapped(pick_step(first_flag, second_value, first_value))
        return own_sum(first_flag, first_value, second_value, other, pieces)

    def hop(value, pairs, cores=(0, 1)):
        pairs = [(core * dp_count + a, core * dp_count + b) for core in cores for a, b in pairs]
        return lax.ppermute(value, ("section", "dp"), pairs)

    def outer_hop(inward=None, outward=None, cores=(0, 1)):
        if dp_count != 4:
            if outward is not None:
                outward[0] = lax.psum(outward[0], "dp")
                outward.append(outward[0])
            return
        pairs = [(0, 1), (3, 2)] * (inward is not None) + [(1, 0), (2, 3)] * (outward is not None)
        if inward is None or outward is None:
            value = (inward or outward)[0]
        else:
            value = pick_step(end_flag, inward[0], outward[0])
        other = hop(value, pairs, cores)
        if inward is not None:
            inward[0] = add_step(inward[0], other)
        if outward is not None:
            outward.append(other)

    def inner_hop(piece, cores=(0, 1)):
        if dp_count == 4:
            piece[0] = add_step(piece[0], hop(piece[0], [(1, 2), (2, 1)], cores))

    def pin(value, *pieces):
        value, found = tie(value, list(pieces))
        for piece, kept in zip(pieces, found):
            piece[:] = kept
        return value

    enc_parts[2], tokens = tie(enc_parts[2], tokens)
    near = near_rows(tokens)
    (enc_out_w, dec_out_w), _ = both(attn_out[0], tokens)
    enc_parts, near, lengths = tie(enc_parts, near, lengths)
    dec_parts = far_rows(tokens, near)
    length = lax.dynamic_index_in_dim(lengths, own, 0, keepdims=False)[0]
    places = jnp.stack([part, jnp.left_shift(1, own), jnp.right_shift(2, own), length, own]).astype(jnp.int32)
    enc_rows, enc_packed, enc_flat, enc_logs, *partial = self_step(enc_parts, Far(enc_vec), Far(enc_in_w), Far(enc_out_w))
    partial, dec_parts, places = tie(partial, dec_parts, places)
    parts = send_sums(partial)
    (enc_up_w, dec_up_w), _ = both(w_up[0], partial[0])
    (enc_down_w, dec_down_w), _ = both(w_down[0], partial[0])
    dec_rows, dec_packed, dec_flat, dec_logs, *dec_partial = self_step(
        dec_parts, Far(dec_vec), Far(dec_in_w), Far(dec_out_w), places
    )
    parts, dec_partial = tie(parts, dec_partial)
    enc_self, normed = after_step(frames, enc_vec, parts, 4)
    normed, dec_partial = tie(normed, dec_partial)
    parts = send_rows(normed)
    onward, kept = far_sums(dec_partial)
    (w_memory, w_cross), _ = both(by_rows(cross_proj), normed)
    w_query, w_back = w_cross.part(0, heads_width), w_cross.part(heads_width, 2 * heads_width)
    parts = tie(*parts)
    enc_ffn_rows, enc_active, enc_slope, *partial = ffn_step(parts, enc_up_w, enc_down_w, enc_vec)
    partial, onward, kept, top_dec = tie(partial, onward, kept, top_dec)
    parts = send_sums(partial)
    dec_parts = near_sums(onward, kept)
    near = near_rows(top_dec)
    parts, dec_parts, near = tie(parts, dec_parts, near)
    dec_self, dec_normed = after_step(tokens, dec_vec, dec_parts, 2)
    enc_final, normed, enc_low = after_step(enc_self, enc_vec, parts, 2, True)
    parts = send_rows(stack_step(normed, dec_normed))
    top_parts = far_rows(top_dec, near)
    parts = tie(*parts)
    post_rows, cross_rows, memory, queries, cross_flat, cross_logs, *partial = cross_step(
        parts, enc_size, w_memory, w_query, w_back
    )
    partial, top_parts = tie(partial, top_parts)
    parts = send_sums(partial)
    dec_cross, normed = after_step(dec_self, dec_vec, parts, 4)
    parts = send_rows(normed)
    dec_ffn_rows, top_rows, dec_active, dec_hidden, dec_bup, *partial = ffn_both_step(
        parts, top_parts, Far(dec_up_w), Far(dec_down_w), dec_vec, places
    )
    partial, dec_active, dec_hidden = tie(partial, dec_active, dec_hidden)
    parts = send_sums(partial)
    g_down = weight_grads(dec_active, top_rows)
    g_up = weight_grads(dec_ffn_rows, dec_hidden)
    parts, g_down, g_up = tie(parts, g_down, g_up)
    dec_grad, grad_low, dec_sums_ffn = back_step(dec_cross, dec_vec, top_dec, parts, 4, "masked", places)
    grad_low, dec_active, g_down, g_up = tie(grad_low, dec_active, g_down, g_up)
    parts = send_rows(grad_low)
    dec_near, dec_far = ([item] for item in over_cores(g_down, g_up, 2))
    out_partial = down_step(dec_active, Far(dec_down_w))
    parts, out_partial = pin((parts, out_partial), dec_near, dec_far)
    grad_rows, grad_query, grad_memory, *partial = cross_back_step(
        parts, w_memory, w_query, w_back, queries, memory, cross_logs
    )
    partial, grad_memory, grad_query, *dec_near = tie(partial, grad_memory, grad_query, *dec_near)
    parts = send_sums(partial)
    outer_hop(dec_near)
    g_cross = weight_grads(grad_query, cross_rows, cross_flat, grad_rows)
    parts, g_cross = pin((parts, g_cross), dec_near)
    enc_grad, dec_grad, grad_low, enc_sums_post, dec_sums_cross = joint_back_step(
        places, enc_final, enc_vec, enc_cot[:, 0], dec_self, dec_vec, dec_grad, parts
    )
    grad_low, grad_memory = tie(grad_low, grad_memory)
    grad_low = pin(grad_low, dec_near, dec_far)
    parts = send_rows(grad_low)
    outer_hop(dec_far)
    inner_hop(dec_near)
    g_memory = weight_grads(grad_memory, post_rows)
    parts, g_memory = pin((parts, g_memory), dec_near, dec_far)
    cross = list(over_cores(g_memory, g_cross))
    grad_rows, dec_grad_rows, enc_hidden, enc_bup, *partial = ffn_back_step(
        parts, enc_up_w, enc_down_w, enc_slope
    )
    partial, enc_hidden, grad_rows, dec_grad_rows = tie(partial, enc_hidden, grad_rows, dec_grad_rows)
    partial = pin(partial, dec_near, dec_far, cross)
    parts = send_sums(partial)
    outer_hop(cross, dec_near)
    inner_hop(dec_far)
    g_down = weight_grads(enc_active, grad_rows)
    g_up = weight_grads(enc_ffn_rows, enc_hidden)
    dec_grad_rows, dec_grad_packed, *dec_partial = self_back_step(
        [dec_grad_rows], dec_in_w, dec_out_w, dec_packed, dec_logs, places
    )
    parts, dec_partial, dec_grad_packed, g_down, g_up = pin(
        (parts, dec_partial, dec_grad_packed, g_down, g_up), cross, dec_near, dec_far
    )
    near_ffn, far_ffn = ([item] for item in over_cores(g_down, g_up, 2))
    enc_grad, grad_low, enc_sums_ffn = back_step(enc_self, enc_vec, enc_grad, parts, 4)
    grad_low, dec_partial, dec_grad_packed = tie(grad_low, dec_partial, dec_grad_packed)
    grad_low = pin(grad_low, near_ffn, far_ffn, cross, dec_far)
    parts = send_rows(grad_low)
    outer_hop(near_ffn, dec_far)
    inner_hop(cross)
    g_dec = weight_grads(dec_grad_packed, dec_rows, dec_flat, dec_grad_rows)
    parts, g_dec = pin((parts, g_dec), near_ffn, cross, dec_far)
    outer_hop(far_ffn, cross)
    inner_hop(near_ffn)
    dec_self_sum, dec_send = scatter_step(first_flag, g_dec)
    dec_self_sum = [add_step(dec_self_sum, swapped(dec_send))]
    out_onward, out_kept = far_sums(out_partial)
    enc_grad_rows, enc_grad_packed, *partial = self_back_step(parts, enc_in_w, enc_out_w, enc_packed, enc_logs)
    partial, enc_grad_packed, dec_partial, out_onward, out_kept = pin(
        (partial, enc_grad_packed, dec_partial, out_onward, out_kept), near_ffn, far_ffn, cross, dec_self_sum
    )
    g_enc = weight_grads(enc_grad_packed, enc_rows, enc_flat, enc_grad_rows)
    enc_self_sum = [add_step(g_enc, lax.ppermute(g_enc, "section", [(1, 0)]))]
    partial = pin(partial, enc_self_sum)
    parts = send_sums(partial)
    outer_hop(dec_self_sum, near_ffn)
    inner_hop(far_ffn)
    parts, dec_partial, out_onward, out_kept = pin(
        (parts, dec_partial, out_onward, out_kept), dec_self_sum, far_ffn, near_ffn, enc_self_sum
    )
    outer_hop(enc_self_sum, cores=(0,))
    outer_hop(None, far_ffn)
    inner_hop(dec_self_sum)
    onward, kept = far_sums(dec_partial)
    enc_in_grad, _, enc_sums_self = back_step(frames, enc_vec, enc_grad, parts, 0)
    enc_in_grad, onward, kept = tie(enc_in_grad, onward, kept)
    dec_parts = near_sums(onward, kept)
    out_parts = near_sums(out_onward, out_kept)
    dec_in_grad, _, dec_sums_self = back_step(tokens, dec_vec, dec_grad, dec_parts, 0)
    pack = pack_step(enc_sums_self, enc_sums_post, enc_sums_ffn, dec_sums_self, dec_sums_cross, dec_sums_ffn)
    pack, out_parts = pin((pack, out_parts), enc_self_sum, far_ffn, dec_self_sum)
    outer_hop(None, dec_self_sum)
    inner_hop(enc_self_sum, cores=(0,))
    pack = plus_step(pack, moved(pack, 1))
    pieces = [pack, moved(pack, 2)]
    mine, theirs = total_step(first_flag, enc_bup.reshape(-1, width), dec_bup.reshape(-1, width), pieces)
    mine = plus_step(mine, swapped(theirs))
    enc_ffn = last_step(end_flag, *near_ffn, *far_ffn)
    dec_ffn = last_step(end_flag, *dec_near, *dec_far)
    other_ffn = swapped(pick_step(first_flag, dec_ffn, enc_ffn))
    if dp_count != 4:
        small = [lax.psum(mine, "dp")]
    else:
        mine = plus_step(mine, lax.ppermute(mine, "dp", [(at, at ^ 1) for at in range(4)]))
        small = [mine, lax.ppermute(mine, "dp", [(at, at ^ 2) for at in range(4)])]
    small, out_parts = pin((small, out_parts), enc_self_sum, dec_self_sum)
    outer_hop(None, enc_self_sum, cores=(0,))
    dec_half = last_step(end_flag, *dec_self_sum)
    dec_lower = lax.ppermute(dec_half, "section", [(0, 1)])
    norm_grad, up_bias_grad, down_bias_grad = small_step(small)
    dec_out = out_step(places, dec_cross, dec_vec, out_parts)
    down_grad = final_step(first_flag, enc_ffn, other_ffn)
    up_grad = final_step(first_flag, other_ffn, dec_ffn)
    cross_grad = last_step(end_flag, *cross, kind=WIDE)
    dec_out, down_grad, up_grad, cross_grad, dec_lower = pin(
        (dec_out, down_grad, up_grad, cross_grad, dec_lower), enc_self_sum
    )
    in_grad, out_grad = self_final_step(
        first_flag, end_flag, *enc_self_sum, dec_lower, dec_half, 3 * heads_width
    )

    def by_columns(value, groups):
        return jnp.transpose(value.reshape(groups, -1, width), (2, 0, 1))[None]

    return (
        enc_low[None, None],
        dec_out[None, None],
        enc_in_grad[None, None],
        dec_in_grad[None, None],
        norm_grad[None],
        by_columns(in_grad, 3),
        out_grad[None],
        by_columns(cross_grad, 2),
        up_grad[None],
        up_bias_grad.reshape(1, -1),
        down_grad[None],
        down_bias_grad,
    )


def solution(mesh):
    placed = (
        P(None, "dp", "tensor", None),
        P(None, "dp", "tensor", None),
        P(None, "dp"),
        P(None, "dp", "tensor", None),
        P(None, "dp", "tensor", None),
        P("section", None, None, None),
        P("section", None, None, "tensor"),
        P("section", "tensor", None),
        P("section", None, None, "tensor"),
        P("section", None, "tensor"),
        P("section", "tensor"),
        P("section", "tensor", None),
        P("section", None),
    )
    return jax.shard_map(
        body,
        mesh=mesh,
        in_specs=placed,
        out_specs=(
            P("section", "dp", "tensor", None),
            P("section", "dp", "tensor", None),
            P("section", "dp", "tensor", None),
            P("section", "dp", "tensor", None),
            P("section", None, None, None),
            P("section", None, None, "tensor"),
            P("section", "tensor", None),
            P("section", None, None, "tensor"),
            P("section", None, "tensor"),
            P("section", "tensor"),
            P("section", "tensor", None),
            P("section", None),
        ),
        check_vma=False,
    )
```

```python
import functools

import jax
import jax.numpy as jnp
from jax import lax
from jax.experimental import pallas as pl
from jax.experimental.pallas import tpu as pltpu
from jax.sharding import PartitionSpec as P

HEAD_DIM = 64
SCALING = HEAD_DIM ** (-0.5)
EPSILON = 1e-05
NEG_FILL = -1e30
LOW = jnp.bfloat16
WIDE = jnp.float32
BESIDE = 20 * 10**9


def dot_nn(left, right):
    return jnp.dot(left, right, preferred_element_type=WIDE)


def dot_tn(left, right):
    return lax.dot_general(left, right, (((0,), (0,)), ((), ())), preferred_element_type=WIDE)


def dot_nt(left, right):
    return lax.dot_general(left, right, (((1,), (1,)), ((), ())), preferred_element_type=WIDE)


def low(*shape):
    return jax.ShapeDtypeStruct(shape, LOW)


def wide(*shape):
    return jax.ShapeDtypeStruct(shape, WIDE)


class Pair:
    def __init__(self, section, own, other, which, rows=None):
        self.section, self.own, self.other, self.which = section, own, other, which
        self.rows = rows or (0, own.shape[0])
        self.shape = (self.rows[1] - self.rows[0], own.shape[1])

    def part(self, start, stop):
        return Pair(self.section, self.own, self.other, self.which, (start, stop))


class Far:
    def __init__(self, item):
        self.item = item
        self.shape = item.shape

    def sources(self):
        return [self.item.own, self.item.other] if isinstance(self.item, Pair) else [self.item]

    def start(self, section, refs, scratch, sem):
        if not isinstance(self.item, Pair):
            copy = pltpu.make_async_copy(refs[0], scratch, sem)
            copy.start()
            return copy
        rows = pl.ds(self.item.rows[0], self.shape[0])
        copies = [pltpu.make_async_copy(ref.at[rows, :], scratch, sem) for ref in refs]
        pl.when(section[0] == self.item.which)(copies[0].start)
        pl.when(section[0] != self.item.which)(copies[1].start)
        return copies[0]


class Held:
    def __init__(self, ref, copy):
        self.ref, self.copy, self.shape, self.dtype = ref, copy, ref.shape, ref.dtype

    def __getitem__(self, index):
        if self.copy is not None:
            self.copy.wait()
            self.copy = None
        return self.ref[index]


class Sent:
    def __init__(self, ref, out, sem):
        self.ref, self.shape, self.dtype = ref, ref.shape, ref.dtype
        self.copy, self.started = pltpu.make_async_copy(ref, out, sem), False

    def __getitem__(self, index):
        return self.ref[index]

    def __setitem__(self, index, value):
        self.ref[index] = value

    def send(self):
        if not self.started:
            self.copy.start()
            self.started = True


def whole(*refs):
    for ref in refs:
        if isinstance(ref, Sent):
            ref.send()


class Chosen:
    def __init__(self, pair, section, own, other):
        self.mine, self.start, self.stop = section[0] == pair.which, *pair.rows
        self.own, self.other = own, other

    def __getitem__(self, index):
        if index is Ellipsis:
            index = (slice(self.start, self.stop), slice(None))
        return jnp.where(self.mine, self.own[index], self.other[index])


def run_kernel(kernel, outs, args, flops, scalars=0, beside=False, scratch=(), last=False):
    away, near = pl.BlockSpec(memory_space=pltpu.HBM), pl.BlockSpec(memory_space=pltpu.VMEM)
    smem = pl.BlockSpec(memory_space=pltpu.SMEM)
    coming = [item for item in args if isinstance(item, Far)]
    going = [item for item in outs if isinstance(item, Far)]
    outs = [(item.item, True) if isinstance(item, Far) else (item, False) for item in outs]
    pairs = [item.item if isinstance(item, Far) else item for item in args]
    pairs = [item for item in pairs if isinstance(item, Pair)]
    flat, specs = [item.section for item in pairs[:1]], [smem] * len(pairs[:1])
    for at, item in enumerate(args):
        kind, place = (away, pltpu.HBM) if isinstance(item, Far) else (near, pltpu.VMEM)
        sources = item.sources() if isinstance(item, Far) else [item]
        if isinstance(item, Pair):
            sources = [item.own, item.other]
        if isinstance(item, (Far, Pair)):
            sources = [pltpu.with_memory_space_constraint(one, place) for one in sources]
        flat += sources
        specs += [smem if at < scalars else kind] * len(sources)

    def body(*refs):
        given, refs = [], list(refs)
        section = refs.pop(0) if pairs else None
        sources = []
        for item in args:
            double = isinstance(item.item if isinstance(item, Far) else item, Pair)
            sources.append([refs.pop(0) for _ in range(1 + double)])
        results, refs = refs[: len(outs)], refs[len(outs) :]
        buffers, refs = refs[: len(coming)], refs[len(coming) :]
        staged, refs = refs[: len(going)], refs[len(going) :]
        sems = refs.pop(0) if coming or going else None
        at, sent = 0, []
        for item, found in zip(args, sources):
            if isinstance(item, Far):
                given.append(Held(buffers[at], item.start(section, found, buffers[at], sems.at[at])))
                at += 1
            else:
                given.append(Chosen(item, section, *found) if isinstance(item, Pair) else found[0])
        for index, (_, leaves) in enumerate(outs):
            if leaves:
                sent.append(Sent(staged[len(sent)], results[index], sems.at[len(coming) + len(sent)]))
                results[index] = sent[-1]
        kernel(*given, *results, *refs)
        whole(*sent)
        for item in given:
            if isinstance(item, Held) and item.copy is not None:
                item.copy.wait()
        for item in sent:
            item.copy.wait()

    moved_bytes = sum(item.size * item.dtype.itemsize for item in (*flat, *(item for item, _ in outs)))
    moves = len(coming) + len(going)
    return pl.pallas_call(
        body,
        out_shape=[
            pltpu.HBM(item.shape, item.dtype) if leaves else item if last else pltpu.VMEM(item.shape, item.dtype)
            for item, leaves in outs
        ],
        in_specs=specs,
        out_specs=[away if leaves else near for _, leaves in outs],
        scratch_shapes=[
            *[pltpu.VMEM(item.shape, item.sources()[0].dtype) for item in coming],
            *[pltpu.VMEM(item.shape, item.item.dtype) for item in going],
            *[pltpu.SemaphoreType.DMA((moves,))] * bool(moves),
            *[pltpu.VMEM(shape, LOW) for shape in scratch],
        ],
        cost_estimate=pl.CostEstimate(
            flops=BESIDE if beside else flops, bytes_accessed=moved_bytes, transcendentals=0
        ),
        compiler_params=pltpu.CompilerParams(vmem_limit_bytes=24 << 20),
    )(*flat)


def put_rows(parts, rows):
    at = 0
    for part in parts:
        rows[at : at + part.shape[0], :] = part[...]
        at += part.shape[0]


def put_partial(value, outs):
    at = 0
    for out in outs:
        out[...] = value[at : at + out.shape[0]].astype(out.dtype)
        at += out.shape[0]


def partial_outs(size, width, halves=False):
    return [wide(size, width), low(size, width)] + ([low(2 * size, width)] if halves else [low(size, width)] * 2)


def normalized(values):
    center = values - jnp.mean(values, axis=-1, keepdims=True)
    rate = lax.rsqrt(jnp.mean(center * center, axis=-1, keepdims=True) + EPSILON)
    return center * rate, rate


def parts_sum(parts):
    total = parts[0][...]
    for part in parts[1:]:
        total = total + part[: total.shape[0], :].astype(WIDE)
    return total


def gelu_both(value):
    size = jnp.abs(value) * 0.7071067811865476
    bell = jnp.exp(-size * size)
    inner = 1.0 / (1.0 + 0.3275911 * size)
    series = 1.061405429 * inner - 1.453152027
    series = series * inner + 1.421413741
    series = series * inner - 0.284496736
    series = series * inner + 0.254829592
    tail = 0.5 * series * inner * bell
    share = jnp.where(value >= 0, 1.0 - tail, tail)
    return value * share, share + value * (0.3989422804014327 * bell)


def allowed_pairs(places, size, rows):
    keys = spots_of(places, size, rows, 1)
    return (keys <= spots_of(places, size, rows, 0)) & (keys < places[3])


def scores_of(queries, keyset, allowed):
    scores = dot_nt(queries, keyset) * SCALING
    return scores if allowed is None else jnp.where(allowed, scores, NEG_FILL)


def attend(queries, keyset, valueset, allowed):
    scores = scores_of(queries, keyset, allowed)
    top = jnp.max(scores, axis=-1, keepdims=True)
    powers = jnp.exp(scores - top)
    total = jnp.sum(powers, axis=-1, keepdims=True)
    weights = (powers * (1.0 / total)).astype(LOW)
    return dot_nn(weights, valueset).astype(LOW), top + jnp.log(total)


def attend_back(queries, keyset, valueset, allowed, log_total, grad):
    shares = jnp.exp(scores_of(queries, keyset, allowed) - log_total)
    grad_weights = dot_nt(grad, valueset)
    along = jnp.sum(grad_weights * shares, axis=-1, keepdims=True)
    grad_scores = (shares * (grad_weights - along)).astype(LOW)
    grad_value = dot_tn(shares.astype(LOW), grad).astype(LOW)
    grad_query = (dot_nn(grad_scores, keyset) * SCALING).astype(LOW)
    grad_key = (dot_tn(grad_scores, queries) * SCALING).astype(LOW)
    return grad_query, grad_key, grad_value


def columns(block, head, width):
    start = block * width + head * HEAD_DIM
    return slice(start, start + HEAD_DIM)


def put_normed(parts, vec, rows):
    at = 0
    for part in parts:
        unit, _ = normalized(part[...].astype(WIDE))
        rows[at : at + part.shape[0], :] = (unit * vec[0:1, :] + vec[1:2, :]).astype(LOW)
        at += part.shape[0]


def spots_of(places, size, rows, axis):
    index = lax.broadcasted_iota(jnp.int32, (rows, 1) if axis == 0 else (1, rows), axis)
    slot = index // size
    mask = jnp.where(slot == 1, places[1], jnp.where(slot == 2, places[2], slot))
    return (places[0] ^ mask) * size + index - slot * size


def after_kernel(line, count, biased, residual, vec, *refs):
    value = residual[...].astype(WIDE) + parts_sum(refs[:count])
    after, normed = refs[count : count + 2]
    if biased:
        value = value + vec[6:7, :]
        refs[-1][...] = value.astype(LOW)
    after[...] = value
    unit, _ = normalized(value)
    normed[...] = (unit * vec[line : line + 1, :] + vec[line + 1 : line + 2, :]).astype(LOW)


def after_step(residual, vec, parts, line, biased=False):
    size, width = residual.shape
    outs = [wide(size, width), low(size, width)] + [low(size, width)] * biased
    kernel = functools.partial(after_kernel, line, len(parts), biased)
    return run_kernel(kernel, outs, [residual, vec, *parts], 20 * size * width)


def back_kernel(line, upper_kind, *refs):
    if upper_kind:
        places, refs = refs[0], refs[1:]
    (after, vec, upper), parts, (grad, grad_low, sums) = refs[:3], refs[3:-3], refs[-3:]
    above = (upper[places[4]] if upper_kind == "picked" else upper[...]).astype(WIDE)
    if upper_kind == "masked":
        size = above.shape[0]
        above = jnp.where(spots_of(places, size, size, 0) < places[3], above, 0.0)
    unit, rate = normalized(after[...].astype(WIDE))
    below = parts_sum(parts)
    scaled = below * vec[line : line + 1, :]
    along = jnp.mean(scaled * unit, axis=-1, keepdims=True)
    value = above + rate * (scaled - jnp.mean(scaled, axis=-1, keepdims=True) - unit * along)
    grad[...] = value
    grad_low[...] = value.astype(LOW)
    sums[0:1, :] = jnp.sum(below * unit, axis=0, keepdims=True)
    sums[1:2, :] = jnp.sum(below, axis=0, keepdims=True)
    sums[2:3, :] = jnp.sum(above, axis=0, keepdims=True)


def back_step(after, vec, upper, parts, line, upper_kind="", places=None):
    size, width = after.shape
    outs = [wide(size, width), low(size, width), wide(3, width)]
    args = [places] * bool(upper_kind) + [after, vec, upper, *parts]
    kernel = functools.partial(back_kernel, line, upper_kind)
    return run_kernel(kernel, outs, args, 30 * size * width, int(bool(upper_kind)), last=line == 0)


def joint_back_kernel(*refs):
    places, enc_after, enc_vec, top, dec_after, dec_vec, upper = refs[:7]
    parts, (enc_grad, dec_grad, both, enc_sums, dec_sums) = refs[7:11], refs[11:]
    size = enc_after.shape[0]
    below = parts_sum(parts)
    for after, vec, above, grad, sums, place in (
        (enc_after, enc_vec, top[places[4]].astype(WIDE), enc_grad, enc_sums, slice(None, size)),
        (dec_after, dec_vec, upper[...], dec_grad, dec_sums, slice(size, None)),
    ):
        unit, rate = normalized(after[...])
        lower = below[place]
        scaled = lower * vec[2:3, :]
        along = jnp.mean(scaled * unit, axis=-1, keepdims=True)
        value = above + rate * (scaled - jnp.mean(scaled, axis=-1, keepdims=True) - unit * along)
        grad[...] = value
        both[place, :] = value.astype(LOW)
        sums[0:1, :] = jnp.sum(lower * unit, axis=0, keepdims=True)
        sums[1:2, :] = jnp.sum(lower, axis=0, keepdims=True)


def joint_back_step(places, enc_after, enc_vec, top, dec_after, dec_vec, upper, parts):
    size, width = enc_after.shape
    other = dec_after.shape[0]
    outs = [wide(size, width), wide(other, width), low(size + other, width), wide(2, width), wide(2, width)]
    args = [places, enc_after, enc_vec, top, dec_after, dec_vec, upper, *parts]
    return run_kernel(joint_back_kernel, outs, args, 60 * size * width, 1)


def self_kernel(count, masked, *refs):
    if masked:
        places, refs = refs[0], refs[1:]
    parts, refs = refs[:count], refs[count:]
    (vec, w_in, w_out, rows, packed, flat, logs), outs = refs[:7], refs[7:]
    put_normed(parts, vec, rows)
    whole(rows)
    packed[...] = dot_nt(rows[...], w_in[...]).astype(LOW)
    whole(packed)
    allowed = allowed_pairs(places, rows.shape[0] // 4, rows.shape[0]) if masked else None
    width = flat.shape[1]
    for head in range(width // HEAD_DIM):
        q, k, v = (packed[:, columns(block, head, width)] for block in range(3))
        flat[:, columns(0, head, width)], logs[:, head : head + 1] = attend(q, k, v, allowed)
    whole(flat, logs)
    put_partial(dot_nn(flat[...], w_out[...]), outs)


def self_step(parts, vec, w_in, w_out, places=None):
    size, depth = parts[0].shape
    rows, width = 4 * size, w_out.shape[0]
    outs = [low(rows, depth), low(rows, 3 * width), low(rows, width), wide(rows, width // HEAD_DIM)]
    outs = [Far(item) for item in outs]
    masked = places is not None
    outs += partial_outs(size, depth, masked)
    flops = 8 * rows * depth * width + 4 * rows * rows * width
    args = [places] * masked + [*parts, vec, w_in, w_out]
    kernel = functools.partial(self_kernel, len(parts), masked)
    return run_kernel(kernel, outs, args, flops, int(masked), masked)


def self_back_kernel(count, masked, *refs):
    if masked:
        places, refs = refs[0], refs[1:]
    parts, refs = refs[:count], refs[count:]
    (w_in, w_out, packed, logs, rows, grad_packed), outs, grad_flat = refs[:6], refs[6:-1], refs[-1]
    put_rows(parts, rows)
    grad_flat[...] = dot_nt(rows[...], w_out[...]).astype(LOW)
    allowed = allowed_pairs(places, rows.shape[0] // 4, rows.shape[0]) if masked else None
    width = grad_flat.shape[1]
    for head in range(width // HEAD_DIM):
        q, k, v = (packed[:, columns(block, head, width)] for block in range(3))
        grads = attend_back(
            q, k, v, allowed, logs[:, head : head + 1], grad_flat[:, columns(0, head, width)]
        )
        for block in range(3):
            grad_packed[:, columns(block, head, width)] = grads[block]
    put_partial(dot_nn(grad_packed[...], w_in[...]), outs)


def self_back_step(parts, w_in, w_out, packed, logs, places=None):
    rows, (width, depth) = packed.shape[0], w_out.shape
    size = rows // 4
    masked = places is not None
    outs = [low(rows, depth), low(rows, 3 * width), *partial_outs(size, depth, masked)]
    flops = 8 * rows * depth * width + 10 * rows * rows * width
    args = [places] * masked + [*parts, w_in, w_out, packed, logs]
    kernel = functools.partial(self_back_kernel, len(parts), masked)
    return run_kernel(kernel, outs, args, flops, int(masked), masked, [(rows, width)])


def ffn_kernel(part0, part1, part2, part3, up, down, vec, rows, active, slope, *outs):
    put_rows((part0, part1, part2, part3), rows)
    value, slant = gelu_both(dot_nn(rows[...], up[...]) + vec[7:8, :])
    active[...] = value.astype(LOW)
    slope[...] = slant.astype(LOW)
    put_partial(dot_nn(active[...], down[...]), outs)


def ffn_step(parts, up, down, vec):
    size, depth = parts[0].shape
    rows, units = 4 * size, up.shape[1]
    outs = [low(rows, depth), low(rows, units), low(rows, units), *partial_outs(size, depth)]
    return run_kernel(ffn_kernel, outs, [*parts, up, down, vec], 4 * rows * depth * units)


def ffn_back_kernel(part0, part1, part2, part3, up, down, slope, rows, other_rows, grad_hidden, sums, *outs):
    put_joint((part0, part1, part2, part3), rows, other_rows)
    grad = (dot_nt(rows[...], down[...]) * slope[...].astype(WIDE)).astype(LOW)
    grad_hidden[...] = grad
    sums[...] = jnp.sum(grad.astype(WIDE), axis=0, keepdims=True)
    put_partial(dot_nt(grad_hidden[...], up[...]), outs)


def ffn_back_step(parts, up, down, slope):
    both, depth = parts[0].shape
    rows, units = slope.shape
    size = rows // 4
    outs = [low(rows, depth), low(4 * (both - size), depth), low(rows, units), wide(1, units)]
    outs += partial_outs(size, depth)
    return run_kernel(ffn_back_kernel, outs, [*parts, up, down, slope], 4 * rows * depth * units)


def ffn_both_kernel(count, *refs):
    places, parts, refs = refs[0], refs[1:5], refs[5:]
    grads, refs = refs[:count], refs[count:]
    (up, down, vec), (rows, grad_rows, active, grad_hidden, sums), outs = refs[:3], refs[3:8], refs[8:]
    put_rows(parts, rows)
    put_rows(grads, grad_rows)
    keep = spots_of(places, parts[0].shape[0], rows.shape[0], 0) < places[3]
    grad_rows[...] = jnp.where(keep, grad_rows[...].astype(WIDE), 0.0).astype(LOW)
    value, slant = gelu_both(dot_nn(rows[...], up[...]) + vec[7:8, :])
    active[...] = value.astype(LOW)
    grad = (dot_nt(grad_rows[...], down[...]) * slant).astype(LOW)
    grad_hidden[...] = grad
    sums[...] = jnp.sum(grad.astype(WIDE), axis=0, keepdims=True)
    put_partial(dot_nt(grad_hidden[...], up[...]), outs)


def ffn_both_step(parts, grads, up, down, vec, places):
    size, depth = parts[0].shape
    rows, units = 4 * size, up.shape[1]
    outs = [low(rows, depth)] * 2 + [low(rows, units)] * 2 + [wide(1, units)]
    args = [places, *parts, *grads, up, down, vec]
    kernel = functools.partial(ffn_both_kernel, len(grads))
    return run_kernel(kernel, outs + partial_outs(size, depth), args, 6 * rows * depth * units, 1)


def down_kernel(active, down, *outs):
    put_partial(dot_nn(active[...], down[...]), outs)


def down_step(active, down):
    rows, units = active.shape
    depth = down.shape[1]
    return run_kernel(
        down_kernel, partial_outs(rows // 4, depth, True), [active, down], 2 * rows * units * depth, beside=True
    )


def put_joint(parts, rows, other_rows):
    size = rows.shape[0] // 4
    other = other_rows.shape[0] // 4
    for slot, part in enumerate(parts):
        rows[slot * size : (slot + 1) * size, :] = part[:size, :]
        other_rows[slot * other : (slot + 1) * other, :] = part[size:, :]


def cross_kernel(*refs):
    parts, (w_memory, w_query, w_back) = refs[:4], refs[4:7]
    rows, query_rows, memory, queries, flat, logs = refs[7:13]
    put_joint(parts, rows, query_rows)
    queries[...] = dot_nt(query_rows[...], w_query[...]).astype(LOW)
    memory[...] = dot_nt(rows[...], w_memory[...]).astype(LOW)
    width = flat.shape[1]
    for head in range(width // HEAD_DIM):
        k, v = (memory[:, columns(block, head, width)] for block in range(2))
        own = columns(0, head, width)
        flat[:, own], logs[:, head : head + 1] = attend(queries[:, own], k, v, None)
    put_partial(dot_nn(flat[...], w_back[...]), refs[13:])


def cross_step(parts, size, w_memory, w_query, w_back):
    both, depth = parts[0].shape
    frames, rows, width = 4 * size, 4 * (both - size), w_query.shape[0]
    outs = [low(frames, depth), low(rows, depth), low(frames, 2 * width), low(rows, width), low(rows, width)]
    outs += [wide(rows, width // HEAD_DIM), *partial_outs(rows // 4, depth)]
    flops = 4 * frames * depth * width + 4 * frames * rows * width + 4 * rows * depth * width
    args = [*parts, w_memory, w_query, w_back]
    return run_kernel(cross_kernel, outs, args, flops)


def cross_back_kernel(*refs):
    parts, (w_memory, w_query, w_back, queries, memory, logs) = refs[:4], refs[4:10]
    (rows, grad_query, grad_memory), grad_flat = refs[10:13], refs[-1]
    put_rows(parts, rows)
    grad_flat[...] = dot_nt(rows[...], w_back[...]).astype(LOW)
    width = queries.shape[1]
    for head in range(width // HEAD_DIM):
        own = columns(0, head, width)
        k, v = (memory[:, columns(block, head, width)] for block in range(2))
        grads = attend_back(queries[:, own], k, v, None, logs[:, head : head + 1], grad_flat[:, own])
        grad_query[:, own] = grads[0]
        grad_memory[:, own] = grads[1]
        grad_memory[:, columns(1, head, width)] = grads[2]
    outs = refs[13:-1]
    size, other = memory.shape[0] // 4, queries.shape[0] // 4
    to_memory = dot_nn(grad_memory[...], w_memory[...])
    to_query = dot_nn(grad_query[...], w_query[...])
    for slot, out in enumerate(outs):
        out[:size, :] = to_memory[slot * size : (slot + 1) * size].astype(out.dtype)
        out[size:, :] = to_query[slot * other : (slot + 1) * other].astype(out.dtype)


def cross_back_step(parts, w_memory, w_query, w_back, queries, memory, logs):
    depth = parts[0].shape[1]
    rows, width = queries.shape
    frames = memory.shape[0]
    outs = [low(rows, depth), low(rows, width), low(frames, 2 * width)]
    outs += partial_outs((frames + rows) // 4, depth)
    flops = 4 * rows * depth * width + 10 * frames * rows * width + 4 * frames * depth * width
    args = [*parts, w_memory, w_query, w_back, queries, memory, logs]
    return run_kernel(cross_back_kernel, outs, args, flops, scratch=[(rows, width)])


def grads_kernel(pairs, *refs):
    out = refs[-1]
    at = 0
    if len(refs) > 2 * pairs + 1:
        at = refs[-2].shape[0]
        out[:at, :] = refs[-2][...]
    for pair in range(pairs):
        left, right = refs[2 * pair], refs[2 * pair + 1]
        size = left.shape[1]
        out[at : at + size, :] = dot_tn(left[...], right[...]).astype(LOW)
        at += size


def weight_grads(*args, under=None):
    depth = args[1].shape[1]
    total = sum(left.shape[1] for left in args[::2])
    flops = sum(2 * left.size * depth for left in args[::2])
    kernel = functools.partial(grads_kernel, len(args) // 2)
    if under is not None:
        total, args = total + under.shape[0], (*args, under)
    return run_kernel(kernel, [low(total, depth)], args, flops, beside=True)[0]


def add_kernel(left, right, out):
    size = out.shape[0]
    out[...] = (left[...].astype(WIDE) + right[-size:, :].astype(WIDE)).astype(out.dtype)


def add_step(left, right):
    return run_kernel(add_kernel, [low(*left.shape)], [left, right], left.size)[0]


def pick_kernel(flag, left, right, out):
    out[...] = jnp.where(flag[0] == 1, left[...], right[...])


def pick_step(flag, left, right):
    return run_kernel(pick_kernel, [low(*left.shape)], [flag, left, right], left.size, 1)[0]


def own_kernel(flag, first_value, second_value, other, *outs):
    at = 0
    for out in outs:
        place = slice(at, at + out.shape[0])
        mine = jnp.where(flag[0] == 1, first_value[place, :], second_value[place, :])
        out[...] = (mine.astype(WIDE) + other[place, :].astype(WIDE)).astype(LOW)
        at += out.shape[0]


def own_sum(flag, first_value, second_value, other, pieces):
    rows, width = other.shape
    outs = [low(rows // pieces, width)] * pieces
    return run_kernel(own_kernel, outs, [flag, first_value, second_value, other], other.size, 1)


def stack_kernel(*refs):
    put_rows(refs[:-1], refs[-1])


def stack_step(*parts):
    rows = sum(part.shape[0] for part in parts)
    return run_kernel(stack_kernel, [low(rows, parts[0].shape[1])], parts, rows)[0]


def last_kernel(flag, *refs):
    out, at = refs[-1], 0
    for value, other in zip(refs[:-1:2], refs[1:-1:2]):
        size = value.shape[0]
        out[at : at + size, :] = jnp.where(flag[0] == 1, other[...], value[...]).astype(out.dtype)
        at += size


def last_step(flag, *args, kind=LOW):
    rows, width = sum(value.shape[0] for value in args[::2]), args[0].shape[1]
    outs = [jax.ShapeDtypeStruct((rows, width), kind)]
    return run_kernel(last_kernel, outs, [flag, *args], rows * width, 1, last=kind == WIDE)[0]


def pack_kernel(*refs):
    out = refs[-1]
    for at, sums in enumerate(refs[:3]):
        out[2 * at : 2 * at + 2, :] = sums[:2, :]
    out[6:7, :] = refs[2][2:3, :]
    for at, sums in enumerate(refs[3:6]):
        out[7 + 2 * at : 9 + 2 * at, :] = sums[:2, :]
    out[13:14, :] = refs[5][2:3, :]


def pack_step(*sums):
    return run_kernel(pack_kernel, [wide(14, sums[0].shape[1])], sums, 1)[0]


def plus_kernel(left, right, out):
    out[...] = left[...] + right[...]


def plus_step(left, right):
    return run_kernel(plus_kernel, [wide(*left.shape)], [left, right], 1)[0]


def total_kernel(flag, enc_bias, dec_bias, part0, part1, part2, part3, mine, other):
    total = part0[...] + part1[...] + part2[...] + part3[...]
    here = flag[0] == 1
    mine[:7, :] = jnp.where(here, total[:7], total[7:])
    other[:7, :] = jnp.where(here, total[7:], total[:7])
    mine[7:, :] = jnp.where(here, enc_bias[...], dec_bias[...])
    other[7:, :] = jnp.where(here, dec_bias[...], enc_bias[...])


def total_step(flag, enc_bias, dec_bias, parts):
    rows, width = 7 + enc_bias.shape[0], enc_bias.shape[1]
    args = [flag, enc_bias, dec_bias, *parts]
    return run_kernel(total_kernel, [wide(rows, width)] * 2, args, 1, 1)


def self_final_kernel(first_flag, end_flag, value, other, lower, upper, w_in, w_out):
    half, split = lower.shape[0], w_in.shape[0]
    enc = jnp.where(end_flag[0] == 1, other[...], value[...])
    here = first_flag[0] == 1
    low_half = jnp.where(here, enc[:half], lower[...]).astype(WIDE)
    high_half = jnp.where(here, enc[half:], upper[...]).astype(WIDE)
    w_in[:half, :] = low_half
    w_in[half:, :] = high_half[: split - half]
    w_out[...] = high_half[split - half :]


def self_final_step(first_flag, end_flag, value, other, lower, upper, split):
    rows, width = value.shape
    args = [first_flag, end_flag, value, other, lower, upper]
    return run_kernel(self_final_kernel, [wide(split, width), wide(rows - split, width)], args, 1, 2, last=True)


def scatter_kernel(flag, rows_in, keep, send):
    half = keep.shape[0]
    here = flag[0] == 1
    keep[...] = jnp.where(here, rows_in[:half, :], rows_in[half:, :])
    send[...] = jnp.where(here, rows_in[half:, :], rows_in[:half, :])


def scatter_step(flag, value):
    rows, width = value.shape
    return run_kernel(scatter_kernel, [low(rows // 2, width)] * 2, [flag, value], 1, 1)


def small_kernel(count, *refs):
    total = refs[0][...]
    for part in refs[1:count]:
        total = total + part[...]
    norm, up, down = refs[count:]
    for at in range(3):
        norm[at] = total[2 * at : 2 * at + 2, :]
    down[...] = total[6:7, :]
    up[...] = total[7:, :]


def small_step(parts):
    rows, width = parts[0].shape
    outs = [wide(3, 2, width), wide(rows - 7, width), wide(1, width)]
    return run_kernel(functools.partial(small_kernel, len(parts)), outs, parts, 1, last=True)


def out_kernel(places, cross, vec, *refs):
    parts, out = refs[:-1], refs[-1]
    size = out.shape[0]
    value = cross[...] + parts_sum(parts) + vec[6:7, :]
    keep = spots_of(places, size, size, 0) < places[3]
    out[...] = jnp.where(keep, value, 0.0).astype(LOW)


def out_step(places, cross, vec, parts):
    outs = [low(*cross.shape)]
    return run_kernel(out_kernel, outs, [places, cross, vec, *parts], 1, 1, last=True)[0]


def final_kernel(flag, first_value, second_value, out):
    out[...] = jnp.where(flag[0] == 1, first_value[...].astype(WIDE), second_value[...].astype(WIDE))


def final_step(flag, first_value, second_value):
    args = [flag, first_value, second_value]
    return run_kernel(final_kernel, [wide(*first_value.shape)], args, first_value.size, 1, last=True)[0]


def peers(slot):
    count = lax.axis_size("tensor")
    pairs = []
    for section in range(lax.axis_size("section")):
        mask = (0, 1 << section, 2 >> section, 3)[slot]
        pairs += [(section * count + at, section * count + (at ^ mask)) for at in range(count)]
    return pairs


def moved(value, slot):
    return lax.ppermute(value, ("section", "tensor"), peers(slot))


def tie(*values):
    return lax.optimization_barrier(values)


def send_rows(rows):
    far, near, side = (moved(rows, slot) for slot in (3, 1, 2))
    return [rows, near, side, far]


def send_sums(blocks):
    far, near, side = (moved(blocks[slot], slot) for slot in (3, 1, 2))
    return [blocks[0], near, side, far]


def near_rows(rows):
    return moved(rows, 1)


def far_rows(rows, near):
    return [rows, near, moved(stack_step(rows, near), 2)]


def far_sums(blocks):
    there = moved(blocks[2], 2)
    return add_step(blocks[1], there), [blocks[0], there]


def near_sums(onward, kept):
    return [*kept, moved(onward, 1)]


def swapped(value):
    return lax.ppermute(value, "section", [(0, 1), (1, 0)])


def body(
    enc_in, dec_in, lengths, enc_cot, dec_cot, norm_params, attn_in, attn_out, cross_proj, w_up, b_up, w_down, b_down
):
    own = lax.axis_index("section")
    part = lax.axis_index("tensor")
    dp_count = lax.axis_size("dp")
    dp_at = lax.axis_index("dp")
    first = own == 0
    width = enc_in.shape[3]
    enc_size = enc_in.shape[2]
    dec_size = dec_in.shape[2]
    heads_width = attn_out.shape[1]

    def own_clip(value):
        return lax.dynamic_index_in_dim(value[:, 0], own, 0, keepdims=False)

    def by_rows(value):
        return jnp.transpose(value[0], (1, 2, 0)).reshape(-1, width)

    frames, tokens, top_dec = own_clip(enc_in), own_clip(dec_in), own_clip(dec_cot)
    enc_parts = send_rows(frames)
    section = jnp.full((1,), own, jnp.int32)
    own_vec = jnp.concatenate([norm_params[0].reshape(6, width), b_down, b_up.reshape(-1, width)])

    def both(value, *after):
        sent, *after = tie(value, *after)
        other = swapped(sent)
        return [Pair(section, value, other, which) for which in (0, 1)], after

    (enc_vec, dec_vec), _ = both(own_vec)
    (enc_in_w, dec_in_w), _ = both(by_rows(attn_in))

    first_flag = first.astype(jnp.int32).reshape(1)

    at_end = (dp_at == 0) | (dp_at == 3)
    end_flag = at_end.astype(jnp.int32).reshape(1)

    def over_cores(first_value, second_value, pieces=1):
        other = swapped(pick_step(first_flag, second_value, first_value))
        return own_sum(first_flag, first_value, second_value, other, pieces)

    def hop(value, pairs, cores=(0, 1)):
        pairs = [(core * dp_count + a, core * dp_count + b) for core in cores for a, b in pairs]
        return lax.ppermute(value, ("section", "dp"), pairs)

    def outer_hop(inward=None, outward=None, cores=(0, 1)):
        if dp_count != 4:
            if outward is not None:
                outward[0] = lax.psum(outward[0], "dp")
                outward.append(outward[0])
            return
        pairs = [(0, 1), (3, 2)] * (inward is not None) + [(1, 0), (2, 3)] * (outward is not None)
        if inward is None or outward is None:
            value = (inward or outward)[0]
        else:
            value = pick_step(end_flag, inward[0], outward[0])
        other = hop(value, pairs, cores)
        if inward is not None:
            inward[0] = add_step(inward[0], other)
        if outward is not None:
            outward.append(other)

    def inner_hop(piece, cores=(0, 1)):
        if dp_count == 4:
            piece[0] = add_step(piece[0], hop(piece[0], [(1, 2), (2, 1)], cores))

    def pin(value, *pieces):
        value, found = tie(value, list(pieces))
        for piece, kept in zip(pieces, found):
            piece[:] = kept
        return value

    enc_parts[1], enc_parts[2], tokens = tie(enc_parts[1], enc_parts[2], tokens)
    near = near_rows(tokens)
    (enc_out_w, dec_out_w), _ = both(attn_out[0], tokens)
    enc_parts, near = tie(enc_parts, near)
    dec_parts = far_rows(tokens, near)
    length = lax.dynamic_index_in_dim(lengths, own, 0, keepdims=False)[0]
    places = jnp.stack([part, jnp.left_shift(1, own), jnp.right_shift(2, own), length, own]).astype(jnp.int32)
    enc_rows, enc_packed, enc_flat, enc_logs, *partial = self_step(enc_parts, Far(enc_vec), Far(enc_in_w), Far(enc_out_w))
    partial, dec_parts, places = tie(partial, dec_parts, places)
    parts = send_sums(partial)
    (enc_up_w, dec_up_w), _ = both(w_up[0], partial[0])
    (enc_down_w, dec_down_w), _ = both(w_down[0], partial[0])
    dec_rows, dec_packed, dec_flat, dec_logs, *dec_partial = self_step(
        dec_parts, Far(dec_vec), Far(dec_in_w), Far(dec_out_w), places
    )
    parts, dec_partial = tie(parts, dec_partial)
    enc_self, normed = after_step(frames, enc_vec, parts, 4)
    normed, dec_partial = tie(normed, dec_partial)
    parts = send_rows(normed)
    onward, kept = far_sums(dec_partial)
    (w_memory, w_cross), _ = both(by_rows(cross_proj), normed)
    w_query, w_back = w_cross.part(0, heads_width), w_cross.part(heads_width, 2 * heads_width)
    parts = tie(*parts)
    enc_ffn_rows, enc_active, enc_slope, *partial = ffn_step(parts, enc_up_w, enc_down_w, enc_vec)
    partial, onward, kept, top_dec = tie(partial, onward, kept, top_dec)
    parts = send_sums(partial)
    dec_parts = near_sums(onward, kept)
    near = near_rows(top_dec)
    parts, dec_parts, near = tie(parts, dec_parts, near)
    dec_self, dec_normed = after_step(tokens, dec_vec, dec_parts, 2)
    enc_final, normed, enc_low = after_step(enc_self, enc_vec, parts, 2, True)
    parts = send_rows(stack_step(normed, dec_normed))
    top_parts = far_rows(top_dec, near)
    parts = tie(*parts)
    post_rows, cross_rows, memory, queries, cross_flat, cross_logs, *partial = cross_step(
        parts, enc_size, w_memory, w_query, w_back
    )
    partial, top_parts = tie(partial, top_parts)
    parts = send_sums(partial)
    dec_cross, normed = after_step(dec_self, dec_vec, parts, 4)
    parts = send_rows(normed)
    dec_ffn_rows, top_rows, dec_active, dec_hidden, dec_bup, *partial = ffn_both_step(
        parts, top_parts, Far(dec_up_w), Far(dec_down_w), dec_vec, places
    )
    partial, dec_active, dec_hidden = tie(partial, dec_active, dec_hidden)
    parts = send_sums(partial)
    g_down = weight_grads(dec_active, top_rows)
    g_up = weight_grads(dec_ffn_rows, dec_hidden)
    parts, g_down, g_up = tie(parts, g_down, g_up)
    dec_grad, grad_low, dec_sums_ffn = back_step(dec_cross, dec_vec, top_dec, parts, 4, "masked", places)
    grad_low, dec_active, g_down, g_up = tie(grad_low, dec_active, g_down, g_up)
    parts = send_rows(grad_low)
    dec_near, dec_far = ([item] for item in over_cores(g_down, g_up, 2))
    out_partial = down_step(dec_active, Far(dec_down_w))
    parts, out_partial = pin((parts, out_partial), dec_near, dec_far)
    grad_rows, grad_query, grad_memory, *partial = cross_back_step(
        parts, w_memory, w_query, w_back, queries, memory, cross_logs
    )
    partial, grad_memory, grad_query, *dec_near = tie(partial, grad_memory, grad_query, *dec_near)
    parts = send_sums(partial)
    outer_hop(dec_near)
    g_cross = weight_grads(grad_query, cross_rows, cross_flat, grad_rows)
    parts, g_cross = pin((parts, g_cross), dec_near)
    enc_grad, dec_grad, grad_low, enc_sums_post, dec_sums_cross = joint_back_step(
        places, enc_final, enc_vec, enc_cot[:, 0], dec_self, dec_vec, dec_grad, parts
    )
    grad_low, grad_memory = tie(grad_low, grad_memory)
    grad_low = pin(grad_low, dec_near, dec_far)
    parts = send_rows(grad_low)
    outer_hop(dec_far)
    inner_hop(dec_near)
    g_memory = weight_grads(grad_memory, post_rows)
    parts, g_memory = pin((parts, g_memory), dec_near, dec_far)
    cross = list(over_cores(g_memory, g_cross))
    grad_rows, dec_grad_rows, enc_hidden, enc_bup, *partial = ffn_back_step(
        parts, enc_up_w, enc_down_w, enc_slope
    )
    partial, enc_hidden, grad_rows, dec_grad_rows = tie(partial, enc_hidden, grad_rows, dec_grad_rows)
    partial = pin(partial, dec_near, dec_far, cross)
    parts = send_sums(partial)
    outer_hop(cross, dec_near)
    inner_hop(dec_far)
    g_down = weight_grads(enc_active, grad_rows)
    g_up = weight_grads(enc_ffn_rows, enc_hidden)
    dec_grad_rows, dec_grad_packed, *dec_partial = self_back_step(
        [dec_grad_rows], dec_in_w, dec_out_w, dec_packed, dec_logs, places
    )
    parts, dec_partial, dec_grad_packed, g_down, g_up = pin(
        (parts, dec_partial, dec_grad_packed, g_down, g_up), cross, dec_near, dec_far
    )
    near_ffn, far_ffn = ([item] for item in over_cores(g_down, g_up, 2))
    enc_grad, grad_low, enc_sums_ffn = back_step(enc_self, enc_vec, enc_grad, parts, 4)
    grad_low, dec_partial, dec_grad_packed = tie(grad_low, dec_partial, dec_grad_packed)
    grad_low = pin(grad_low, near_ffn, far_ffn, cross, dec_far)
    parts = send_rows(grad_low)
    outer_hop(near_ffn, dec_far)
    inner_hop(cross)
    g_dec = weight_grads(dec_grad_packed, dec_rows, dec_flat, dec_grad_rows)
    parts, g_dec = pin((parts, g_dec), near_ffn, cross, dec_far)
    outer_hop(far_ffn, cross)
    inner_hop(near_ffn)
    dec_self_sum, dec_send = scatter_step(first_flag, g_dec)
    dec_self_sum = [add_step(dec_self_sum, swapped(dec_send))]
    out_onward, out_kept = far_sums(out_partial)
    enc_grad_rows, enc_grad_packed, *partial = self_back_step(parts, enc_in_w, enc_out_w, enc_packed, enc_logs)
    partial, enc_grad_packed, dec_partial, out_onward, out_kept = pin(
        (partial, enc_grad_packed, dec_partial, out_onward, out_kept), near_ffn, far_ffn, cross, dec_self_sum
    )
    g_enc = weight_grads(enc_grad_packed, enc_rows, enc_flat, enc_grad_rows)
    enc_self_sum = [add_step(g_enc, lax.ppermute(g_enc, "section", [(1, 0)]))]
    partial = pin(partial, enc_self_sum)
    parts = send_sums(partial)
    outer_hop(dec_self_sum, near_ffn)
    inner_hop(far_ffn)
    parts, dec_partial, out_onward, out_kept = pin(
        (parts, dec_partial, out_onward, out_kept), dec_self_sum, far_ffn, near_ffn, enc_self_sum
    )
    outer_hop(enc_self_sum, cores=(0,))
    outer_hop(None, far_ffn)
    inner_hop(dec_self_sum)
    onward, kept = far_sums(dec_partial)
    enc_in_grad, _, enc_sums_self = back_step(frames, enc_vec, enc_grad, parts, 0)
    enc_in_grad, onward, kept = tie(enc_in_grad, onward, kept)
    dec_parts = near_sums(onward, kept)
    out_parts = near_sums(out_onward, out_kept)
    dec_in_grad, _, dec_sums_self = back_step(tokens, dec_vec, dec_grad, dec_parts, 0)
    pack = pack_step(enc_sums_self, enc_sums_post, enc_sums_ffn, dec_sums_self, dec_sums_cross, dec_sums_ffn)
    pack, out_parts = pin((pack, out_parts), enc_self_sum, far_ffn, dec_self_sum)
    outer_hop(None, dec_self_sum)
    inner_hop(enc_self_sum, cores=(0,))
    pieces = [pack, moved(pack, 1), moved(pack, 2), moved(pack, 3)]
    mine, theirs = total_step(first_flag, enc_bup.reshape(-1, width), dec_bup.reshape(-1, width), pieces)
    mine = plus_step(mine, swapped(theirs))
    enc_ffn = last_step(end_flag, *near_ffn, *far_ffn)
    dec_ffn = last_step(end_flag, *dec_near, *dec_far)
    other_ffn = swapped(pick_step(first_flag, dec_ffn, enc_ffn))
    if dp_count != 4:
        small = [lax.psum(mine, "dp")]
    else:
        mine = plus_step(mine, lax.ppermute(mine, "dp", [(at, at ^ 1) for at in range(4)]))
        small = [mine, lax.ppermute(mine, "dp", [(at, at ^ 2) for at in range(4)])]
    small, out_parts = pin((small, out_parts), enc_self_sum, dec_self_sum)
    outer_hop(None, enc_self_sum, cores=(0,))
    dec_half = last_step(end_flag, *dec_self_sum)
    dec_lower = lax.ppermute(dec_half, "section", [(0, 1)])
    norm_grad, up_bias_grad, down_bias_grad = small_step(small)
    dec_out = out_step(places, dec_cross, dec_vec, out_parts)
    down_grad = final_step(first_flag, enc_ffn, other_ffn)
    up_grad = final_step(first_flag, other_ffn, dec_ffn)
    cross_grad = last_step(end_flag, *cross, kind=WIDE)
    dec_out, down_grad, up_grad, cross_grad, dec_lower = pin(
        (dec_out, down_grad, up_grad, cross_grad, dec_lower), enc_self_sum
    )
    in_grad, out_grad = self_final_step(
        first_flag, end_flag, *enc_self_sum, dec_lower, dec_half, 3 * heads_width
    )

    def by_columns(value, groups):
        return jnp.transpose(value.reshape(groups, -1, width), (2, 0, 1))[None]

    return (
        enc_low[None, None],
        dec_out[None, None],
        enc_in_grad[None, None],
        dec_in_grad[None, None],
        norm_grad[None],
        by_columns(in_grad, 3),
        out_grad[None],
        by_columns(cross_grad, 2),
        up_grad[None],
        up_bias_grad.reshape(1, -1),
        down_grad[None],
        down_bias_grad,
    )


def solution(mesh):
    placed = (
        P(None, "dp", "tensor", None),
        P(None, "dp", "tensor", None),
        P(None, "dp"),
        P(None, "dp", "tensor", None),
        P(None, "dp", "tensor", None),
        P("section", None, None, None),
        P("section", None, None, "tensor"),
        P("section", "tensor", None),
        P("section", None, None, "tensor"),
        P("section", None, "tensor"),
        P("section", "tensor"),
        P("section", "tensor", None),
        P("section", None),
    )
    return jax.shard_map(
        body,
        mesh=mesh,
        in_specs=placed,
        out_specs=(
            P("section", "dp", "tensor", None),
            P("section", "dp", "tensor", None),
            P("section", "dp", "tensor", None),
            P("section", "dp", "tensor", None),
            P("section", None, None, None),
            P("section", None, None, "tensor"),
            P("section", "tensor", None),
            P("section", None, None, "tensor"),
            P("section", None, "tensor"),
            P("section", "tensor"),
            P("section", "tensor", None),
            P("section", None),
        ),
        check_vma=False,
    )
```

```python
import functools

import jax
import jax.numpy as jnp
from jax import lax
from jax.experimental import pallas as pl
from jax.experimental.pallas import tpu as pltpu
from jax.sharding import PartitionSpec as P

HEAD_DIM = 64
SCALING = HEAD_DIM ** (-0.5)
EPSILON = 1e-05
NEG_FILL = -1e30
LOW = jnp.bfloat16
WIDE = jnp.float32
BESIDE = 20 * 10**9


def dot_nn(left, right):
    return jnp.dot(left, right, preferred_element_type=WIDE)


def dot_tn(left, right):
    return lax.dot_general(left, right, (((0,), (0,)), ((), ())), preferred_element_type=WIDE)


def dot_nt(left, right):
    return lax.dot_general(left, right, (((1,), (1,)), ((), ())), preferred_element_type=WIDE)


def low(*shape):
    return jax.ShapeDtypeStruct(shape, LOW)


def wide(*shape):
    return jax.ShapeDtypeStruct(shape, WIDE)


class Pair:
    def __init__(self, section, own, other, which, rows=None):
        self.section, self.own, self.other, self.which = section, own, other, which
        self.rows = rows or (0, own.shape[0])
        self.shape = (self.rows[1] - self.rows[0], own.shape[1])

    def part(self, start, stop):
        return Pair(self.section, self.own, self.other, self.which, (start, stop))


class Far:
    def __init__(self, item):
        self.item = item
        self.shape = item.shape

    def sources(self):
        return [self.item.own, self.item.other] if isinstance(self.item, Pair) else [self.item]

    def start(self, section, refs, scratch, sem):
        if not isinstance(self.item, Pair):
            copy = pltpu.make_async_copy(refs[0], scratch, sem)
            copy.start()
            return copy
        rows = pl.ds(self.item.rows[0], self.shape[0])
        copies = [pltpu.make_async_copy(ref.at[rows, :], scratch, sem) for ref in refs]
        pl.when(section[0] == self.item.which)(copies[0].start)
        pl.when(section[0] != self.item.which)(copies[1].start)
        return copies[0]


class Held:
    def __init__(self, ref, copy):
        self.ref, self.copy, self.shape, self.dtype = ref, copy, ref.shape, ref.dtype

    def __getitem__(self, index):
        if self.copy is not None:
            self.copy.wait()
            self.copy = None
        return self.ref[index]


class Sent:
    def __init__(self, ref, out, sem):
        self.ref, self.shape, self.dtype = ref, ref.shape, ref.dtype
        self.copy, self.started = pltpu.make_async_copy(ref, out, sem), False

    def __getitem__(self, index):
        return self.ref[index]

    def __setitem__(self, index, value):
        self.ref[index] = value

    def send(self):
        if not self.started:
            self.copy.start()
            self.started = True


def whole(*refs):
    for ref in refs:
        if isinstance(ref, Sent):
            ref.send()


class Chosen:
    def __init__(self, pair, section, own, other):
        self.mine, self.start, self.stop = section[0] == pair.which, *pair.rows
        self.own, self.other = own, other

    def __getitem__(self, index):
        if index is Ellipsis:
            index = (slice(self.start, self.stop), slice(None))
        return jnp.where(self.mine, self.own[index], self.other[index])


def run_kernel(kernel, outs, args, flops, scalars=0, beside=False, scratch=(), last=False):
    away, near = pl.BlockSpec(memory_space=pltpu.HBM), pl.BlockSpec(memory_space=pltpu.VMEM)
    smem = pl.BlockSpec(memory_space=pltpu.SMEM)
    coming = [item for item in args if isinstance(item, Far)]
    going = [item for item in outs if isinstance(item, Far)]
    outs = [(item.item, True) if isinstance(item, Far) else (item, False) for item in outs]
    pairs = [item.item if isinstance(item, Far) else item for item in args]
    pairs = [item for item in pairs if isinstance(item, Pair)]
    flat, specs = [item.section for item in pairs[:1]], [smem] * len(pairs[:1])
    for at, item in enumerate(args):
        kind, place = (away, pltpu.HBM) if isinstance(item, Far) else (near, pltpu.VMEM)
        sources = item.sources() if isinstance(item, Far) else [item]
        if isinstance(item, Pair):
            sources = [item.own, item.other]
        if isinstance(item, (Far, Pair)):
            sources = [pltpu.with_memory_space_constraint(one, place) for one in sources]
        flat += sources
        specs += [smem if at < scalars else kind] * len(sources)

    def body(*refs):
        given, refs = [], list(refs)
        section = refs.pop(0) if pairs else None
        sources = []
        for item in args:
            double = isinstance(item.item if isinstance(item, Far) else item, Pair)
            sources.append([refs.pop(0) for _ in range(1 + double)])
        results, refs = refs[: len(outs)], refs[len(outs) :]
        buffers, refs = refs[: len(coming)], refs[len(coming) :]
        staged, refs = refs[: len(going)], refs[len(going) :]
        sems = refs.pop(0) if coming or going else None
        at, sent = 0, []
        for item, found in zip(args, sources):
            if isinstance(item, Far):
                given.append(Held(buffers[at], item.start(section, found, buffers[at], sems.at[at])))
                at += 1
            else:
                given.append(Chosen(item, section, *found) if isinstance(item, Pair) else found[0])
        for index, (_, leaves) in enumerate(outs):
            if leaves:
                sent.append(Sent(staged[len(sent)], results[index], sems.at[len(coming) + len(sent)]))
                results[index] = sent[-1]
        kernel(*given, *results, *refs)
        whole(*sent)
        for item in given:
            if isinstance(item, Held) and item.copy is not None:
                item.copy.wait()
        for item in sent:
            item.copy.wait()

    moved_bytes = sum(item.size * item.dtype.itemsize for item in (*flat, *(item for item, _ in outs)))
    moves = len(coming) + len(going)
    return pl.pallas_call(
        body,
        out_shape=[
            pltpu.HBM(item.shape, item.dtype) if leaves else item if last else pltpu.VMEM(item.shape, item.dtype)
            for item, leaves in outs
        ],
        in_specs=specs,
        out_specs=[away if leaves else near for _, leaves in outs],
        scratch_shapes=[
            *[pltpu.VMEM(item.shape, item.sources()[0].dtype) for item in coming],
            *[pltpu.VMEM(item.shape, item.item.dtype) for item in going],
            *[pltpu.SemaphoreType.DMA((moves,))] * bool(moves),
            *[pltpu.VMEM(shape, LOW) for shape in scratch],
        ],
        cost_estimate=pl.CostEstimate(
            flops=BESIDE if beside else flops, bytes_accessed=moved_bytes, transcendentals=0
        ),
        compiler_params=pltpu.CompilerParams(vmem_limit_bytes=24 << 20),
    )(*flat)


def put_rows(parts, rows):
    at = 0
    for part in parts:
        rows[at : at + part.shape[0], :] = part[...]
        at += part.shape[0]


def put_partial(value, outs):
    at = 0
    for out in outs:
        out[...] = value[at : at + out.shape[0]].astype(out.dtype)
        at += out.shape[0]


def partial_outs(size, width, halves=False):
    return [wide(size, width), low(size, width)] + ([low(2 * size, width)] if halves else [low(size, width)] * 2)


def normalized(values):
    center = values - jnp.mean(values, axis=-1, keepdims=True)
    rate = lax.rsqrt(jnp.mean(center * center, axis=-1, keepdims=True) + EPSILON)
    return center * rate, rate


def parts_sum(parts):
    total = parts[0][...]
    for part in parts[1:]:
        total = total + part[: total.shape[0], :].astype(WIDE)
    return total


def gelu_both(value):
    size = jnp.abs(value) * 0.7071067811865476
    bell = jnp.exp(-size * size)
    inner = 1.0 / (1.0 + 0.3275911 * size)
    series = 1.061405429 * inner - 1.453152027
    series = series * inner + 1.421413741
    series = series * inner - 0.284496736
    series = series * inner + 0.254829592
    tail = 0.5 * series * inner * bell
    share = jnp.where(value >= 0, 1.0 - tail, tail)
    return value * share, share + value * (0.3989422804014327 * bell)


def allowed_pairs(places, size, rows):
    keys = spots_of(places, size, rows, 1)
    return (keys <= spots_of(places, size, rows, 0)) & (keys < places[3])


def scores_of(queries, keyset, allowed):
    scores = dot_nt(queries, keyset) * SCALING
    return scores if allowed is None else jnp.where(allowed, scores, NEG_FILL)


def attend(queries, keyset, valueset, allowed):
    scores = scores_of(queries, keyset, allowed)
    top = jnp.max(scores, axis=-1, keepdims=True)
    powers = jnp.exp(scores - top)
    total = jnp.sum(powers, axis=-1, keepdims=True)
    weights = (powers * (1.0 / total)).astype(LOW)
    return dot_nn(weights, valueset).astype(LOW), top + jnp.log(total)


def attend_back(queries, keyset, valueset, allowed, log_total, grad):
    shares = jnp.exp(scores_of(queries, keyset, allowed) - log_total)
    grad_weights = dot_nt(grad, valueset)
    along = jnp.sum(grad_weights * shares, axis=-1, keepdims=True)
    grad_scores = (shares * (grad_weights - along)).astype(LOW)
    grad_value = dot_tn(shares.astype(LOW), grad).astype(LOW)
    grad_query = (dot_nn(grad_scores, keyset) * SCALING).astype(LOW)
    grad_key = (dot_tn(grad_scores, queries) * SCALING).astype(LOW)
    return grad_query, grad_key, grad_value


def columns(block, head, width):
    start = block * width + head * HEAD_DIM
    return slice(start, start + HEAD_DIM)


def put_normed(parts, vec, rows):
    at = 0
    for part in parts:
        unit, _ = normalized(part[...].astype(WIDE))
        rows[at : at + part.shape[0], :] = (unit * vec[0:1, :] + vec[1:2, :]).astype(LOW)
        at += part.shape[0]


def spots_of(places, size, rows, axis):
    index = lax.broadcasted_iota(jnp.int32, (rows, 1) if axis == 0 else (1, rows), axis)
    slot = index // size
    mask = jnp.where(slot == 1, places[1], jnp.where(slot == 2, places[2], slot))
    return (places[0] ^ mask) * size + index - slot * size


def after_kernel(line, count, biased, residual, vec, *refs):
    value = residual[...].astype(WIDE) + parts_sum(refs[:count])
    after, normed = refs[count : count + 2]
    if biased:
        value = value + vec[6:7, :]
        refs[-1][...] = value.astype(LOW)
    after[...] = value
    unit, _ = normalized(value)
    normed[...] = (unit * vec[line : line + 1, :] + vec[line + 1 : line + 2, :]).astype(LOW)


def after_step(residual, vec, parts, line, biased=False):
    size, width = residual.shape
    outs = [wide(size, width), low(size, width)] + [low(size, width)] * biased
    kernel = functools.partial(after_kernel, line, len(parts), biased)
    return run_kernel(kernel, outs, [residual, vec, *parts], 20 * size * width)


def back_kernel(line, upper_kind, *refs):
    if upper_kind:
        places, refs = refs[0], refs[1:]
    (after, vec, upper), parts, (grad, grad_low, sums) = refs[:3], refs[3:-3], refs[-3:]
    above = (upper[places[4]] if upper_kind == "picked" else upper[...]).astype(WIDE)
    if upper_kind == "masked":
        size = above.shape[0]
        above = jnp.where(spots_of(places, size, size, 0) < places[3], above, 0.0)
    unit, rate = normalized(after[...].astype(WIDE))
    below = parts_sum(parts)
    scaled = below * vec[line : line + 1, :]
    along = jnp.mean(scaled * unit, axis=-1, keepdims=True)
    value = above + rate * (scaled - jnp.mean(scaled, axis=-1, keepdims=True) - unit * along)
    grad[...] = value
    grad_low[...] = value.astype(LOW)
    sums[0:1, :] = jnp.sum(below * unit, axis=0, keepdims=True)
    sums[1:2, :] = jnp.sum(below, axis=0, keepdims=True)
    sums[2:3, :] = jnp.sum(above, axis=0, keepdims=True)


def back_step(after, vec, upper, parts, line, upper_kind="", places=None):
    size, width = after.shape
    outs = [wide(size, width), low(size, width), wide(3, width)]
    args = [places] * bool(upper_kind) + [after, vec, upper, *parts]
    kernel = functools.partial(back_kernel, line, upper_kind)
    return run_kernel(kernel, outs, args, 30 * size * width, int(bool(upper_kind)), last=line == 0)


def joint_back_kernel(*refs):
    places, enc_after, enc_vec, top, dec_after, dec_vec, upper = refs[:7]
    parts, (enc_grad, dec_grad, both, enc_sums, dec_sums) = refs[7:11], refs[11:]
    size = enc_after.shape[0]
    below = parts_sum(parts)
    for after, vec, above, grad, sums, place in (
        (enc_after, enc_vec, top[places[4]].astype(WIDE), enc_grad, enc_sums, slice(None, size)),
        (dec_after, dec_vec, upper[...], dec_grad, dec_sums, slice(size, None)),
    ):
        unit, rate = normalized(after[...])
        lower = below[place]
        scaled = lower * vec[2:3, :]
        along = jnp.mean(scaled * unit, axis=-1, keepdims=True)
        value = above + rate * (scaled - jnp.mean(scaled, axis=-1, keepdims=True) - unit * along)
        grad[...] = value
        both[place, :] = value.astype(LOW)
        sums[0:1, :] = jnp.sum(lower * unit, axis=0, keepdims=True)
        sums[1:2, :] = jnp.sum(lower, axis=0, keepdims=True)


def joint_back_step(places, enc_after, enc_vec, top, dec_after, dec_vec, upper, parts):
    size, width = enc_after.shape
    other = dec_after.shape[0]
    outs = [wide(size, width), wide(other, width), low(size + other, width), wide(2, width), wide(2, width)]
    args = [places, enc_after, enc_vec, top, dec_after, dec_vec, upper, *parts]
    return run_kernel(joint_back_kernel, outs, args, 60 * size * width, 1)


def self_kernel(count, masked, *refs):
    if masked:
        places, refs = refs[0], refs[1:]
    parts, refs = refs[:count], refs[count:]
    (vec, w_in, w_out, rows, packed, flat, logs), outs = refs[:7], refs[7:]
    put_normed(parts, vec, rows)
    whole(rows)
    packed[...] = dot_nt(rows[...], w_in[...]).astype(LOW)
    whole(packed)
    allowed = allowed_pairs(places, rows.shape[0] // 4, rows.shape[0]) if masked else None
    width = flat.shape[1]
    for head in range(width // HEAD_DIM):
        q, k, v = (packed[:, columns(block, head, width)] for block in range(3))
        flat[:, columns(0, head, width)], logs[:, head : head + 1] = attend(q, k, v, allowed)
    whole(flat, logs)
    put_partial(dot_nn(flat[...], w_out[...]), outs)


def self_step(parts, vec, w_in, w_out, places=None):
    size, depth = parts[0].shape
    rows, width = 4 * size, w_out.shape[0]
    outs = [low(rows, depth), low(rows, 3 * width), low(rows, width), wide(rows, width // HEAD_DIM)]
    outs = [Far(item) for item in outs]
    masked = places is not None
    outs += partial_outs(size, depth, masked)
    flops = 8 * rows * depth * width + 4 * rows * rows * width
    args = [places] * masked + [*parts, vec, w_in, w_out]
    kernel = functools.partial(self_kernel, len(parts), masked)
    return run_kernel(kernel, outs, args, flops, int(masked), masked)


def self_back_kernel(count, masked, *refs):
    if masked:
        places, refs = refs[0], refs[1:]
    parts, refs = refs[:count], refs[count:]
    (w_in, w_out, packed, logs, rows, grad_packed), outs, grad_flat = refs[:6], refs[6:-1], refs[-1]
    put_rows(parts, rows)
    grad_flat[...] = dot_nt(rows[...], w_out[...]).astype(LOW)
    allowed = allowed_pairs(places, rows.shape[0] // 4, rows.shape[0]) if masked else None
    width = grad_flat.shape[1]
    for head in range(width // HEAD_DIM):
        q, k, v = (packed[:, columns(block, head, width)] for block in range(3))
        grads = attend_back(
            q, k, v, allowed, logs[:, head : head + 1], grad_flat[:, columns(0, head, width)]
        )
        for block in range(3):
            grad_packed[:, columns(block, head, width)] = grads[block]
    put_partial(dot_nn(grad_packed[...], w_in[...]), outs)


def self_back_step(parts, w_in, w_out, packed, logs, places=None):
    rows, (width, depth) = packed.shape[0], w_out.shape
    size = rows // 4
    masked = places is not None
    outs = [low(rows, depth), low(rows, 3 * width), *partial_outs(size, depth, masked)]
    flops = 8 * rows * depth * width + 10 * rows * rows * width
    args = [places] * masked + [*parts, w_in, w_out, packed, logs]
    kernel = functools.partial(self_back_kernel, len(parts), masked)
    return run_kernel(kernel, outs, args, flops, int(masked), masked, [(rows, width)])


def ffn_kernel(part0, part1, part2, part3, up, down, vec, rows, active, slope, *outs):
    put_rows((part0, part1, part2, part3), rows)
    value, slant = gelu_both(dot_nn(rows[...], up[...]) + vec[7:8, :])
    active[...] = value.astype(LOW)
    slope[...] = slant.astype(LOW)
    put_partial(dot_nn(active[...], down[...]), outs)


def ffn_step(parts, up, down, vec):
    size, depth = parts[0].shape
    rows, units = 4 * size, up.shape[1]
    outs = [low(rows, depth), low(rows, units), low(rows, units), *partial_outs(size, depth)]
    return run_kernel(ffn_kernel, outs, [*parts, up, down, vec], 4 * rows * depth * units)


def ffn_back_kernel(part0, part1, part2, part3, up, down, slope, rows, other_rows, grad_hidden, sums, *outs):
    put_joint((part0, part1, part2, part3), rows, other_rows)
    grad = (dot_nt(rows[...], down[...]) * slope[...].astype(WIDE)).astype(LOW)
    grad_hidden[...] = grad
    sums[...] = jnp.sum(grad.astype(WIDE), axis=0, keepdims=True)
    put_partial(dot_nt(grad_hidden[...], up[...]), outs)


def ffn_back_step(parts, up, down, slope):
    both, depth = parts[0].shape
    rows, units = slope.shape
    size = rows // 4
    outs = [low(rows, depth), low(4 * (both - size), depth), low(rows, units), wide(1, units)]
    outs += partial_outs(size, depth)
    return run_kernel(ffn_back_kernel, outs, [*parts, up, down, slope], 4 * rows * depth * units)


def ffn_both_kernel(count, *refs):
    places, parts, refs = refs[0], refs[1:5], refs[5:]
    grads, refs = refs[:count], refs[count:]
    (up, down, vec), (rows, grad_rows, active, grad_hidden, sums), outs = refs[:3], refs[3:8], refs[8:]
    put_rows(parts, rows)
    put_rows(grads, grad_rows)
    keep = spots_of(places, parts[0].shape[0], rows.shape[0], 0) < places[3]
    grad_rows[...] = jnp.where(keep, grad_rows[...].astype(WIDE), 0.0).astype(LOW)
    value, slant = gelu_both(dot_nn(rows[...], up[...]) + vec[7:8, :])
    active[...] = value.astype(LOW)
    grad = (dot_nt(grad_rows[...], down[...]) * slant).astype(LOW)
    grad_hidden[...] = grad
    sums[...] = jnp.sum(grad.astype(WIDE), axis=0, keepdims=True)
    put_partial(dot_nt(grad_hidden[...], up[...]), outs)


def ffn_both_step(parts, grads, up, down, vec, places):
    size, depth = parts[0].shape
    rows, units = 4 * size, up.shape[1]
    outs = [low(rows, depth)] * 2 + [low(rows, units)] * 2 + [wide(1, units)]
    args = [places, *parts, *grads, up, down, vec]
    kernel = functools.partial(ffn_both_kernel, len(grads))
    return run_kernel(kernel, outs + partial_outs(size, depth), args, 6 * rows * depth * units, 1)


def down_kernel(active, down, *outs):
    put_partial(dot_nn(active[...], down[...]), outs)


def down_step(active, down):
    rows, units = active.shape
    depth = down.shape[1]
    return run_kernel(
        down_kernel, partial_outs(rows // 4, depth, True), [active, down], 2 * rows * units * depth, beside=True
    )


def put_joint(parts, rows, other_rows):
    size = rows.shape[0] // 4
    other = other_rows.shape[0] // 4
    for slot, part in enumerate(parts):
        rows[slot * size : (slot + 1) * size, :] = part[:size, :]
        other_rows[slot * other : (slot + 1) * other, :] = part[size:, :]


def cross_kernel(*refs):
    parts, (w_memory, w_query, w_back) = refs[:4], refs[4:7]
    rows, query_rows, memory, queries, flat, logs = refs[7:13]
    put_joint(parts, rows, query_rows)
    queries[...] = dot_nt(query_rows[...], w_query[...]).astype(LOW)
    memory[...] = dot_nt(rows[...], w_memory[...]).astype(LOW)
    width = flat.shape[1]
    for head in range(width // HEAD_DIM):
        k, v = (memory[:, columns(block, head, width)] for block in range(2))
        own = columns(0, head, width)
        flat[:, own], logs[:, head : head + 1] = attend(queries[:, own], k, v, None)
    put_partial(dot_nn(flat[...], w_back[...]), refs[13:])


def cross_step(parts, size, w_memory, w_query, w_back):
    both, depth = parts[0].shape
    frames, rows, width = 4 * size, 4 * (both - size), w_query.shape[0]
    outs = [low(frames, depth), low(rows, depth), low(frames, 2 * width), low(rows, width), low(rows, width)]
    outs += [wide(rows, width // HEAD_DIM), *partial_outs(rows // 4, depth)]
    flops = 4 * frames * depth * width + 4 * frames * rows * width + 4 * rows * depth * width
    args = [*parts, w_memory, w_query, w_back]
    return run_kernel(cross_kernel, outs, args, flops)


def cross_back_kernel(*refs):
    parts, (w_memory, w_query, w_back, queries, memory, logs) = refs[:4], refs[4:10]
    (rows, grad_query, grad_memory), grad_flat = refs[10:13], refs[-1]
    put_rows(parts, rows)
    grad_flat[...] = dot_nt(rows[...], w_back[...]).astype(LOW)
    width = queries.shape[1]
    for head in range(width // HEAD_DIM):
        own = columns(0, head, width)
        k, v = (memory[:, columns(block, head, width)] for block in range(2))
        grads = attend_back(queries[:, own], k, v, None, logs[:, head : head + 1], grad_flat[:, own])
        grad_query[:, own] = grads[0]
        grad_memory[:, own] = grads[1]
        grad_memory[:, columns(1, head, width)] = grads[2]
    outs = refs[13:-1]
    size, other = memory.shape[0] // 4, queries.shape[0] // 4
    to_memory = dot_nn(grad_memory[...], w_memory[...])
    to_query = dot_nn(grad_query[...], w_query[...])
    for slot, out in enumerate(outs):
        out[:size, :] = to_memory[slot * size : (slot + 1) * size].astype(out.dtype)
        out[size:, :] = to_query[slot * other : (slot + 1) * other].astype(out.dtype)


def cross_back_step(parts, w_memory, w_query, w_back, queries, memory, logs):
    depth = parts[0].shape[1]
    rows, width = queries.shape
    frames = memory.shape[0]
    outs = [low(rows, depth), low(rows, width), low(frames, 2 * width)]
    outs += partial_outs((frames + rows) // 4, depth)
    flops = 4 * rows * depth * width + 10 * frames * rows * width + 4 * frames * depth * width
    args = [*parts, w_memory, w_query, w_back, queries, memory, logs]
    return run_kernel(cross_back_kernel, outs, args, flops, scratch=[(rows, width)])


def grads_kernel(pairs, *refs):
    out = refs[-1]
    at = 0
    if len(refs) > 2 * pairs + 1:
        at = refs[-2].shape[0]
        out[:at, :] = refs[-2][...]
    for pair in range(pairs):
        left, right = refs[2 * pair], refs[2 * pair + 1]
        size = left.shape[1]
        out[at : at + size, :] = dot_tn(left[...], right[...]).astype(LOW)
        at += size


def weight_grads(*args, under=None):
    depth = args[1].shape[1]
    total = sum(left.shape[1] for left in args[::2])
    flops = sum(2 * left.size * depth for left in args[::2])
    kernel = functools.partial(grads_kernel, len(args) // 2)
    if under is not None:
        total, args = total + under.shape[0], (*args, under)
    return run_kernel(kernel, [low(total, depth)], args, flops, beside=True)[0]


def add_kernel(left, right, out):
    size = out.shape[0]
    out[...] = (left[...].astype(WIDE) + right[-size:, :].astype(WIDE)).astype(out.dtype)


def add_step(left, right):
    return run_kernel(add_kernel, [low(*left.shape)], [left, right], left.size)[0]


def pick_kernel(flag, left, right, out):
    out[...] = jnp.where(flag[0] == 1, left[...], right[...])


def pick_step(flag, left, right):
    return run_kernel(pick_kernel, [low(*left.shape)], [flag, left, right], left.size, 1)[0]


def own_kernel(flag, first_value, second_value, other, *outs):
    at = 0
    for out in outs:
        place = slice(at, at + out.shape[0])
        mine = jnp.where(flag[0] == 1, first_value[place, :], second_value[place, :])
        out[...] = (mine.astype(WIDE) + other[place, :].astype(WIDE)).astype(LOW)
        at += out.shape[0]


def own_sum(flag, first_value, second_value, other, pieces):
    rows, width = other.shape
    outs = [low(rows // pieces, width)] * pieces
    return run_kernel(own_kernel, outs, [flag, first_value, second_value, other], other.size, 1)


def stack_kernel(*refs):
    put_rows(refs[:-1], refs[-1])


def stack_step(*parts):
    rows = sum(part.shape[0] for part in parts)
    return run_kernel(stack_kernel, [low(rows, parts[0].shape[1])], parts, rows)[0]


def last_kernel(flag, *refs):
    out, at = refs[-1], 0
    for value, other in zip(refs[:-1:2], refs[1:-1:2]):
        size = value.shape[0]
        out[at : at + size, :] = jnp.where(flag[0] == 1, other[...], value[...]).astype(out.dtype)
        at += size


def last_step(flag, *args, kind=LOW):
    rows, width = sum(value.shape[0] for value in args[::2]), args[0].shape[1]
    outs = [jax.ShapeDtypeStruct((rows, width), kind)]
    return run_kernel(last_kernel, outs, [flag, *args], rows * width, 1, last=kind == WIDE)[0]


def pack_kernel(*refs):
    out = refs[-1]
    for at, sums in enumerate(refs[:3]):
        out[2 * at : 2 * at + 2, :] = sums[:2, :]
    out[6:7, :] = refs[2][2:3, :]
    for at, sums in enumerate(refs[3:6]):
        out[7 + 2 * at : 9 + 2 * at, :] = sums[:2, :]
    out[13:14, :] = refs[5][2:3, :]


def pack_step(*sums):
    return run_kernel(pack_kernel, [wide(14, sums[0].shape[1])], sums, 1)[0]


def plus_kernel(left, right, out):
    out[...] = left[...] + right[...]


def plus_step(left, right):
    return run_kernel(plus_kernel, [wide(*left.shape)], [left, right], 1)[0]


def total_kernel(flag, enc_bias, dec_bias, part0, part1, mine, other):
    total = part0[...] + part1[...]
    here = flag[0] == 1
    mine[:7, :] = jnp.where(here, total[:7], total[7:])
    other[:7, :] = jnp.where(here, total[7:], total[:7])
    mine[7:, :] = jnp.where(here, enc_bias[...], dec_bias[...])
    other[7:, :] = jnp.where(here, dec_bias[...], enc_bias[...])


def total_step(flag, enc_bias, dec_bias, parts):
    rows, width = 7 + enc_bias.shape[0], enc_bias.shape[1]
    args = [flag, enc_bias, dec_bias, *parts]
    return run_kernel(total_kernel, [wide(rows, width)] * 2, args, 1, 1)


def self_final_kernel(first_flag, end_flag, value, other, lower, upper, w_in, w_out):
    half, split = lower.shape[0], w_in.shape[0]
    enc = jnp.where(end_flag[0] == 1, other[...], value[...])
    here = first_flag[0] == 1
    low_half = jnp.where(here, enc[:half], lower[...]).astype(WIDE)
    high_half = jnp.where(here, enc[half:], upper[...]).astype(WIDE)
    w_in[:half, :] = low_half
    w_in[half:, :] = high_half[: split - half]
    w_out[...] = high_half[split - half :]


def self_final_step(first_flag, end_flag, value, other, lower, upper, split):
    rows, width = value.shape
    args = [first_flag, end_flag, value, other, lower, upper]
    return run_kernel(self_final_kernel, [wide(split, width), wide(rows - split, width)], args, 1, 2, last=True)


def scatter_kernel(flag, rows_in, keep, send):
    half = keep.shape[0]
    here = flag[0] == 1
    keep[...] = jnp.where(here, rows_in[:half, :], rows_in[half:, :])
    send[...] = jnp.where(here, rows_in[half:, :], rows_in[:half, :])


def scatter_step(flag, value):
    rows, width = value.shape
    return run_kernel(scatter_kernel, [low(rows // 2, width)] * 2, [flag, value], 1, 1)


def small_kernel(count, *refs):
    total = refs[0][...]
    for part in refs[1:count]:
        total = total + part[...]
    norm, up, down = refs[count:]
    for at in range(3):
        norm[at] = total[2 * at : 2 * at + 2, :]
    down[...] = total[6:7, :]
    up[...] = total[7:, :]


def small_step(parts):
    rows, width = parts[0].shape
    outs = [wide(3, 2, width), wide(rows - 7, width), wide(1, width)]
    return run_kernel(functools.partial(small_kernel, len(parts)), outs, parts, 1, last=True)


def out_kernel(places, cross, vec, *refs):
    parts, out = refs[:-1], refs[-1]
    size = out.shape[0]
    value = cross[...] + parts_sum(parts) + vec[6:7, :]
    keep = spots_of(places, size, size, 0) < places[3]
    out[...] = jnp.where(keep, value, 0.0).astype(LOW)


def out_step(places, cross, vec, parts):
    outs = [low(*cross.shape)]
    return run_kernel(out_kernel, outs, [places, cross, vec, *parts], 1, 1, last=True)[0]


def final_kernel(flag, first_value, second_value, out):
    out[...] = jnp.where(flag[0] == 1, first_value[...].astype(WIDE), second_value[...].astype(WIDE))


def final_step(flag, first_value, second_value):
    args = [flag, first_value, second_value]
    return run_kernel(final_kernel, [wide(*first_value.shape)], args, first_value.size, 1, last=True)[0]


def peers(slot):
    count = lax.axis_size("tensor")
    pairs = []
    for section in range(lax.axis_size("section")):
        mask = (0, 1 << section, 2 >> section, 3)[slot]
        pairs += [(section * count + at, section * count + (at ^ mask)) for at in range(count)]
    return pairs


def moved(value, slot):
    return lax.ppermute(value, ("section", "tensor"), peers(slot))


def tie(*values):
    return lax.optimization_barrier(values)


def send_rows(rows):
    far, near, side = (moved(rows, slot) for slot in (3, 1, 2))
    return [rows, near, side, far]


def send_sums(blocks):
    far, near, side = (moved(blocks[slot], slot) for slot in (3, 1, 2))
    return [blocks[0], near, side, far]


def near_rows(rows):
    return moved(rows, 1)


def far_rows(rows, near):
    return [rows, near, moved(stack_step(rows, near), 2)]


def far_sums(blocks):
    there = moved(blocks[2], 2)
    return add_step(blocks[1], there), [blocks[0], there]


def near_sums(onward, kept):
    return [*kept, moved(onward, 1)]


def swapped(value):
    return lax.ppermute(value, "section", [(0, 1), (1, 0)])


def body(
    enc_in, dec_in, lengths, enc_cot, dec_cot, norm_params, attn_in, attn_out, cross_proj, w_up, b_up, w_down, b_down
):
    own = lax.axis_index("section")
    part = lax.axis_index("tensor")
    dp_count = lax.axis_size("dp")
    dp_at = lax.axis_index("dp")
    first = own == 0
    width = enc_in.shape[3]
    enc_size = enc_in.shape[2]
    dec_size = dec_in.shape[2]
    heads_width = attn_out.shape[1]

    def own_clip(value):
        return lax.dynamic_index_in_dim(value[:, 0], own, 0, keepdims=False)

    def by_rows(value):
        return jnp.transpose(value[0], (1, 2, 0)).reshape(-1, width)

    frames, tokens, top_dec = own_clip(enc_in), own_clip(dec_in), own_clip(dec_cot)
    enc_parts = send_rows(frames)
    section = jnp.full((1,), own, jnp.int32)
    own_vec = jnp.concatenate([norm_params[0].reshape(6, width), b_down, b_up.reshape(-1, width)])

    def both(value, *after):
        sent, *after = tie(value, *after)
        other = swapped(sent)
        return [Pair(section, value, other, which) for which in (0, 1)], after

    (enc_vec, dec_vec), _ = both(own_vec)
    (enc_in_w, dec_in_w), _ = both(by_rows(attn_in))

    first_flag = first.astype(jnp.int32).reshape(1)

    at_end = (dp_at == 0) | (dp_at == 3)
    end_flag = at_end.astype(jnp.int32).reshape(1)

    def over_cores(first_value, second_value, pieces=1):
        other = swapped(pick_step(first_flag, second_value, first_value))
        return own_sum(first_flag, first_value, second_value, other, pieces)

    def hop(value, pairs, cores=(0, 1)):
        pairs = [(core * dp_count + a, core * dp_count + b) for core in cores for a, b in pairs]
        return lax.ppermute(value, ("section", "dp"), pairs)

    def outer_hop(inward=None, outward=None, cores=(0, 1)):
        if dp_count != 4:
            if outward is not None:
                outward[0] = lax.psum(outward[0], "dp")
                outward.append(outward[0])
            return
        pairs = [(0, 1), (3, 2)] * (inward is not None) + [(1, 0), (2, 3)] * (outward is not None)
        if inward is None or outward is None:
            value = (inward or outward)[0]
        else:
            value = pick_step(end_flag, inward[0], outward[0])
        other = hop(value, pairs, cores)
        if inward is not None:
            inward[0] = add_step(inward[0], other)
        if outward is not None:
            outward.append(other)

    def inner_hop(piece, cores=(0, 1)):
        if dp_count == 4:
            piece[0] = add_step(piece[0], hop(piece[0], [(1, 2), (2, 1)], cores))

    def pin(value, *pieces):
        value, found = tie(value, list(pieces))
        for piece, kept in zip(pieces, found):
            piece[:] = kept
        return value

    enc_parts[1], enc_parts[2], tokens = tie(enc_parts[1], enc_parts[2], tokens)
    near = near_rows(tokens)
    (enc_out_w, dec_out_w), _ = both(attn_out[0], tokens)
    enc_parts, near = tie(enc_parts, near)
    dec_parts = far_rows(tokens, near)
    length = lax.dynamic_index_in_dim(lengths, own, 0, keepdims=False)[0]
    places = jnp.stack([part, jnp.left_shift(1, own), jnp.right_shift(2, own), length, own]).astype(jnp.int32)
    enc_rows, enc_packed, enc_flat, enc_logs, *partial = self_step(enc_parts, Far(enc_vec), Far(enc_in_w), Far(enc_out_w))
    partial, dec_parts, places = tie(partial, dec_parts, places)
    parts = send_sums(partial)
    (enc_up_w, dec_up_w), _ = both(w_up[0], partial[0])
    (enc_down_w, dec_down_w), _ = both(w_down[0], partial[0])
    dec_rows, dec_packed, dec_flat, dec_logs, *dec_partial = self_step(
        dec_parts, Far(dec_vec), Far(dec_in_w), Far(dec_out_w), places
    )
    parts, dec_partial = tie(parts, dec_partial)
    enc_self, normed = after_step(frames, enc_vec, parts, 4)
    normed, dec_partial = tie(normed, dec_partial)
    parts = send_rows(normed)
    onward, kept = far_sums(dec_partial)
    (w_memory, w_cross), _ = both(by_rows(cross_proj), normed)
    w_query, w_back = w_cross.part(0, heads_width), w_cross.part(heads_width, 2 * heads_width)
    parts = tie(*parts)
    enc_ffn_rows, enc_active, enc_slope, *partial = ffn_step(parts, enc_up_w, enc_down_w, enc_vec)
    partial, onward, kept, top_dec = tie(partial, onward, kept, top_dec)
    parts = send_sums(partial)
    dec_parts = near_sums(onward, kept)
    near = near_rows(top_dec)
    parts, dec_parts, near = tie(parts, dec_parts, near)
    dec_self, dec_normed = after_step(tokens, dec_vec, dec_parts, 2)
    enc_final, normed, enc_low = after_step(enc_self, enc_vec, parts, 2, True)
    parts = send_rows(stack_step(normed, dec_normed))
    top_parts = far_rows(top_dec, near)
    parts = tie(*parts)
    post_rows, cross_rows, memory, queries, cross_flat, cross_logs, *partial = cross_step(
        parts, enc_size, w_memory, w_query, w_back
    )
    partial, top_parts = tie(partial, top_parts)
    parts = send_sums(partial)
    dec_cross, normed = after_step(dec_self, dec_vec, parts, 4)
    parts = send_rows(normed)
    dec_ffn_rows, top_rows, dec_active, dec_hidden, dec_bup, *partial = ffn_both_step(
        parts, top_parts, Far(dec_up_w), Far(dec_down_w), dec_vec, places
    )
    partial, dec_active, dec_hidden = tie(partial, dec_active, dec_hidden)
    parts = send_sums(partial)
    g_down = weight_grads(dec_active, top_rows)
    g_up = weight_grads(dec_ffn_rows, dec_hidden)
    parts, g_down, g_up = tie(parts, g_down, g_up)
    dec_grad, grad_low, dec_sums_ffn = back_step(dec_cross, dec_vec, top_dec, parts, 4, "masked", places)
    grad_low, dec_active, g_down, g_up = tie(grad_low, dec_active, g_down, g_up)
    parts = send_rows(grad_low)
    dec_near, dec_far = ([item] for item in over_cores(g_down, g_up, 2))
    out_partial = down_step(dec_active, Far(dec_down_w))
    parts, out_partial = pin((parts, out_partial), dec_near, dec_far)
    grad_rows, grad_query, grad_memory, *partial = cross_back_step(
        parts, w_memory, w_query, w_back, queries, memory, cross_logs
    )
    partial, grad_memory, grad_query, *dec_near = tie(partial, grad_memory, grad_query, *dec_near)
    parts = send_sums(partial)
    outer_hop(dec_near)
    g_cross = weight_grads(grad_query, cross_rows, cross_flat, grad_rows)
    parts, g_cross = pin((parts, g_cross), dec_near)
    enc_grad, dec_grad, grad_low, enc_sums_post, dec_sums_cross = joint_back_step(
        places, enc_final, enc_vec, enc_cot[:, 0], dec_self, dec_vec, dec_grad, parts
    )
    grad_low, grad_memory = tie(grad_low, grad_memory)
    grad_low = pin(grad_low, dec_near, dec_far)
    parts = send_rows(grad_low)
    outer_hop(dec_far)
    inner_hop(dec_near)
    g_memory = weight_grads(grad_memory, post_rows)
    parts, g_memory = pin((parts, g_memory), dec_near, dec_far)
    cross = list(over_cores(g_memory, g_cross))
    grad_rows, dec_grad_rows, enc_hidden, enc_bup, *partial = ffn_back_step(
        parts, enc_up_w, enc_down_w, enc_slope
    )
    partial, enc_hidden, grad_rows, dec_grad_rows = tie(partial, enc_hidden, grad_rows, dec_grad_rows)
    partial = pin(partial, dec_near, dec_far, cross)
    parts = send_sums(partial)
    outer_hop(cross, dec_near)
    inner_hop(dec_far)
    g_down = weight_grads(enc_active, grad_rows)
    g_up = weight_grads(enc_ffn_rows, enc_hidden)
    dec_grad_rows, dec_grad_packed, *dec_partial = self_back_step(
        [dec_grad_rows], dec_in_w, dec_out_w, dec_packed, dec_logs, places
    )
    parts, dec_partial, dec_grad_packed, g_down, g_up = pin(
        (parts, dec_partial, dec_grad_packed, g_down, g_up), cross, dec_near, dec_far
    )
    near_ffn, far_ffn = ([item] for item in over_cores(g_down, g_up, 2))
    enc_grad, grad_low, enc_sums_ffn = back_step(enc_self, enc_vec, enc_grad, parts, 4)
    grad_low, dec_partial, dec_grad_packed = tie(grad_low, dec_partial, dec_grad_packed)
    grad_low = pin(grad_low, near_ffn, far_ffn, cross, dec_far)
    parts = send_rows(grad_low)
    outer_hop(near_ffn, dec_far)
    inner_hop(cross)
    g_dec = weight_grads(dec_grad_packed, dec_rows, dec_flat, dec_grad_rows)
    parts, g_dec = pin((parts, g_dec), near_ffn, cross, dec_far)
    outer_hop(far_ffn, cross)
    inner_hop(near_ffn)
    dec_self_sum, dec_send = scatter_step(first_flag, g_dec)
    dec_self_sum = [add_step(dec_self_sum, swapped(dec_send))]
    onward, kept = far_sums(dec_partial)
    enc_grad_rows, enc_grad_packed, *partial = self_back_step(parts, enc_in_w, enc_out_w, enc_packed, enc_logs)
    partial, enc_grad_packed, onward, kept = pin(
        (partial, enc_grad_packed, onward, kept), near_ffn, far_ffn, cross, dec_self_sum
    )
    g_enc = weight_grads(enc_grad_packed, enc_rows, enc_flat, enc_grad_rows)
    enc_self_sum = [add_step(g_enc, lax.ppermute(g_enc, "section", [(1, 0)]))]
    partial = pin(partial, enc_self_sum)
    parts = send_sums(partial)
    outer_hop(dec_self_sum, near_ffn)
    inner_hop(far_ffn)
    parts, onward, kept, out_partial = pin(
        (parts, onward, kept, out_partial), dec_self_sum, far_ffn, near_ffn, enc_self_sum
    )
    inner_hop(dec_self_sum)
    outer_hop(None, far_ffn)
    outer_hop(enc_self_sum, cores=(0,))
    dec_parts = near_sums(onward, kept)
    enc_in_grad, _, enc_sums_self = back_step(frames, enc_vec, enc_grad, parts, 0)
    out_onward, out_kept = far_sums(out_partial)
    dec_in_grad, _, dec_sums_self = back_step(tokens, dec_vec, dec_grad, dec_parts, 0)
    pack = pack_step(enc_sums_self, enc_sums_post, enc_sums_ffn, dec_sums_self, dec_sums_cross, dec_sums_ffn)
    pack = plus_step(pack, moved(pack, 1))
    pieces = [pack, moved(pack, 2)]
    pieces, out_onward, out_kept = pin((pieces, out_onward, out_kept), enc_self_sum, far_ffn, dec_self_sum)
    out_parts = near_sums(out_onward, out_kept)
    outer_hop(None, dec_self_sum)
    inner_hop(enc_self_sum, cores=(0,))
    mine, theirs = total_step(first_flag, enc_bup.reshape(-1, width), dec_bup.reshape(-1, width), pieces)
    mine = plus_step(mine, swapped(theirs))
    enc_ffn = last_step(end_flag, *near_ffn, *far_ffn)
    dec_ffn = last_step(end_flag, *dec_near, *dec_far)
    other_ffn = swapped(pick_step(first_flag, dec_ffn, enc_ffn))
    if dp_count != 4:
        small = [lax.psum(mine, "dp")]
    else:
        mine = plus_step(mine, lax.ppermute(mine, "dp", [(at, at ^ 1) for at in range(4)]))
        small = [mine, lax.ppermute(mine, "dp", [(at, at ^ 2) for at in range(4)])]
    small, out_parts = pin((small, out_parts), enc_self_sum, dec_self_sum)
    outer_hop(None, enc_self_sum, cores=(0,))
    dec_half = last_step(end_flag, *dec_self_sum)
    dec_lower = lax.ppermute(dec_half, "section", [(0, 1)])
    norm_grad, up_bias_grad, down_bias_grad = small_step(small)
    dec_out = out_step(places, dec_cross, dec_vec, out_parts)
    down_grad = final_step(first_flag, enc_ffn, other_ffn)
    up_grad = final_step(first_flag, other_ffn, dec_ffn)
    cross_grad = last_step(end_flag, *cross, kind=WIDE)
    dec_out, down_grad, up_grad, cross_grad, dec_lower = pin(
        (dec_out, down_grad, up_grad, cross_grad, dec_lower), enc_self_sum
    )
    in_grad, out_grad = self_final_step(
        first_flag, end_flag, *enc_self_sum, dec_lower, dec_half, 3 * heads_width
    )

    def by_columns(value, groups):
        return jnp.transpose(value.reshape(groups, -1, width), (2, 0, 1))[None]

    return (
        enc_low[None, None],
        dec_out[None, None],
        enc_in_grad[None, None],
        dec_in_grad[None, None],
        norm_grad[None],
        by_columns(in_grad, 3),
        out_grad[None],
        by_columns(cross_grad, 2),
        up_grad[None],
        up_bias_grad.reshape(1, -1),
        down_grad[None],
        down_bias_grad,
    )


def solution(mesh):
    placed = (
        P(None, "dp", "tensor", None),
        P(None, "dp", "tensor", None),
        P(None, "dp"),
        P(None, "dp", "tensor", None),
        P(None, "dp", "tensor", None),
        P("section", None, None, None),
        P("section", None, None, "tensor"),
        P("section", "tensor", None),
        P("section", None, None, "tensor"),
        P("section", None, "tensor"),
        P("section", "tensor"),
        P("section", "tensor", None),
        P("section", None),
    )
    return jax.shard_map(
        body,
        mesh=mesh,
        in_specs=placed,
        out_specs=(
            P("section", "dp", "tensor", None),
            P("section", "dp", "tensor", None),
            P("section", "dp", "tensor", None),
            P("section", "dp", "tensor", None),
            P("section", None, None, None),
            P("section", None, None, "tensor"),
            P("section", "tensor", None),
            P("section", None, None, "tensor"),
            P("section", None, "tensor"),
            P("section", "tensor"),
            P("section", "tensor", None),
            P("section", None),
        ),
        check_vma=False,
    )
```
